32 devices in a mesh: pipe: 2 (over y), dp: 16 (over z, x, core).
Axes of the slice: x: 2, y: 2, z: 4, core: 2. Of those that a mesh axis runs over, the one named last changes fastest.
Arguments:
- hidden_in: bfloat16 [20480, 768], P('dp'), may hold values from -9 to 9
- attend_weight: bfloat16 [2, 768, 2304], P('pipe'), may hold values from -0.21875 to 0.21875
- attend_bias: float32 [2, 1536], P('pipe'), may hold values from -3 to 3
- mixing_weight: bfloat16 [2, 768, 768], P('pipe'), may hold values from -0.875 to 0.875
- mixing_bias: float32 [2, 768], P('pipe'), may hold values from -3 to 3
- norm_gain: float32 [2, 2, 768], P('pipe'), may hold values from 0.1 to 1.9
- norm_shift: float32 [2, 2, 768], P('pipe'), may hold values from -3 to 3
- expand_weight: bfloat16 [2, 768, 3072], P('pipe'), may hold values from -0.21875 to 0.21875
- expand_bias: float32 [2, 3072], P('pipe'), may hold values from -3 to 3
- reduce_weight: bfloat16 [2, 3072, 768], P('pipe'), may hold values from -0.109375 to 0.109375
- reduce_bias: float32 [2, 768], P('pipe'), may hold values from -3 to 3
- colbert_weight: bfloat16 [768, 128], replicated, may hold values from -0.21875 to 0.21875
- pass_lengths: int32 [32, 4], P('dp'), may hold values from 16 to 448, as said below
- positives: int32 [32, 4], P('dp'), may hold values from 0 to 3
Outputs:
- grad_attend_weight: float32 [2, 768, 2304], P('pipe')
- grad_attend_bias: float32 [2, 1536], P('pipe')
- grad_mixing_weight: float32 [2, 768, 768], P('pipe')
- grad_mixing_bias: float32 [2, 768], P('pipe')
- grad_norm_gain: float32 [2, 2, 768], P('pipe')
- grad_norm_shift: float32 [2, 2, 768], P('pipe')
- grad_expand_weight: float32 [2, 768, 3072], P('pipe')
- grad_expand_bias: float32 [2, 3072], P('pipe')
- grad_reduce_weight: float32 [2, 3072, 768], P('pipe')
- grad_reduce_bias: float32 [2, 768], P('pipe')
- grad_colbert_weight: float32 [768, 128], replicated
- loss: float32 [32], P('dp')
- stats: float32 [32, 2, 3], P('dp')
The draws below stay inside these ranges and needn't reach their ends.
Inputs may be any that keep to these rules, and one draw needn't show every extreme that they name: `pass_lengths`: in each micro-batch the 4 passage lengths sum to at most 512; some micro-batch has a passage of exactly 448 tokens.
All inputs are finite; a program needn't handle non-finite values.
Results may differ from the reference program's by a relative error of at most 0.023.
Values may be sent and summed in bfloat16 or wider, within the bound.
No kernel may reach another device: no remote copies, remote signals or barrier semaphores. Data moves between devices by JAX's collectives and lax.ppermute only.
A program may use at most 320 MiB of HBM per device.

```python
import jax
import jax.numpy as jnp
from jax import lax

D = 768
HEADS = 12
HEAD_DIM = 64
FF = 3072
EMB = 128
QLEN = 32
NQ = 4
NP = 4
PSLOTS = 512
PMAX = 448
PMIN = 16
SEQ_MB = 640
PACKS = 32
TOKENS = 20480


def draw_hidden_in(key, part):
    key = jax.random.fold_in(key, 3)
    row_place = jnp.arange(TOKENS, dtype=jnp.float32)[:, None] / TOKENS
    base = jnp.clip(jax.random.normal(key, (TOKENS, D), jnp.float32), -6.0, 6.0)
    return (base * (0.5 + row_place)).astype(jnp.bfloat16)


def draw_pass_lengths(key, part):
    key = jax.random.fold_in(key, 7)
    subkeys = jax.random.split(key, 6)
    rest_bound = (PSLOTS - PMAX) // (NP - 1)
    shorter = jax.random.randint(subkeys[0], (PACKS, NP), PMIN, PSLOTS // NP + 1)
    others = jax.random.randint(subkeys[1], (PACKS, NP), PMIN, rest_bound + 1)
    leading = jax.random.randint(subkeys[2], (PACKS, 1), PSLOTS // 2, PMAX + 1)
    long_slot = jax.random.randint(subkeys[3], (PACKS, 1), 0, NP)
    long_bin = jax.random.randint(subkeys[4], (PACKS, 1), 0, 3) == 0
    forced = jax.random.randint(subkeys[5], (), 0, PACKS)
    row_index = jnp.arange(PACKS, dtype=jnp.int32)[:, None]
    leading = jnp.where(row_index == forced, PMAX, leading)
    long_bin = long_bin | (row_index == forced)
    slot_index = jnp.arange(NP, dtype=jnp.int32)[None, :]
    long_row = jnp.where(slot_index == long_slot, leading, others)
    return jnp.where(long_bin, long_row, shorter).astype(jnp.int32)


def with_ends(values, stream_key, smallest, high):
    shape = values.shape
    place = [jax.random.randint(jax.random.fold_in(stream_key, axis), (), 0, shape[axis]) for axis in range(len(shape))]
    values = values.at[tuple(place)].set(smallest)
    longest = shape.index(max(shape))
    place[longest] = (place[longest] + 1) % shape[longest]
    return values.at[tuple(place)].set(high)


def levels(own_key, dims, cuts, smallest, largest):
    def one(position, shards_of):
        steps = jax.random.uniform(jax.random.fold_in(jax.random.fold_in(own_key, 6), position), (shards_of,), jnp.float32, smallest / len(cuts), largest / len(cuts))
        return jnp.repeat(jnp.exp(steps), dims[position] // shards_of).reshape((-1,) + (1,) * (len(dims) - position - 1))

    factor_of = one(*cuts[0])
    for cut in cuts[1:]:
        factor_of = factor_of * one(*cut)
    return factor_of


def scatter_about(stream_key, shape, scale, most, shards=(), kind=jnp.bfloat16):
    level = levels(stream_key, shape, shards, -0.22, 0.18) if shards else 1.0
    result = jax.random.normal(stream_key, shape, jnp.float32) * scale * level
    return jnp.minimum(jnp.maximum(result, -most), most).astype(kind)


def setup_inputs(seed: int = 0) -> dict:
    streams_of = jax.random.split(jax.random.key(seed), 15)
    return {
        "hidden_in": draw_hidden_in(jax.random.fold_in(streams_of[14], 71), 0),
        "attend_weight": scatter_about(streams_of[1], (2, D, 3 * D), D ** -0.5, 0.21875, ((0, 2),)),
        "attend_bias": scatter_about(streams_of[2], (2, 2 * D), 0.5, 3.0, ((0, 2),), jnp.float32),
        "mixing_weight": scatter_about(streams_of[3], (2, D, D), (D // 16) ** -0.5, 0.875, ((0, 2),)),
        "mixing_bias": scatter_about(streams_of[4], (2, D), 0.5, 3.0, ((0, 2),), jnp.float32),
        "norm_gain": jnp.clip(1.0 + 0.18 * jax.random.normal(streams_of[5], (2, 2, D), jnp.float32), 0.1, 1.9),
        "norm_shift": scatter_about(streams_of[6], (2, 2, D), 0.5, 3.0, ((0, 2),), jnp.float32),
        "expand_weight": scatter_about(streams_of[7], (2, D, FF), D ** -0.5, 0.21875, ((0, 2),)),
        "expand_bias": scatter_about(streams_of[8], (2, FF), 0.5, 3.0, ((0, 2),), jnp.float32),
        "reduce_weight": scatter_about(streams_of[9], (2, FF, D), FF ** -0.5, 0.109375, ((0, 2),)),
        "reduce_bias": scatter_about(streams_of[10], (2, D), 0.5, 3.0, ((0, 2),), jnp.float32),
        "colbert_weight": scatter_about(streams_of[11], (D, EMB), D ** -0.5, 0.21875),
        "pass_lengths": draw_pass_lengths(jax.random.fold_in(streams_of[14], 71), 0),
        "positives": with_ends(jax.random.randint(streams_of[13], (PACKS, NQ), 0, NP), jax.random.fold_in(streams_of[13], 1), 0, NP - 1).astype(jnp.int32),
    }


@jax.custom_vjp
def low(v):
    return lax.optimization_barrier(v.astype(jnp.bfloat16)).astype(jnp.float32)

@jax.custom_vjp
def low_back(v):
    return v

def low_keep(v):
    return (low(v), None)

def low_pass(kept, grad):
    return (grad,)

def back_keep(v):
    return (v, None)

def back_low(kept, grad):
    return (low(grad),)
low.defvjp(low_keep, low_pass)
low_back.defvjp(back_keep, back_low)
LAYER_EPSILON = 1e-12
UNIT_EPSILON = 1e-06
SMOOTHING = 0.05
LOGIT_SCALE = 4.0
ROOT_HALF = 0.7071067811865476
PRECISE = lax.Precision.HIGHEST

def matmul_plain(left, right):
    return jnp.dot(left, right, precision=PRECISE, preferred_element_type=jnp.float32)

def gelu_exact(values):
    return 0.5 * values * (1.0 + lax.erf(values * ROOT_HALF))

def layout(lengths):
    end_pos = jnp.cumsum(lengths.astype(jnp.int32)).astype(jnp.int32)
    slot_ids = jnp.arange(PSLOTS, dtype=jnp.int32)
    passage_id = lax.optimization_barrier(jnp.sum((slot_ids[:, None] >= end_pos[None, :]).astype(jnp.int32), axis=1)).astype(jnp.int32)
    query_ids = jnp.arange(NQ * QLEN, dtype=jnp.int32) // QLEN
    segment = jnp.concatenate([query_ids, (NQ + passage_id).astype(jnp.int32)])
    usable = (segment < NQ + NP).astype(jnp.float32)
    member = (passage_id[None, :] == jnp.arange(NP, dtype=jnp.int32)[:, None]).astype(jnp.float32)
    return (segment, usable, member)

def norm_forward(resid, gain_row, shift_row):
    centre = resid - lax.optimization_barrier(jnp.mean(resid, axis=1, keepdims=True))
    inv_std = lax.rsqrt(lax.optimization_barrier(jnp.mean(centre * centre, axis=1, keepdims=True)) + LAYER_EPSILON)
    return centre * inv_std * gain_row + shift_row

def encoder_layer(inputs, weights, segment, usable):
    attend_weight, attend_bias, mixing_weight, mixing_bias, gain_rows, shift_rows, expand_weight, expand_bias, reduce_weight, reduce_bias = weights
    model_width = inputs.shape[1]
    row_count = inputs.shape[0]
    joined_bias = jnp.concatenate([attend_bias[:model_width], jnp.zeros((model_width,), jnp.float32), attend_bias[model_width:]])
    joined = low_back(low(matmul_plain(inputs, attend_weight) + joined_bias))
    query_rows = joined[:, :model_width].reshape(row_count, HEADS, HEAD_DIM)
    key_rows = joined[:, model_width:2 * model_width].reshape(row_count, HEADS, HEAD_DIM)
    value_rows = joined[:, 2 * model_width:].reshape(row_count, HEADS, HEAD_DIM)
    scores = low_back(jnp.einsum('qhd,khd->hqk', query_rows, key_rows, precision=PRECISE) * HEAD_DIM ** (-0.5))
    same_seq = segment[:, None] == segment[None, :]
    scores = jnp.where(same_seq[None], scores, -1e+30)
    row_max = lax.optimization_barrier(jnp.max(scores, axis=2, keepdims=True))
    exp_terms = jnp.exp(scores - row_max)
    softmax_rows = low(exp_terms / lax.optimization_barrier(jnp.sum(exp_terms, axis=2, keepdims=True)))
    context = jnp.einsum('hqk,khd->qhd', softmax_rows, value_rows, precision=PRECISE).reshape(row_count, model_width)
    context = low_back(low(context))
    branch_one = low_back(matmul_plain(context, mixing_weight) + mixing_bias)
    hidden = low(norm_forward(inputs + branch_one, gain_rows[0], shift_rows[0]))
    inner = low_back(matmul_plain(hidden, expand_weight) + expand_bias)
    active = low(gelu_exact(inner))
    branch_two = low_back(matmul_plain(active, reduce_weight) + reduce_bias)
    output = norm_forward(hidden + branch_two, gain_rows[1], shift_rows[1])
    row_mask = usable[:, None]
    squares = jnp.stack([jnp.sum(row_mask * inputs * inputs), jnp.sum(row_mask * branch_one * branch_one), jnp.sum(row_mask * branch_two * branch_two)])
    return (output, squares)

def pack_terms(params, colbert_mat, inputs, lengths, chosen):
    segment, usable, member = layout(lengths)
    squares = []
    current = inputs
    for layer_index in range(2):
        weights = tuple((leaf[layer_index] for leaf in params))
        current, layer_squares = encoder_layer(current, weights, segment, usable)
        squares.append(layer_squares)
        if layer_index == 0:
            current = low_back(low(current))
    embedded = low_back(matmul_plain(low(current), colbert_mat))
    unit_vec = low(embedded * lax.rsqrt(lax.optimization_barrier(jnp.sum(embedded * embedded, axis=1, keepdims=True)) + UNIT_EPSILON))
    query_count = NQ * QLEN
    similar = low_back(matmul_plain(unit_vec[:query_count], unit_vec[query_count:].T))
    scaled = similar / SMOOTHING
    passage_ok = usable[query_count:] > 0.5
    row_max = lax.optimization_barrier(jnp.max(jnp.where(passage_ok[None, :], scaled, -1e+30), axis=1, keepdims=True))
    totals = matmul_plain(jnp.exp(scaled - row_max), member.T)
    smooth = SMOOTHING * (jnp.log(totals) + row_max - jnp.log(lengths.astype(jnp.float32))[None, :])
    scores = LOGIT_SCALE * lax.optimization_barrier(jnp.sum(smooth.reshape(NQ, QLEN, NP), axis=1))
    score_max = lax.optimization_barrier(jnp.max(scores, axis=1, keepdims=True))
    log_total = jnp.log(lax.optimization_barrier(jnp.sum(jnp.exp(scores - score_max), axis=1))) + score_max[:, 0]
    onehot = (chosen[:, None] == jnp.arange(NP, dtype=jnp.int32)[None, :]).astype(jnp.float32)
    losses = jnp.sum(log_total - lax.optimization_barrier(jnp.sum(scores * onehot, axis=1)))
    return (losses, jnp.stack(squares), jnp.sum(usable))

def reference(hidden_in, attend_weight, attend_bias, mixing_weight, mixing_bias, norm_gain, norm_shift, expand_weight, expand_bias, reduce_weight, reduce_bias, colbert_weight, pass_lengths, positives):
    packs_in = hidden_in.astype(jnp.float32).reshape(PACKS, SEQ_MB, D)
    params = tuple((leaf.astype(jnp.float32) for leaf in (attend_weight, attend_bias, mixing_weight, mixing_bias, norm_gain, norm_shift, expand_weight, expand_bias, reduce_weight, reduce_bias)))
    colbert_wide = colbert_weight.astype(jnp.float32)

    def objective(params, colbert_mat):

        def add_pack(running, pack_items):
            losses, squares, counted = jax.checkpoint(pack_terms)(params, colbert_mat, *pack_items)
            return (running + losses, (losses, squares, counted))
        total, per_pack = lax.scan(add_pack, jnp.zeros((), jnp.float32), (packs_in, pass_lengths, positives))
        return (total / (PACKS * NQ), per_pack)
    unused_mean, pullback, extras = jax.vjp(objective, params, colbert_wide, has_aux=True)
    grads, grad_colbert = pullback(jnp.ones((), jnp.float32))
    loss = extras[0] / NQ
    stats = jnp.sqrt(extras[1] / (extras[2][:, None, None] * D))
    return (grads[0], grads[1], grads[2], grads[3], grads[4], grads[5], grads[6], grads[7], grads[8], grads[9], grad_colbert, loss, stats)
```

```python
import jax
import jax.numpy as jnp
from jax import lax
from jax.sharding import PartitionSpec as P

HEAD_DIM = 64
QLEN = 32
NQ = 4
NP = 4
PSLOTS = 512


LAYER_EPSILON = 1e-12
UNIT_EPSILON = 1e-06
SMOOTHING = 0.05
LOGIT_SCALE = 4.0
ROOT_HALF = 0.7071067811865476
NORMAL_PEAK = 0.3989422804014327
PRECISE = lax.Precision.HIGHEST


def passed_along(array, axis, by):
    count = lax.axis_size(axis)
    pairs = [(i, i + by) for i in range(count) if 0 <= i + by < count]
    return lax.ppermute(array, axis, pairs)


def matmul_plain(left, right):
    return jnp.dot(left, right, preferred_element_type=jnp.float32)


def matmul_rows(left, right):
    return lax.dot_general(
        left, right, (((0,), (0,)), ((), ())), preferred_element_type=jnp.float32
    )


def matmul_cols(left, right):
    return lax.dot_general(
        left, right, (((1,), (1,)), ((), ())), preferred_element_type=jnp.float32
    )


def gelu_exact(values):
    return 0.5 * values * (1.0 + lax.erf(values * ROOT_HALF))


def gelu_slope(values):
    return 0.5 * (1.0 + lax.erf(values * ROOT_HALF)) + values * NORMAL_PEAK * jnp.exp(
        -0.5 * values * values
    )


def layout(lengths):
    places = jnp.arange(NP, dtype=jnp.int32)
    end_pos = jnp.sum(jnp.where(places[None, :] <= places[:, None], lengths[None, :], 0), axis=1)
    slot_ids = jnp.arange(PSLOTS, dtype=jnp.int32)
    passage_id = jnp.sum((slot_ids[:, None] >= end_pos[None, :]).astype(jnp.int32), axis=1)
    query_ids = jnp.arange(NQ * QLEN, dtype=jnp.int32) // QLEN
    segment = jnp.concatenate([query_ids, NQ + passage_id])
    usable = (segment < NQ + NP).astype(jnp.float32)
    member = (passage_id[None, :] == jnp.arange(NP, dtype=jnp.int32)[:, None]).astype(jnp.float32)
    return (segment, usable, member)


def norm_forward(resid, gain_row, shift_row):
    centre = resid - jnp.mean(resid, axis=1, keepdims=True)
    inv_std = lax.rsqrt(jnp.mean(centre * centre, axis=1, keepdims=True) + LAYER_EPSILON)
    unit_rows = centre * inv_std
    return (unit_rows * gain_row + shift_row, unit_rows, inv_std)


def norm_backward(grad_out, unit_rows, inv_std, gain_row):
    grad_gain = jnp.sum(grad_out * unit_rows, axis=0)
    grad_shift = jnp.sum(grad_out, axis=0)
    grad_unit = grad_out * gain_row
    centred = grad_unit - jnp.mean(grad_unit, axis=1, keepdims=True)
    grad_in = inv_std * (
        centred - unit_rows * jnp.mean(grad_unit * unit_rows, axis=1, keepdims=True)
    )
    return (grad_in, grad_gain, grad_shift)


def split_heads(joined_b):
    row_count = joined_b.shape[0]
    model_width = joined_b.shape[1] // 3
    head_count = model_width // HEAD_DIM
    pieces = [
        joined_b[:, block_index * model_width : (block_index + 1) * model_width].reshape(
            row_count, head_count, HEAD_DIM
        )
        for block_index in range(3)
    ]
    return (pieces[0], pieces[1], pieces[2])


def scores_of(query_rows, key_rows, segment):
    same_seq = segment[:, None] == segment[None, :]
    scores = jnp.einsum(
        "qhd,khd->hqk", query_rows, key_rows, preferred_element_type=jnp.float32
    ) * HEAD_DIM ** (-0.5)
    return jnp.where(same_seq[None], scores, -1e30)


def attend(joined_b, segment):
    query_rows, key_rows, value_rows = split_heads(joined_b)
    scores = scores_of(query_rows, key_rows, segment)
    row_max = jnp.max(scores, axis=2, keepdims=True)
    exp_terms = jnp.exp(scores - row_max)
    totals = jnp.sum(exp_terms, axis=2, keepdims=True)
    softmax_rows = (exp_terms / totals).astype(jnp.bfloat16)
    context = jnp.einsum(
        "hqk,khd->qhd", softmax_rows, value_rows, preferred_element_type=jnp.float32
    )
    return (context.reshape(context.shape[0], -1), row_max + jnp.log(totals))


def attend_back(joined_b, segment, log_total, grad_context_b):
    query_rows, key_rows, value_rows = split_heads(joined_b)
    scores = scores_of(query_rows, key_rows, segment)
    softmax_rows = jnp.exp(scores - log_total)
    grad_heads = grad_context_b.reshape(value_rows.shape)
    grad_probs = jnp.einsum(
        "qhd,khd->hqk", grad_heads, value_rows, preferred_element_type=jnp.float32
    )
    grad_scores = softmax_rows * (
        grad_probs - jnp.sum(softmax_rows * grad_probs, axis=2, keepdims=True)
    )
    grad_scores_b = grad_scores.astype(jnp.bfloat16)
    head_scale = HEAD_DIM ** (-0.5)
    grad_query = (
        jnp.einsum("hqk,khd->qhd", grad_scores_b, key_rows, preferred_element_type=jnp.float32)
        * head_scale
    )
    grad_key = (
        jnp.einsum("hqk,qhd->khd", grad_scores_b, query_rows, preferred_element_type=jnp.float32)
        * head_scale
    )
    grad_value = jnp.einsum(
        "hqk,qhd->khd",
        softmax_rows.astype(jnp.bfloat16),
        grad_heads,
        preferred_element_type=jnp.float32,
    )
    row_count = joined_b.shape[0]
    return jnp.concatenate(
        [
            grad_query.reshape(row_count, -1),
            grad_key.reshape(row_count, -1),
            grad_value.reshape(row_count, -1),
        ],
        axis=1,
    )


def layer_forward(inputs, weights, segment):
    (
        attend_weight,
        attend_bias,
        mixing_weight,
        mixing_bias,
        norm_gain,
        norm_shift,
        expand_weight,
        expand_bias,
        reduce_weight,
        reduce_bias,
    ) = weights
    model_width = inputs.shape[1]
    joined_bias = jnp.concatenate(
        [
            attend_bias[:model_width],
            jnp.zeros((model_width,), jnp.float32),
            attend_bias[model_width:],
        ]
    )
    joined_b = (matmul_plain(inputs, attend_weight) + joined_bias).astype(jnp.bfloat16)
    context, log_total = attend(joined_b, segment)
    context_b = context.astype(jnp.bfloat16)
    branch_one = matmul_plain(context_b, mixing_weight) + mixing_bias
    hidden, unit_one, scale_one = norm_forward(
        inputs.astype(jnp.float32) + branch_one, norm_gain[0], norm_shift[0]
    )
    hidden_b = hidden.astype(jnp.bfloat16)
    inner = matmul_plain(hidden_b, expand_weight) + expand_bias
    active_b = gelu_exact(inner).astype(jnp.bfloat16)
    branch_two = matmul_plain(active_b, reduce_weight) + reduce_bias
    output, unit_two, scale_two = norm_forward(
        hidden_b.astype(jnp.float32) + branch_two, norm_gain[1], norm_shift[1]
    )
    stored = (
        inputs,
        joined_b,
        log_total,
        context_b,
        unit_one,
        scale_one,
        hidden_b,
        inner,
        active_b,
        unit_two,
        scale_two,
    )
    return (output, branch_one, branch_two, stored)


def layer_backward(grad_output, stored, weights, segment):
    (
        attend_weight,
        attend_bias,
        mixing_weight,
        mixing_bias,
        norm_gain,
        norm_shift,
        expand_weight,
        expand_bias,
        reduce_weight,
        reduce_bias,
    ) = weights
    (
        inputs,
        joined_b,
        log_total,
        context_b,
        unit_one,
        scale_one,
        hidden_b,
        inner,
        active_b,
        unit_two,
        scale_two,
    ) = stored
    grad_resid_two, gain_two, shift_two = norm_backward(
        grad_output, unit_two, scale_two, norm_gain[1]
    )
    grad_two_b = grad_resid_two.astype(jnp.bfloat16)
    grad_active = matmul_cols(grad_two_b, reduce_weight)
    grad_inner_b = (grad_active * gelu_slope(inner)).astype(jnp.bfloat16)
    grad_hidden = grad_resid_two + matmul_cols(grad_inner_b, expand_weight)
    grad_resid_one, gain_one, shift_one = norm_backward(
        grad_hidden, unit_one, scale_one, norm_gain[0]
    )
    grad_one_b = grad_resid_one.astype(jnp.bfloat16)
    grad_context_b = matmul_cols(grad_one_b, mixing_weight).astype(jnp.bfloat16)
    grad_joined_b = attend_back(joined_b, segment, log_total, grad_context_b).astype(jnp.bfloat16)
    grad_inputs = grad_resid_one + matmul_cols(grad_joined_b, attend_weight)
    model_width = inputs.shape[1]
    joined_sums = jnp.sum(grad_joined_b, axis=0, dtype=jnp.float32)
    grad_attend_bias = jnp.concatenate([joined_sums[:model_width], joined_sums[2 * model_width :]])
    small_grads = (
        grad_attend_bias,
        jnp.sum(grad_one_b, axis=0, dtype=jnp.float32),
        jnp.stack([gain_one, gain_two]),
        jnp.stack([shift_one, shift_two]),
        jnp.sum(grad_inner_b, axis=0, dtype=jnp.float32),
        jnp.sum(grad_two_b, axis=0, dtype=jnp.float32),
    )
    return (grad_inputs, (grad_joined_b, grad_one_b, grad_inner_b, grad_two_b), small_grads)


def colbert_loss(output_b, colbert_weight, lengths, member, usable, chosen, grad_scale):
    embedded = matmul_plain(output_b, colbert_weight)
    inv_norm = lax.rsqrt(jnp.sum(embedded * embedded, axis=1, keepdims=True) + UNIT_EPSILON)
    unit_vec = embedded * inv_norm
    unit_b = unit_vec.astype(jnp.bfloat16)
    query_count = NQ * QLEN
    similar = matmul_cols(unit_b[:query_count], unit_b[query_count:])
    scaled = similar / SMOOTHING
    passage_ok = usable[query_count:] > 0.5
    row_max = jnp.max(jnp.where(passage_ok[None, :], scaled, -1e30), axis=1, keepdims=True)
    exp_terms = jnp.exp(scaled - row_max)
    totals = jnp.dot(exp_terms, member.T, precision=PRECISE, preferred_element_type=jnp.float32)
    smooth = SMOOTHING * (jnp.log(totals) + row_max - jnp.log(lengths.astype(jnp.float32))[None, :])
    scores = LOGIT_SCALE * jnp.sum(smooth.reshape(NQ, QLEN, NP), axis=1)
    score_max = jnp.max(scores, axis=1, keepdims=True)
    score_exp = jnp.exp(scores - score_max)
    score_total = jnp.sum(score_exp, axis=1, keepdims=True)
    onehot = (chosen[:, None] == jnp.arange(NP, dtype=jnp.int32)[None, :]).astype(jnp.float32)
    pack_loss = jnp.sum(
        jnp.log(score_total[:, 0]) + score_max[:, 0] - jnp.sum(scores * onehot, axis=1)
    )
    grad_scores = (score_exp / score_total - onehot) * grad_scale
    grad_smooth = LOGIT_SCALE * jnp.repeat(grad_scores, QLEN, axis=0)
    grad_totals = grad_smooth * SMOOTHING / totals
    grad_scaled = exp_terms * jnp.dot(
        grad_totals, member, precision=PRECISE, preferred_element_type=jnp.float32
    )
    grad_similar_b = (grad_scaled / SMOOTHING).astype(jnp.bfloat16)
    grad_query = matmul_plain(grad_similar_b, unit_b[query_count:])
    grad_passage = matmul_rows(grad_similar_b, unit_b[:query_count])
    grad_unit = jnp.concatenate([grad_query, grad_passage])
    grad_embed_b = (
        inv_norm * (grad_unit - unit_vec * jnp.sum(grad_unit * unit_vec, axis=1, keepdims=True))
    ).astype(jnp.bfloat16)
    grad_output = matmul_cols(grad_embed_b, colbert_weight)
    return (pack_loss, grad_output, grad_embed_b)


def swapped(array, bit):
    count = lax.axis_size("dp")
    return lax.ppermute(array, "dp", [(i, i ^ bit) for i in range(count)])


def piece(array, index):
    return lax.dynamic_index_in_dim(array, index, 0, keepdims=False)


def placed_at(array, update, index):
    return lax.dynamic_update_index_in_dim(array, update, index, 0)


def sum_low(*arrays):
    total = arrays[0].astype(jnp.float32)
    for array in arrays[1:]:
        total = total + array.astype(jnp.float32)
    return total.astype(jnp.bfloat16)


def summed_over_data(partial):
    count = lax.axis_size("dp")
    rows, columns = partial.shape
    if count != 16:
        share = lax.psum_scatter(partial, "dp", scatter_dimension=0, tiled=True)
        return lax.all_gather(share, "dp", axis=0, tiled=True).astype(jnp.float32)
    place = lax.axis_index("dp")
    core, along_x, along_z = place & 1, (place >> 1) & 1, place >> 2
    halves = partial.reshape(2, rows // 2, columns)
    half = sum_low(piece(halves, core), swapped(piece(halves, 1 - core), 1))
    quarters = half.reshape(2, rows // 4, columns)
    quarter = sum_low(piece(quarters, along_x), swapped(piece(quarters, 1 - along_x), 2))
    parts = quarter.reshape(4, rows // 16, columns)
    arrived = [swapped(piece(parts, along_z ^ step), 4 * step) for step in (1, 2, 3)]
    share = sum_low(piece(parts, along_z), *arrived)
    parts = placed_at(jnp.zeros_like(parts), share, along_z)
    for step in (1, 2, 3):
        parts = placed_at(parts, swapped(share, 4 * step), along_z ^ step)
    quarter = parts.reshape(rows // 4, columns)
    quarters = placed_at(jnp.zeros_like(quarters), quarter, along_x)
    quarters = placed_at(quarters, swapped(quarter, 2), 1 - along_x)
    half = quarters.reshape(rows // 2, columns)
    other = swapped(half, 1)
    whole = jnp.stack([jnp.where(core == 0, half, other), jnp.where(core == 0, other, half)])
    return whole.reshape(rows, columns).astype(jnp.float32)


def flatten_rows(leaf):
    return leaf.reshape(-1, leaf.shape[-1])


def shards(
    hidden_in,
    attend_weight,
    attend_bias,
    mixing_weight,
    mixing_bias,
    norm_gain,
    norm_shift,
    expand_weight,
    expand_bias,
    reduce_weight,
    reduce_bias,
    colbert_weight,
    pass_lengths,
    positives,
):
    section_id = lax.axis_index("pipe")
    data_count = lax.axis_size("dp")
    micro_count = pass_lengths.shape[0]
    seq_rows = hidden_in.shape[0] // micro_count
    model_width = hidden_in.shape[1]
    weights = (
        attend_weight[0],
        attend_bias[0],
        mixing_weight[0],
        mixing_bias[0],
        norm_gain[0],
        norm_shift[0],
        expand_weight[0],
        expand_bias[0],
        reduce_weight[0],
        reduce_bias[0],
    )
    layouts = [layout(pass_lengths[micro_index]) for micro_index in range(micro_count)]
    segments = jnp.stack([layout_item[0] for layout_item in layouts])
    usables = jnp.stack([layout_item[1] for layout_item in layouts])
    members = jnp.stack([layout_item[2] for layout_item in layouts])
    grad_scale = 1.0 / (data_count * micro_count * NQ)
    is_first = section_id == 0
    is_last = section_id == 1
    last_weight = is_last.astype(jnp.float32)
    micro_ids = jnp.arange(micro_count, dtype=jnp.int32)
    received = jnp.zeros((seq_rows, model_width), jnp.bfloat16)
    forward_store = []
    squares = jnp.zeros((micro_count, 3), jnp.float32)
    losses = jnp.zeros((micro_count,), jnp.float32)
    for tick_index in range(micro_count + 1):
        offset = tick_index - section_id
        micro_index = jnp.clip(offset, 0, micro_count - 1)
        live_tick = ((offset >= 0) & (offset < micro_count)).astype(jnp.float32)
        slot_weight = (micro_ids == micro_index).astype(jnp.float32) * live_tick
        own_rows = lax.dynamic_slice_in_dim(hidden_in, micro_index * seq_rows, seq_rows, 0)
        inputs = jnp.where(is_first, own_rows, received)
        usable = usables[micro_index]
        output, branch_one, branch_two, stored = layer_forward(
            inputs, weights, segments[micro_index]
        )
        row_mask = usable[:, None]
        inputs_wide = inputs.astype(jnp.float32)
        tick_squares = jnp.stack(
            [
                jnp.sum(row_mask * inputs_wide * inputs_wide),
                jnp.sum(row_mask * branch_one * branch_one),
                jnp.sum(row_mask * branch_two * branch_two),
            ]
        )
        squares = squares + slot_weight[:, None] * tick_squares[None, :]
        output_b = output.astype(jnp.bfloat16)
        pack_loss, grad_output, grad_embed_b = colbert_loss(
            output_b,
            colbert_weight,
            pass_lengths[micro_index],
            members[micro_index],
            usable,
            positives[micro_index],
            grad_scale,
        )
        losses = losses + slot_weight * pack_loss
        forward_store.append((stored, grad_output, output_b, grad_embed_b))
        if tick_index < micro_count:
            received = passed_along(output_b, "pipe", 1)
    forward_stack = jax.tree.map(lambda *leaves: jnp.stack(leaves), *forward_store)
    forward_sel = jax.tree.map(
        lambda leaf: lax.dynamic_slice_in_dim(leaf, section_id, micro_count, 0), forward_stack
    )
    stored_all, loss_grads, outputs_b, grad_embeds_b = forward_sel
    grad_received = jnp.zeros((seq_rows, model_width), jnp.bfloat16)
    backward_store = []
    for tick_index in range(micro_count + 1):
        micro_index = jnp.clip(tick_index - 1 + section_id, 0, micro_count - 1)
        stored = jax.tree.map(lambda leaf: leaf[micro_index], stored_all)
        upstream = jnp.where(is_last, loss_grads[micro_index], grad_received.astype(jnp.float32))
        grad_inputs, big_grads, small_grads = layer_backward(
            upstream, stored, weights, segments[micro_index]
        )
        backward_store.append((big_grads, small_grads))
        if tick_index < micro_count:
            grad_received = passed_along(grad_inputs.astype(jnp.bfloat16), "pipe", -1)
    backward_stack = jax.tree.map(lambda *leaves: jnp.stack(leaves), *backward_store)
    backward_sel = jax.tree.map(
        lambda leaf: lax.dynamic_slice_in_dim(leaf, 1 - section_id, micro_count, 0), backward_stack
    )
    big_sel, small_sel = backward_sel
    grad_joined_all, grad_one_all, grad_inner_all, grad_two_all = big_sel
    small_sums = jax.tree.map(lambda leaf: jnp.sum(leaf, axis=0), small_sel)
    (
        grad_attend_bias,
        grad_mixing_bias,
        grad_gain,
        grad_shift,
        grad_expand_bias,
        grad_reduce_bias,
    ) = small_sums
    inputs_all = stored_all[0]
    context_all = stored_all[3]
    hidden_all = stored_all[6]
    active_all = stored_all[8]
    grad_colbert = matmul_rows(flatten_rows(outputs_b), flatten_rows(grad_embeds_b)) * last_weight
    grad_attend = matmul_rows(flatten_rows(inputs_all), flatten_rows(grad_joined_all))
    grad_mixing = matmul_rows(flatten_rows(context_all), flatten_rows(grad_one_all))
    grad_expand = matmul_rows(flatten_rows(hidden_all), flatten_rows(grad_inner_all))
    grad_reduce = matmul_rows(flatten_rows(active_all), flatten_rows(grad_two_all))
    small_parts = [
        grad_attend_bias,
        grad_mixing_bias,
        grad_gain.reshape(-1),
        grad_shift.reshape(-1),
        grad_expand_bias,
        grad_reduce_bias,
    ]
    small_sum = lax.psum(jnp.concatenate(small_parts), "dp")
    cuts = [0]
    for part in small_parts:
        cuts.append(cuts[-1] + part.shape[0])
    smalls = [small_sum[cuts[i] : cuts[i + 1]] for i in range(len(small_parts))]
    colbert_sum = lax.psum(grad_colbert.astype(jnp.bfloat16), ("pipe", "dp")).astype(jnp.float32)
    big_sums = [
        summed_over_data(part.astype(jnp.bfloat16))
        for part in (grad_reduce, grad_expand, grad_mixing, grad_attend)
    ]
    section_rows = (jnp.arange(2, dtype=jnp.int32) == section_id).astype(jnp.float32)
    square_parts = section_rows[None, :, None] * squares[:, None, :]
    square_sum = lax.psum(square_parts, "pipe")
    loss_sum = lax.psum(losses * last_weight, "pipe")
    count_micro = jnp.sum(usables, axis=1)
    stats = jnp.sqrt(square_sum / (count_micro[:, None, None] * model_width))
    loss = loss_sum / NQ
    return (
        big_sums[3][None],
        smalls[0][None],
        big_sums[2][None],
        smalls[1][None],
        smalls[2].reshape(1, 2, model_width),
        smalls[3].reshape(1, 2, model_width),
        big_sums[1][None],
        smalls[4][None],
        big_sums[0][None],
        smalls[5][None],
        colbert_sum,
        loss,
        stats,
    )


def solution(mesh):
    placed = (
        P("dp", None),
        P("pipe", None, None),
        P("pipe", None),
        P("pipe", None, None),
        P("pipe", None),
        P("pipe", None, None),
        P("pipe", None, None),
        P("pipe", None, None),
        P("pipe", None),
        P("pipe", None, None),
        P("pipe", None),
        P(),
        P("dp", None),
        P("dp", None),
    )
    return jax.shard_map(
        shards,
        mesh=mesh,
        in_specs=placed,
        out_specs=(
            P("pipe", None, None),
            P("pipe", None),
            P("pipe", None, None),
            P("pipe", None),
            P("pipe", None, None),
            P("pipe", None, None),
            P("pipe", None, None),
            P("pipe", None),
            P("pipe", None, None),
            P("pipe", None),
            P(),
            P("dp"),
            P("dp", None, None),
        ),
        check_vma=False,
    )
```

```python
import functools
import jax
import jax.numpy as jnp
from jax import lax
from jax.experimental import pallas as pl
from jax.experimental.pallas import tpu as pltpu
from jax.sharding import PartitionSpec as P

HEAD_DIM = 64
QLEN = 32
NQ = 4
NP = 4
PSLOTS = 512
LAYER_EPSILON = 1e-12
UNIT_EPSILON = 1e-06
SMOOTHING = 0.05
LOGIT_SCALE = 4.0
ROOT_HALF = 0.7071067811865476
NORMAL_PEAK = 0.3989422804014327
BF = jnp.bfloat16
F32 = jnp.float32
QROWS = NQ * QLEN
SLAB = 256
FFBLOCK = 768
VMEM_LIMIT = 56 * 1024 * 1024
NEG = -1e30


def dot_nn(a, b):
    return jnp.dot(a, b, preferred_element_type=F32)


def dot_nt(a, b):
    return lax.dot_general(a, b, (((1,), (1,)), ((), ())), preferred_element_type=F32)


def dot_tn(a, b):
    return lax.dot_general(a, b, (((0,), (0,)), ((), ())), preferred_element_type=F32)


def gelu_pair(u):
    z = jnp.abs(u) * ROOT_HALF
    t = 1.0 / (1.0 + 0.3275911 * z)
    e = jnp.exp(-0.5 * u * u)
    poly = ((((1.061405429 * t - 1.453152027) * t) + 1.421413741) * t - 0.284496736) * t + 0.254829592
    tail = 0.5 * poly * t * e
    phi = jnp.where(u >= 0, 1.0 - tail, tail)
    return u * phi, phi + NORMAL_PEAK * u * e


def norm_rows(resid):
    centre = resid - jnp.mean(resid, axis=1, keepdims=True)
    inv = lax.rsqrt(jnp.mean(centre * centre, axis=1, keepdims=True) + LAYER_EPSILON)
    return centre * inv, inv


def ends_of(info, micro):
    base = 1 + micro * NP
    ends = []
    total = jnp.int32(0)
    for j in range(NP):
        total = total + info[base + j]
        ends.append(total)
    return ends


def passage_of(place, ends):
    out = jnp.zeros(place.shape, jnp.int32)
    for end in ends:
        out = out + jnp.where(place >= end, 1, 0)
    return out


def fwd_micro(info, tick, micros):
    return jnp.minimum(jnp.maximum(tick - info[0], 0), micros - 1)


def bwd_micro(info, tick, micros):
    return jnp.minimum(jnp.maximum(tick - 1 + info[0], 0), micros - 1)


def fill_masks(info, micro, bias_ref):
    ends = ends_of(info, micro)
    down = passage_of(lax.broadcasted_iota(jnp.int32, (PSLOTS, 1), 0), ends)
    across = passage_of(lax.broadcasted_iota(jnp.int32, (1, PSLOTS), 1), ends)
    bias_ref[...] = jnp.where(down == across, 0.0, NEG).astype(F32)


def query_bias():
    down = lax.broadcasted_iota(jnp.int32, (QROWS, QROWS), 0) // QLEN
    across = lax.broadcasted_iota(jnp.int32, (QROWS, QROWS), 1) // QLEN
    return jnp.where(down == across, 0.0, NEG).astype(F32)


def usable_rows(info, micro, rows):
    ends = ends_of(info, micro)
    place = lax.broadcasted_iota(jnp.int32, (rows, 1), 0)
    return (place < QROWS + ends[-1]).astype(F32)


def half_lanes(value, h):
    lane = lax.broadcasted_iota(jnp.int32, (1, 128), 1) // HEAD_DIM
    return jnp.where(lane == h, value, jnp.zeros_like(value))


def attn_fwd_body(tick, micros, first_tick, info, hid, rec, wq, wk, wv, bq, bv, wm, bm, gain, shift, *rest):
    rest = rest[8:] if not first_tick else rest
    x_out, joined_out, lse_out, ctx_out, hid_out, n_out, inv_out, sq_out, acc, bias, xs, otr, vtr = rest
    g = pl.program_id(0)
    micro = fwd_micro(info, tick, micros)
    rows = hid.shape[0]

    @pl.when(g == 0)
    def _():
        if first_tick:
            xs[...] = hid[...]
        else:
            xs[...] = jnp.where(info[0] == 0, hid[...], rec[...])
        x_out[...] = xs[...]
        fill_masks(info, micro, bias)

    x = xs[...]
    q = (dot_nn(x, wq[...]) + bq[...]).astype(BF)
    joined_out[:, 0:SLAB] = q
    k = dot_nn(x, wk[...]).astype(BF)
    joined_out[:, SLAB : 2 * SLAB] = k
    v32 = dot_nn(x, wv[...]) + bv[...]
    v = v32.astype(BF)
    joined_out[:, 2 * SLAB : 3 * SLAB] = v
    vtr[...] = jnp.transpose(v)
    qbias = query_bias()
    for pair in range(SLAB // 128):
        cols = slice(pair * 128, pair * 128 + 128)
        qs = joined_out[:, cols] * BF(HEAD_DIM**-0.5)
        ks = joined_out[:, SLAB + pair * 128 : SLAB + pair * 128 + 128]
        for h in range(2):
            head = pair * 2 + h
            qm = half_lanes(qs, h)
            vh = slice(head * HEAD_DIM, head * HEAD_DIM + HEAD_DIM)
            st = dot_nt(ks[:QROWS], qm[:QROWS]) + qbias
            top = jnp.max(st, axis=0, keepdims=True)
            p = jnp.exp(st - top)
            total = jnp.sum(p, axis=0, keepdims=True)
            lse_out[head : head + 1, 0:QROWS] = top + jnp.log(total)
            otr[vh, 0:QROWS] = dot_nn(vtr[vh, 0:QROWS], p.astype(BF)) * (1.0 / total)
            for c in range(PSLOTS // 256):
                at = slice(QROWS + c * 256, QROWS + c * 256 + 256)
                st = dot_nt(ks[QROWS:], qm[at]) + bias[:, c * 256 : c * 256 + 256]
                top = jnp.max(st, axis=0, keepdims=True)
                p = jnp.exp(st - top)
                total = jnp.sum(p, axis=0, keepdims=True)
                lse_out[head : head + 1, at] = top + jnp.log(total)
                otr[vh, at] = dot_nn(vtr[vh, QROWS:], p.astype(BF)) * (1.0 / total)
    ctx = jnp.transpose(otr[...]).astype(BF)
    ctx_out[...] = ctx
    part = dot_nn(ctx, wm[...])

    @pl.when(g == 0)
    def _():
        acc[...] = part

    @pl.when(g > 0)
    def _():
        acc[...] += part

    @pl.when(g == pl.num_programs(0) - 1)
    def _():
        b1 = acc[...] + bm[...]
        x32 = xs[...].astype(F32)
        n, inv = norm_rows(x32 + b1)
        hid_out[...] = (n * gain[...] + shift[...]).astype(BF)
        n_out[...] = n.astype(BF)
        inv_out[...] = inv
        mask = usable_rows(info, micro, rows)
        sq_out[0:1, :] = jnp.sum(mask * x32 * x32, axis=0, keepdims=True)
        sq_out[1:2, :] = jnp.sum(mask * b1 * b1, axis=0, keepdims=True)


def attn_forward(tick, micros, info, hidden_in, received, weights, old):
    (wa, ba, wm, bm, gains, shifts) = weights
    rows = hidden_in.shape[0] // micros
    width = hidden_in.shape[1]
    steps = width // SLAB
    first = old is None
    slot = lambda info: fwd_micro(info, tick, micros)
    one = lambda *shape: pl.BlockSpec(shape, lambda g, info: (0,) * len(shape))
    in_specs = [
        pl.BlockSpec((rows, width), lambda g, info: (slot(info), 0)),
        one(rows, width),
        pl.BlockSpec((width, SLAB), lambda g, info: (0, g)),
        pl.BlockSpec((width, SLAB), lambda g, info: (0, steps + g)),
        pl.BlockSpec((width, SLAB), lambda g, info: (0, 2 * steps + g)),
        pl.BlockSpec((1, SLAB), lambda g, info: (0, g)),
        pl.BlockSpec((1, SLAB), lambda g, info: (0, steps + g)),
        pl.BlockSpec((SLAB, width), lambda g, info: (g, 0)),
        one(1, width),
        one(1, width),
        one(1, width),
    ]
    args = [hidden_in, received, wa, wa, wa, ba, ba, wm, bm, gains[0:1], shifts[0:1]]
    shapes = [
        ((micros, rows, width), BF, (None, rows, width), lambda g, i: (slot(i), 0, 0)),
        ((micros, steps, rows, 3 * SLAB), BF, (None, None, rows, 3 * SLAB), lambda g, i: (slot(i), g, 0, 0)),
        ((micros, steps, 8, rows), F32, (None, None, 8, rows), lambda g, i: (slot(i), g, 0, 0)),
        ((micros, rows, width), BF, (None, rows, SLAB), lambda g, i: (slot(i), 0, g)),
        ((micros, rows, width), BF, (None, rows, width), lambda g, i: (slot(i), 0, 0)),
        ((micros, rows, width), BF, (None, rows, width), lambda g, i: (slot(i), 0, 0)),
        ((micros, rows, 1), F32, (None, rows, 1), lambda g, i: (slot(i), 0, 0)),
        ((micros, 8, width), F32, (None, 8, width), lambda g, i: (slot(i), 0, 0)),
    ]
    return call(
        functools.partial(attn_fwd_body, tick, micros, first),
        steps, info, args, in_specs, shapes, old,
        [
            pltpu.VMEM((rows, width), F32),
            pltpu.VMEM((PSLOTS, PSLOTS), F32),
            pltpu.VMEM((rows, width), BF),
            pltpu.VMEM((SLAB, rows), F32),
            pltpu.VMEM((SLAB, rows), BF),
        ],
        flops=2 * rows * width * width * 4 + 4 * 12 * 64 * rows * rows,
    )


def call(body, steps, info, args, in_specs, shapes, old, scratch, flops):
    aliases = {}
    if old is not None:
        in_specs = in_specs + [pl.BlockSpec(memory_space=pl.ANY)] * len(old)
        aliases = {1 + len(args) + i: i for i in range(len(old))}
        args = args + list(old)
    return pl.pallas_call(
        body,
        out_shape=[jax.ShapeDtypeStruct(s[0], s[1]) for s in shapes],
        grid_spec=pltpu.PrefetchScalarGridSpec(
            num_scalar_prefetch=1,
            grid=(steps,),
            in_specs=in_specs,
            out_specs=[pl.BlockSpec(s[2], s[3]) for s in shapes],
            scratch_shapes=scratch,
        ),
        input_output_aliases=aliases,
        compiler_params=pltpu.CompilerParams(
            dimension_semantics=("arbitrary",), vmem_limit_bytes=VMEM_LIMIT
        ),
        cost_estimate=pl.CostEstimate(flops=flops, bytes_accessed=20_000_000, transcendentals=0),
    )(info, *args)


def ffn_fwd_body(tick, micros, first_tick, info, hid, we, be, wr, br, gain, shift, *rest):
    rest = rest[6:] if not first_tick else rest
    act_out, slope_out, out_all, n_out, inv_out, sq_out, send_out, acc = rest
    j = pl.program_id(0)
    micro = fwd_micro(info, tick, micros)
    rows = hid.shape[0]
    step = 128
    for r in range(rows // step):
        at = slice(r * step, r * step + step)
        inner = dot_nn(hid[at], we[...]) + be[...]
        active, slope = gelu_pair(inner)
        active = active.astype(BF)
        act_out[at] = active
        slope_out[at] = slope.astype(BF)
        part = dot_nn(active, wr[...])

        @pl.when(j == 0)
        def _():
            acc[at] = part

        @pl.when(j > 0)
        def _():
            acc[at] += part

    @pl.when(j == pl.num_programs(0) - 1)
    def _():
        b2 = acc[...] + br[...]
        n, inv = norm_rows(hid[...].astype(F32) + b2)
        out = (n * gain[...] + shift[...]).astype(BF)
        out_all[...] = out
        send_out[...] = out
        n_out[...] = n.astype(BF)
        inv_out[...] = inv
        mask = usable_rows(info, micro, rows)
        sq_out[0:1, :] = jnp.sum(mask * b2 * b2, axis=0, keepdims=True)


def ffn_forward(tick, micros, info, hidden, weights, old):
    (we, be, wr, br, gains, shifts) = weights
    _, rows, width = hidden.shape
    ff = we.shape[1]
    steps = ff // FFBLOCK
    first = old is None
    slot = lambda info: fwd_micro(info, tick, micros)
    one = lambda *shape: pl.BlockSpec(shape, lambda g, info: (0,) * len(shape))
    in_specs = [
        pl.BlockSpec((None, rows, width), lambda g, i: (slot(i), 0, 0)),
        pl.BlockSpec((width, FFBLOCK), lambda g, i: (0, g)),
        pl.BlockSpec((1, FFBLOCK), lambda g, i: (0, g)),
        pl.BlockSpec((FFBLOCK, width), lambda g, i: (g, 0)),
        one(1, width),
        one(1, width),
        one(1, width),
    ]
    args = [hidden, we, be, wr, br, gains[1:2], shifts[1:2]]
    shapes = [
        ((micros, rows, ff), BF, (None, rows, FFBLOCK), lambda g, i: (slot(i), 0, g)),
        ((micros, rows, ff), BF, (None, rows, FFBLOCK), lambda g, i: (slot(i), 0, g)),
        ((micros, rows, width), BF, (None, rows, width), lambda g, i: (slot(i), 0, 0)),
        ((micros, rows, width), BF, (None, rows, width), lambda g, i: (slot(i), 0, 0)),
        ((micros, rows, 1), F32, (None, rows, 1), lambda g, i: (slot(i), 0, 0)),
        ((micros, 8, width), F32, (None, 8, width), lambda g, i: (slot(i), 0, 0)),
        ((rows, width), BF, (rows, width), lambda g, i: (0, 0)),
    ]
    return call(
        functools.partial(ffn_fwd_body, tick, micros, first),
        steps, info, args, in_specs, shapes, old,
        [pltpu.VMEM((rows, width), F32)],
        flops=4 * rows * width * ff,
    )


def column_sum(value):
    return jnp.sum(value, axis=0, keepdims=True)


def norm_rows_back(grad_out, n, inv, gain):
    grad_unit = grad_out * gain
    mean_grad = jnp.mean(grad_unit, axis=1, keepdims=True)
    mean_along = jnp.mean(grad_unit * n, axis=1, keepdims=True)
    return inv * (grad_unit - mean_grad - n * mean_along)


def loss_parts(info, micro, micros, grad_scale, out_b, wc):
    ends = ends_of(info, micro)
    embedded = dot_nn(out_b, wc)
    inv_norm = lax.rsqrt(jnp.sum(embedded * embedded, axis=1, keepdims=True) + UNIT_EPSILON)
    unit = embedded * inv_norm
    unit_b = unit.astype(BF)
    queries, passages = unit_b[:QROWS], unit_b[QROWS:]
    scaled = dot_nt(queries, passages) / SMOOTHING
    owner = passage_of(lax.broadcasted_iota(jnp.int32, (1, PSLOTS), 1), ends)
    top = jnp.max(jnp.where(owner < NP, scaled, NEG), axis=1, keepdims=True)
    terms = jnp.exp(scaled - top)
    lane = lax.broadcasted_iota(jnp.int32, (1, 128), 1)
    totals = jnp.ones((QROWS, 128), F32)
    lengths = jnp.ones((1, 128), F32)
    for j in range(NP):
        total = jnp.sum(jnp.where(owner == j, terms, 0.0), axis=1, keepdims=True)
        totals = jnp.where(lane == j, total, totals)
        lengths = jnp.where(lane == j, info[1 + micro * NP + j].astype(F32), lengths)
    smooth = SMOOTHING * (jnp.log(totals) + top - jnp.log(lengths))
    grouped = jnp.sum(smooth.reshape(NQ, QLEN, 128), axis=1, keepdims=True)
    scores = LOGIT_SCALE * grouped
    scores = jnp.where(lane[None] < NP, scores, NEG)
    score_max = jnp.max(scores, axis=2, keepdims=True)
    score_exp = jnp.exp(scores - score_max)
    score_total = jnp.sum(score_exp, axis=2, keepdims=True)
    query = lax.broadcasted_iota(jnp.int32, (NQ, 1, 128), 0)
    chosen = jnp.zeros((NQ, 1, 128), jnp.int32)
    for i in range(NQ):
        chosen = jnp.where(query == i, info[1 + micros * NP + micro * NQ + i], chosen)
    onehot = (chosen == lane[None]).astype(F32)
    own_score = jnp.sum(jnp.where(chosen == lane[None], scores, 0.0), axis=2, keepdims=True)
    losses = jnp.log(score_total) + score_max - own_score
    loss = jnp.sum(losses, axis=0)
    grad_scores = (score_exp / score_total - onehot) * grad_scale
    grad_smooth = jnp.broadcast_to(LOGIT_SCALE * grad_scores, (NQ, QLEN, 128)).reshape(QROWS, 128)
    share = grad_smooth / totals
    weight = jnp.zeros((QROWS, PSLOTS), F32)
    for j in range(NP):
        weight = jnp.where(owner == j, share[:, j : j + 1], weight)
    grad_similar = jnp.where(owner < NP, terms * weight, 0.0).astype(BF)
    grad_unit = jnp.concatenate([dot_nn(grad_similar, passages), dot_tn(grad_similar, queries)])
    grad_embed = inv_norm * (grad_unit - unit * jnp.sum(grad_unit * unit, axis=1, keepdims=True))
    return loss, grad_embed.astype(BF)


def ffn_bwd_body(tick, micros, grad_scale, first_tick, info, out_all, wc, rec, n2, inv2, gain2, slope, wr, we, n1, inv1, gain1, *rest):
    rest = rest[6:] if not first_tick else rest
    two_out, inner_out, one_out, emb_out, small_out, ff_out, resid_out, acc, resid, grad = rest
    j = pl.program_id(0)
    micro = bwd_micro(info, tick, micros)

    @pl.when(j == 0)
    def _():
        small_out[...] = jnp.zeros(small_out.shape, F32)

        @pl.when(info[0] == 1)
        def _():
            loss, grad_embed = loss_parts(info, micro, micros, grad_scale, out_all[...], wc[...])
            emb_out[...] = grad_embed
            grad[...] = dot_nt(grad_embed, wc[...])
            small_out[6:7, 0:128] = jnp.broadcast_to(loss, (1, 128))

        @pl.when(info[0] == 0)
        def _():
            emb_out[...] = jnp.zeros(emb_out.shape, BF)
            grad[...] = rec[...].astype(F32)

        upstream = grad[...]
        n = n2[...].astype(F32)
        small_out[0:1, :] = column_sum(upstream * n)
        small_out[1:2, :] = column_sum(upstream)
        d_two = norm_rows_back(upstream, n, inv2[...], gain2[...])
        resid[...] = d_two
        d_two_b = d_two.astype(BF)
        two_out[...] = d_two_b
        small_out[2:3, :] = column_sum(d_two_b.astype(F32))

    rows = two_out.shape[0]
    step = 128
    total = jnp.zeros((1, FFBLOCK), F32)
    for r in range(rows // step):
        at = slice(r * step, r * step + step)
        d_act = dot_nt(two_out[at], wr[...])
        d_inner = (d_act * slope[at].astype(F32)).astype(BF)
        inner_out[at] = d_inner
        total = total + column_sum(d_inner.astype(F32))
        part = dot_nt(d_inner, we[...])

        @pl.when(j == 0)
        def _():
            acc[at] = part

        @pl.when(j > 0)
        def _():
            acc[at] += part
    ff_out[0:1, :] = total

    @pl.when(j == pl.num_programs(0) - 1)
    def _():
        upstream = resid[...] + acc[...]
        n = n1[...].astype(F32)
        small_out[3:4, :] = column_sum(upstream * n)
        small_out[4:5, :] = column_sum(upstream)
        d_one = norm_rows_back(upstream, n, inv1[...], gain1[...])
        resid_out[...] = d_one
        d_one_b = d_one.astype(BF)
        one_out[...] = d_one_b
        small_out[5:6, :] = column_sum(d_one_b.astype(F32))


def ffn_backward(tick, micros, grad_scale, info, received, kept, weights, old):
    (out_all, n2, inv2, slope, n1, inv1) = kept
    (wc, gains, wr, we) = weights
    _, rows, width = out_all.shape
    ff = we.shape[1]
    steps = ff // FFBLOCK
    first = old is None
    slot = lambda info: bwd_micro(info, tick, micros)
    one = lambda *shape: pl.BlockSpec(shape, lambda g, info: (0,) * len(shape))
    at_slot = lambda *shape: pl.BlockSpec((None,) + shape, lambda g, i: (slot(i), 0, 0))
    in_specs = [
        at_slot(rows, width),
        one(*wc.shape),
        one(rows, width),
        at_slot(rows, width),
        at_slot(rows, 1),
        one(1, width),
        pl.BlockSpec((None, rows, FFBLOCK), lambda g, i: (slot(i), 0, g)),
        pl.BlockSpec((FFBLOCK, width), lambda g, i: (g, 0)),
        pl.BlockSpec((width, FFBLOCK), lambda g, i: (0, g)),
        at_slot(rows, width),
        at_slot(rows, 1),
        one(1, width),
    ]
    args = [out_all, wc, received, n2, inv2, gains[1:2], slope, wr, we, n1, inv1, gains[0:1]]
    emb = wc.shape[1]
    shapes = [
        ((micros, rows, width), BF, (None, rows, width), lambda g, i: (slot(i), 0, 0)),
        ((micros, rows, ff), BF, (None, rows, FFBLOCK), lambda g, i: (slot(i), 0, g)),
        ((micros, rows, width), BF, (None, rows, width), lambda g, i: (slot(i), 0, 0)),
        ((micros, rows, emb), BF, (None, rows, emb), lambda g, i: (slot(i), 0, 0)),
        ((micros, 8, width), F32, (None, 8, width), lambda g, i: (slot(i), 0, 0)),
        ((micros, 8, ff), F32, (None, 8, FFBLOCK), lambda g, i: (slot(i), 0, g)),
        ((rows, width), F32, (rows, width), lambda g, i: (0, 0)),
    ]
    return call(
        functools.partial(ffn_bwd_body, tick, micros, grad_scale, first),
        steps, info, args, in_specs, shapes, old,
        [pltpu.VMEM((rows, width), F32), pltpu.VMEM((rows, width), F32), pltpu.VMEM((rows, width), F32)],
        flops=4 * rows * width * ff,
    )


def attn_bwd_body(tick, micros, first_tick, info, resid, one_b, joined, lse, ctx, wm, wq, wk, wv, *rest):
    rest = rest[4:] if not first_tick else rest
    dq_out, dk_out, dv_out, sum_out, send_out, acc, bias, dctx, delta, ktr, dqtr, pbuf, sbuf = rest
    g = pl.program_id(0)
    micro = bwd_micro(info, tick, micros)

    @pl.when(g == 0)
    def _():
        fill_masks(info, micro, bias)

    dctx32 = dot_nt(one_b[...], wm[...])
    dctx[...] = dctx32.astype(BF)
    along = dctx[...].astype(F32) * ctx[...].astype(F32)
    pick = lax.broadcasted_iota(jnp.int32, (8, SLAB), 0) == lax.broadcasted_iota(jnp.int32, (8, SLAB), 1) // HEAD_DIM
    delta[...] = lax.dot_general(
        pick.astype(F32), along, (((1,), (1,)), ((), ())),
        precision=lax.Precision.HIGHEST, preferred_element_type=F32,
    )
    ktr[...] = jnp.transpose(joined[:, SLAB : 2 * SLAB])
    qbias = query_bias()
    for pair in range(SLAB // 128):
        lo = pair * 128
        qs = joined[:, lo : lo + 128] * BF(HEAD_DIM**-0.5)
        ks = joined[:, SLAB + lo : SLAB + lo + 128]
        vs = joined[:, 2 * SLAB + lo : 2 * SLAB + lo + 128]
        do = dctx[:, lo : lo + 128]
        qms = []
        dos = []
        pq = []
        sq = []
        for h in range(2):
            head = pair * 2 + h
            qm = half_lanes(qs, h)
            dm = half_lanes(do, h)
            qms.append(qm)
            dos.append(dm)
            kh = slice(head * HEAD_DIM, head * HEAD_DIM + HEAD_DIM)
            st = dot_nt(ks[:QROWS], qm[:QROWS]) + qbias
            p = jnp.exp(st - lse[head : head + 1, 0:QROWS])
            dp = dot_nt(vs[:QROWS], dm[:QROWS])
            ds = (p * (dp - delta[head : head + 1, 0:QROWS])).astype(BF)
            pq.append(p.astype(BF))
            sq.append(ds)
            dqtr[kh, 0:QROWS] = dot_nn(ktr[kh, 0:QROWS], ds)
            for c in range(PSLOTS // 256):
                at = slice(QROWS + c * 256, QROWS + c * 256 + 256)
                into = slice(h * PSLOTS + c * 256, h * PSLOTS + c * 256 + 256)
                st = dot_nt(ks[QROWS:], qm[at]) + bias[:, c * 256 : c * 256 + 256]
                p = jnp.exp(st - lse[head : head + 1, at])
                dp = dot_nt(vs[QROWS:], dm[at])
                ds = (p * (dp - delta[head : head + 1, at])).astype(BF)
                pbuf[:, into] = p.astype(BF)
                sbuf[:, into] = ds
                dqtr[kh, at] = dot_nn(ktr[kh, QROWS:], ds)
        both_q = jnp.concatenate(qms)
        rows = qs.shape[0]
        q_heads = jnp.concatenate([qms[0][:QROWS], qms[1][:QROWS]])
        d_heads = jnp.concatenate([dos[0][:QROWS], dos[1][:QROWS]])
        dk_out[0:QROWS, lo : lo + 128] = dot_nn(jnp.concatenate(sq, axis=1), q_heads).astype(BF)
        dv_out[0:QROWS, lo : lo + 128] = dot_nn(jnp.concatenate(pq, axis=1), d_heads).astype(BF)
        q_heads = jnp.concatenate([qms[0][QROWS:], qms[1][QROWS:]])
        d_heads = jnp.concatenate([dos[0][QROWS:], dos[1][QROWS:]])
        dk_out[QROWS:rows, lo : lo + 128] = dot_nn(sbuf[...], q_heads).astype(BF)
        dv_out[QROWS:rows, lo : lo + 128] = dot_nn(pbuf[...], d_heads).astype(BF)
    dq = (jnp.transpose(dqtr[...]) * HEAD_DIM**-0.5).astype(BF)
    dq_out[...] = dq
    dk = dk_out[...]
    dv = dv_out[...]
    sum_out[0:1, 0:SLAB] = column_sum(dq.astype(F32))
    sum_out[0:1, SLAB : 2 * SLAB] = column_sum(dv.astype(F32))
    part = dot_nt(dq, wq[...]) + dot_nt(dk, wk[...]) + dot_nt(dv, wv[...])

    @pl.when(g == 0)
    def _():
        acc[...] = part

    @pl.when(g > 0)
    def _():
        acc[...] += part

    @pl.when(g == pl.num_programs(0) - 1)
    def _():
        send_out[...] = (resid[...] + acc[...]).astype(BF)


def attn_backward(tick, micros, info, resid, one_all, kept, weights, old):
    (joined, lse, ctx) = kept
    (wa, wm) = weights
    _, rows, width = one_all.shape
    steps = width // SLAB
    first = old is None
    slot = lambda info: bwd_micro(info, tick, micros)
    one = lambda *shape: pl.BlockSpec(shape, lambda g, info: (0,) * len(shape))
    in_specs = [
        one(rows, width),
        pl.BlockSpec((None, rows, width), lambda g, i: (slot(i), 0, 0)),
        pl.BlockSpec((None, None, rows, 3 * SLAB), lambda g, i: (slot(i), g, 0, 0)),
        pl.BlockSpec((None, None, 8, rows), lambda g, i: (slot(i), g, 0, 0)),
        pl.BlockSpec((None, rows, SLAB), lambda g, i: (slot(i), 0, g)),
        pl.BlockSpec((SLAB, width), lambda g, i: (g, 0)),
        pl.BlockSpec((width, SLAB), lambda g, i: (0, g)),
        pl.BlockSpec((width, SLAB), lambda g, i: (0, steps + g)),
        pl.BlockSpec((width, SLAB), lambda g, i: (0, 2 * steps + g)),
    ]
    args = [resid, one_all, joined, lse, ctx, wm, wa, wa, wa]
    slab = ((micros, rows, width), BF, (None, rows, SLAB), lambda g, i: (slot(i), 0, g))
    shapes = [
        slab,
        slab,
        slab,
        ((micros, steps, 8, 2 * SLAB), F32, (None, None, 8, 2 * SLAB), lambda g, i: (slot(i), g, 0, 0)),
        ((rows, width), BF, (rows, width), lambda g, i: (0, 0)),
    ]
    return call(
        functools.partial(attn_bwd_body, tick, micros, first),
        steps, info, args, in_specs, shapes, old,
        [
            pltpu.VMEM((rows, width), F32),
            pltpu.VMEM((PSLOTS, PSLOTS), F32),
            pltpu.VMEM((rows, SLAB), BF),
            pltpu.VMEM((8, rows), F32),
            pltpu.VMEM((SLAB, rows), BF),
            pltpu.VMEM((SLAB, rows), F32),
            pltpu.VMEM((PSLOTS, 2 * PSLOTS), BF),
            pltpu.VMEM((PSLOTS, 2 * PSLOTS), BF),
        ],
        flops=2 * rows * width * width * 4 + 10 * 12 * 64 * rows * rows,
    )


def passed_along(array, axis, by):
    count = lax.axis_size(axis)
    pairs = [(i, i + by) for i in range(count) if 0 <= i + by < count]
    return lax.ppermute(array, axis, pairs)


def flatten_rows(leaf):
    return leaf.reshape(-1, leaf.shape[-1])


def swapped(array, bit):
    count = lax.axis_size("dp")
    return lax.ppermute(array, "dp", [(i, i ^ bit) for i in range(count)])


def piece(array, index):
    return lax.dynamic_index_in_dim(array, index, 0, keepdims=False)


def placed_at(array, update, index):
    return lax.dynamic_update_index_in_dim(array, update, index, 0)


def sum_low(*arrays):
    total = arrays[0].astype(F32)
    for array in arrays[1:]:
        total = total + array.astype(F32)
    return total.astype(BF)


def summed_over_data(partial):
    count = lax.axis_size("dp")
    rows, columns = partial.shape
    if count != 16:
        share = lax.psum_scatter(partial, "dp", scatter_dimension=0, tiled=True)
        return lax.all_gather(share, "dp", axis=0, tiled=True).astype(F32)
    place = lax.axis_index("dp")
    core, along_x, along_z = place & 1, (place >> 1) & 1, place >> 2
    halves = partial.reshape(2, rows // 2, columns)
    half = sum_low(piece(halves, core), swapped(piece(halves, 1 - core), 1))
    quarters = half.reshape(2, rows // 4, columns)
    quarter = sum_low(piece(quarters, along_x), swapped(piece(quarters, 1 - along_x), 2))
    parts = quarter.reshape(4, rows // 16, columns)
    arrived = [swapped(piece(parts, along_z ^ step), 4 * step) for step in (1, 2, 3)]
    share = sum_low(piece(parts, along_z), *arrived)
    parts = placed_at(jnp.zeros_like(parts), share, along_z)
    for step in (1, 2, 3):
        parts = placed_at(parts, swapped(share, 4 * step), along_z ^ step)
    quarter = parts.reshape(rows // 4, columns)
    quarters = placed_at(jnp.zeros_like(quarters), quarter, along_x)
    quarters = placed_at(quarters, swapped(quarter, 2), 1 - along_x)
    half = quarters.reshape(rows // 2, columns)
    other = swapped(half, 1)
    whole = jnp.stack([jnp.where(core == 0, half, other), jnp.where(core == 0, other, half)])
    return whole.reshape(rows, columns).astype(F32)


def shards(
    hidden_in,
    attend_weight,
    attend_bias,
    mixing_weight,
    mixing_bias,
    norm_gain,
    norm_shift,
    expand_weight,
    expand_bias,
    reduce_weight,
    reduce_bias,
    colbert_weight,
    pass_lengths,
    positives,
):
    section_id = lax.axis_index("pipe")
    data_count = lax.axis_size("dp")
    micros = pass_lengths.shape[0]
    rows = hidden_in.shape[0] // micros
    width = hidden_in.shape[1]
    grad_scale = 1.0 / (data_count * micros * NQ)
    wa, wm, we, wr = attend_weight[0], mixing_weight[0], expand_weight[0], reduce_weight[0]
    gains, shifts = norm_gain[0], norm_shift[0]
    info = jnp.concatenate(
        [section_id.astype(jnp.int32)[None], pass_lengths.reshape(-1), positives.reshape(-1)]
    )
    attn_weights = (wa, attend_bias, wm, mixing_bias, gains, shifts)
    ffn_weights = (we, expand_bias, wr, reduce_bias, gains, shifts)
    received = jnp.zeros((rows, width), BF)
    attn, ffn = None, None
    for tick in range(micros + 1):
        attn = attn_forward(tick, micros, info, hidden_in, received, attn_weights, attn)
        ffn = ffn_forward(tick, micros, info, attn[4], ffn_weights, ffn and ffn[:6])
        if tick < micros:
            received = passed_along(ffn[6], "pipe", 1)
    inputs, joined, lse, context, hidden, unit_one, inv_one, squares_one = attn
    active, slope, outputs, unit_two, inv_two, squares_two, _ = ffn
    received = jnp.zeros((rows, width), BF)
    ffn_back, attn_back = None, None
    for tick in range(micros + 1):
        ffn_back = ffn_backward(
            tick, micros, grad_scale, info, received,
            (outputs, unit_two, inv_two, slope, unit_one, inv_one),
            (colbert_weight, gains, wr, we), ffn_back and ffn_back[:6],
        )
        attn_back = attn_backward(
            tick, micros, info, ffn_back[6], ffn_back[2], (joined, lse, context), (wa, wm),
            attn_back and attn_back[:4],
        )
        if tick < micros:
            received = passed_along(attn_back[4], "pipe", -1)
    d_two, d_inner, d_one, d_embed, small, small_ff, _ = ffn_back
    d_query, d_key, d_value, joined_sums, _ = attn_back

    def weight_grad(left, right):
        return dot_tn(flatten_rows(left), flatten_rows(right)).astype(BF)

    big_reduce = summed_over_data(weight_grad(active, d_two))
    big_expand = summed_over_data(weight_grad(hidden, d_inner))
    big_rest = summed_over_data(
        jnp.concatenate(
            [weight_grad(inputs, d) for d in (d_query, d_key, d_value)] + [weight_grad(context, d_one)],
            axis=1,
        )
    )
    colbert_sum = lax.psum(weight_grad(outputs, d_embed), ("pipe", "dp")).astype(F32)
    small_sum = jnp.sum(small, axis=0)
    joined_sum = jnp.sum(joined_sums[:, :, 0], axis=0)
    attend_sum = jnp.concatenate(
        [joined_sum[:, :SLAB].reshape(-1), joined_sum[:, SLAB:].reshape(-1)]
    )
    vector = jnp.concatenate(
        [small_sum[:6].reshape(-1), attend_sum, jnp.sum(small_ff[:, 0], axis=0)]
    )
    vector = lax.psum(vector, "dp")
    line = vector[: 8 * width].reshape(8, width)
    squares = jnp.stack(
        [
            jnp.sum(squares_one[:, 0], axis=1),
            jnp.sum(squares_one[:, 1], axis=1),
            jnp.sum(squares_two[:, 0], axis=1),
        ],
        axis=1,
    )
    section_rows = (jnp.arange(2, dtype=jnp.int32) == section_id).astype(F32)
    square_sum = lax.psum(section_rows[None, :, None] * squares[:, None, :], "pipe")
    loss_sum = lax.psum(jnp.where(section_id == 1, small[:, 6, 0], 0.0), "pipe")
    counted = (QROWS + jnp.sum(pass_lengths, axis=1)).astype(F32)
    stats = jnp.sqrt(square_sum / (counted[:, None, None] * width))
    return (
        big_rest[None, :, : 3 * width],
        line[6:8].reshape(1, -1),
        big_rest[None, :, 3 * width :],
        line[5][None],
        jnp.stack([line[3], line[0]])[None],
        jnp.stack([line[4], line[1]])[None],
        big_expand[None],
        vector[8 * width :][None],
        big_reduce[None],
        line[2][None],
        colbert_sum,
        loss_sum / NQ,
        stats,
    )


def solution(mesh):
    placed = (
        P("dp", None),
        P("pipe", None, None),
        P("pipe", None),
        P("pipe", None, None),
        P("pipe", None),
        P("pipe", None, None),
        P("pipe", None, None),
        P("pipe", None, None),
        P("pipe", None),
        P("pipe", None, None),
        P("pipe", None),
        P(),
        P("dp", None),
        P("dp", None),
    )
    return jax.shard_map(
        shards,
        mesh=mesh,
        in_specs=placed,
        out_specs=(
            P("pipe", None, None),
            P("pipe", None),
            P("pipe", None, None),
            P("pipe", None),
            P("pipe", None, None),
            P("pipe", None, None),
            P("pipe", None, None),
            P("pipe", None),
            P("pipe", None, None),
            P("pipe", None),
            P(),
            P("dp"),
            P("dp", None, None),
        ),
        check_vma=False,
    )
```

```python
import functools
import jax
import jax.numpy as jnp
from jax import lax
from jax.experimental import pallas as pl
from jax.experimental.pallas import tpu as pltpu
from jax.sharding import PartitionSpec as P

HEAD_DIM = 64
QLEN = 32
NQ = 4
NP = 4
PSLOTS = 512
LAYER_EPSILON = 1e-12
UNIT_EPSILON = 1e-06
SMOOTHING = 0.05
LOGIT_SCALE = 4.0
ROOT_HALF = 0.7071067811865476
NORMAL_PEAK = 0.3989422804014327
BF = jnp.bfloat16
F32 = jnp.float32
QROWS = NQ * QLEN
SLAB = 256
FFBLOCK = 768
VMEM_LIMIT = 56 * 1024 * 1024
NEG = -1e30


def dot_nn(a, b):
    return jnp.dot(a, b, preferred_element_type=F32)


def dot_nt(a, b):
    return lax.dot_general(a, b, (((1,), (1,)), ((), ())), preferred_element_type=F32)


def dot_tn(a, b):
    return lax.dot_general(a, b, (((0,), (0,)), ((), ())), preferred_element_type=F32)


def gelu_pair(u):
    z = jnp.abs(u) * ROOT_HALF
    t = 1.0 / (1.0 + 0.3275911 * z)
    e = jnp.exp(-0.5 * u * u)
    poly = ((((1.061405429 * t - 1.453152027) * t) + 1.421413741) * t - 0.284496736) * t + 0.254829592
    tail = 0.5 * poly * t * e
    phi = jnp.where(u >= 0, 1.0 - tail, tail)
    return u * phi, phi + NORMAL_PEAK * u * e


def norm_rows(resid):
    centre = resid - jnp.mean(resid, axis=1, keepdims=True)
    inv = lax.rsqrt(jnp.mean(centre * centre, axis=1, keepdims=True) + LAYER_EPSILON)
    return centre * inv, inv


def ends_of(info, micro):
    base = 1 + micro * NP
    ends = []
    total = jnp.int32(0)
    for j in range(NP):
        total = total + info[base + j]
        ends.append(total)
    return ends


def passage_of(place, ends):
    out = jnp.zeros(place.shape, jnp.int32)
    for end in ends:
        out = out + jnp.where(place >= end, 1, 0)
    return out


def fwd_micro(info, tick, micros):
    return jnp.minimum(jnp.maximum(tick - info[0], 0), micros - 1)


def bwd_micro(info, tick, micros):
    return jnp.minimum(jnp.maximum(tick - 1 + info[0], 0), micros - 1)


def fill_masks(info, micro, bias_ref):
    ends = ends_of(info, micro)
    down = passage_of(lax.broadcasted_iota(jnp.int32, (PSLOTS, 1), 0), ends)
    across = passage_of(lax.broadcasted_iota(jnp.int32, (1, PSLOTS), 1), ends)
    bias_ref[...] = jnp.where(down == across, 0.0, NEG).astype(F32)


def query_bias():
    down = lax.broadcasted_iota(jnp.int32, (QROWS, QROWS), 0) // QLEN
    across = lax.broadcasted_iota(jnp.int32, (QROWS, QROWS), 1) // QLEN
    return jnp.where(down == across, 0.0, NEG).astype(F32)


def usable_rows(info, micro, rows):
    ends = ends_of(info, micro)
    place = lax.broadcasted_iota(jnp.int32, (rows, 1), 0)
    return (place < QROWS + ends[-1]).astype(F32)


def half_lanes(value, h):
    lane = lax.broadcasted_iota(jnp.int32, (1, 128), 1) // HEAD_DIM
    return jnp.where(lane == h, value, jnp.zeros_like(value))


def attn_fwd_body(tick, micros, first_tick, info, hid, rec, wq, wk, wv, bq, bv, wm, bm, gain, shift, *rest):
    rest = rest[8:] if not first_tick else rest
    x_out, joined_out, lse_out, ctx_out, hid_out, n_out, inv_out, sq_out, acc, bias, xs, otr, vtr = rest
    g = pl.program_id(0)
    micro = fwd_micro(info, tick, micros)
    rows = hid.shape[0]

    @pl.when(g == 0)
    def _():
        if first_tick:
            xs[...] = hid[...]
        else:
            xs[...] = jnp.where(info[0] == 0, hid[...], rec[...])
        x_out[...] = xs[...]
        fill_masks(info, micro, bias)

    x = xs[...]
    q = (dot_nn(x, wq[...]) + bq[...]).astype(BF)
    joined_out[:, 0:SLAB] = q
    k = dot_nn(x, wk[...]).astype(BF)
    joined_out[:, SLAB : 2 * SLAB] = k
    v32 = dot_nn(x, wv[...]) + bv[...]
    v = v32.astype(BF)
    joined_out[:, 2 * SLAB : 3 * SLAB] = v
    vtr[...] = jnp.transpose(v)
    qbias = query_bias()
    for pair in range(SLAB // 128):
        cols = slice(pair * 128, pair * 128 + 128)
        qs = joined_out[:, cols] * BF(HEAD_DIM**-0.5)
        ks = joined_out[:, SLAB + pair * 128 : SLAB + pair * 128 + 128]
        for h in range(2):
            head = pair * 2 + h
            qm = half_lanes(qs, h)
            vh = slice(head * HEAD_DIM, head * HEAD_DIM + HEAD_DIM)
            st = dot_nt(ks[:QROWS], qm[:QROWS]) + qbias
            top = jnp.max(st, axis=0, keepdims=True)
            p = jnp.exp(st - top)
            total = jnp.sum(p, axis=0, keepdims=True)
            lse_out[head : head + 1, 0:QROWS] = top + jnp.log(total)
            otr[vh, 0:QROWS] = dot_nn(vtr[vh, 0:QROWS], p.astype(BF)) * (1.0 / total)
            for c in range(PSLOTS // 256):
                at = slice(QROWS + c * 256, QROWS + c * 256 + 256)
                st = dot_nt(ks[QROWS:], qm[at]) + bias[:, c * 256 : c * 256 + 256]
                top = jnp.max(st, axis=0, keepdims=True)
                p = jnp.exp(st - top)
                total = jnp.sum(p, axis=0, keepdims=True)
                lse_out[head : head + 1, at] = top + jnp.log(total)
                otr[vh, at] = dot_nn(vtr[vh, QROWS:], p.astype(BF)) * (1.0 / total)
    ctx = jnp.transpose(otr[...]).astype(BF)
    ctx_out[...] = ctx
    part = dot_nn(ctx, wm[...])

    @pl.when(g == 0)
    def _():
        acc[...] = part

    @pl.when(g > 0)
    def _():
        acc[...] += part

    @pl.when(g == pl.num_programs(0) - 1)
    def _():
        b1 = acc[...] + bm[...]
        x32 = xs[...].astype(F32)
        n, inv = norm_rows(x32 + b1)
        hid_out[...] = (n * gain[...] + shift[...]).astype(BF)
        n_out[...] = n.astype(BF)
        inv_out[...] = inv
        mask = usable_rows(info, micro, rows)
        sq_out[0:1, :] = jnp.sum(mask * x32 * x32, axis=0, keepdims=True)
        sq_out[1:2, :] = jnp.sum(mask * b1 * b1, axis=0, keepdims=True)


def attn_forward(tick, micros, info, hidden_in, received, weights, old):
    (wa, ba, wm, bm, gains, shifts) = weights
    rows = hidden_in.shape[0] // micros
    width = hidden_in.shape[1]
    steps = width // SLAB
    first = old is None
    slot = lambda info: fwd_micro(info, tick, micros)
    one = lambda *shape: pl.BlockSpec(shape, lambda g, info: (0,) * len(shape))
    in_specs = [
        pl.BlockSpec((rows, width), lambda g, info: (slot(info), 0)),
        one(rows, width),
        pl.BlockSpec((width, SLAB), lambda g, info: (0, g)),
        pl.BlockSpec((width, SLAB), lambda g, info: (0, steps + g)),
        pl.BlockSpec((width, SLAB), lambda g, info: (0, 2 * steps + g)),
        pl.BlockSpec((1, SLAB), lambda g, info: (0, g)),
        pl.BlockSpec((1, SLAB), lambda g, info: (0, steps + g)),
        pl.BlockSpec((SLAB, width), lambda g, info: (g, 0)),
        one(1, width),
        one(1, width),
        one(1, width),
    ]
    args = [hidden_in, received, wa, wa, wa, ba, ba, wm, bm, gains[0:1], shifts[0:1]]
    shapes = [
        ((micros, rows, width), BF, (None, rows, width), lambda g, i: (slot(i), 0, 0)),
        ((micros, steps, rows, 3 * SLAB), BF, (None, None, rows, 3 * SLAB), lambda g, i: (slot(i), g, 0, 0)),
        ((micros, steps, 8, rows), F32, (None, None, 8, rows), lambda g, i: (slot(i), g, 0, 0)),
        ((micros, rows, width), BF, (None, rows, SLAB), lambda g, i: (slot(i), 0, g)),
        ((micros, rows, width), BF, (None, rows, width), lambda g, i: (slot(i), 0, 0)),
        ((micros, rows, width), BF, (None, rows, width), lambda g, i: (slot(i), 0, 0)),
        ((micros, rows, 1), F32, (None, rows, 1), lambda g, i: (slot(i), 0, 0)),
        ((micros, 8, width), F32, (None, 8, width), lambda g, i: (slot(i), 0, 0)),
    ]
    return call(
        functools.partial(attn_fwd_body, tick, micros, first),
        steps, info, args, in_specs, shapes, old,
        [
            pltpu.VMEM((rows, width), F32),
            pltpu.VMEM((PSLOTS, PSLOTS), F32),
            pltpu.VMEM((rows, width), BF),
            pltpu.VMEM((SLAB, rows), F32),
            pltpu.VMEM((SLAB, rows), BF),
        ],
        flops=2 * rows * width * width * 4 + 4 * 12 * 64 * rows * rows,
    )


def call(body, steps, info, args, in_specs, shapes, old, scratch, flops):
    aliases = {}
    if old is not None:
        in_specs = in_specs + [pl.BlockSpec(memory_space=pl.ANY)] * len(old)
        aliases = {1 + len(args) + i: i for i in range(len(old))}
        args = args + list(old)
    return pl.pallas_call(
        body,
        out_shape=[jax.ShapeDtypeStruct(s[0], s[1]) for s in shapes],
        grid_spec=pltpu.PrefetchScalarGridSpec(
            num_scalar_prefetch=1,
            grid=(steps,),
            in_specs=in_specs,
            out_specs=[pl.BlockSpec(s[2], s[3]) for s in shapes],
            scratch_shapes=scratch,
        ),
        input_output_aliases=aliases,
        compiler_params=pltpu.CompilerParams(
            dimension_semantics=("arbitrary",), vmem_limit_bytes=VMEM_LIMIT
        ),
        cost_estimate=pl.CostEstimate(flops=flops, bytes_accessed=20_000_000, transcendentals=0),
    )(info, *args)


def ffn_fwd_body(tick, micros, first_tick, info, hid, we, be, wr, br, gain, shift, *rest):
    rest = rest[6:] if not first_tick else rest
    act_out, slope_out, out_all, n_out, inv_out, sq_out, send_out, acc = rest
    j = pl.program_id(0)
    micro = fwd_micro(info, tick, micros)
    rows = hid.shape[0]
    step = 128
    for r in range(rows // step):
        at = slice(r * step, r * step + step)
        inner = dot_nn(hid[at], we[...]) + be[...]
        active, slope = gelu_pair(inner)
        active = active.astype(BF)
        act_out[at] = active
        slope_out[at] = slope.astype(BF)
        part = dot_nn(active, wr[...])

        @pl.when(j == 0)
        def _():
            acc[at] = part

        @pl.when(j > 0)
        def _():
            acc[at] += part

    @pl.when(j == pl.num_programs(0) - 1)
    def _():
        b2 = acc[...] + br[...]
        n, inv = norm_rows(hid[...].astype(F32) + b2)
        out = (n * gain[...] + shift[...]).astype(BF)
        out_all[...] = out
        send_out[...] = out
        n_out[...] = n.astype(BF)
        inv_out[...] = inv
        mask = usable_rows(info, micro, rows)
        sq_out[0:1, :] = jnp.sum(mask * b2 * b2, axis=0, keepdims=True)


def ffn_forward(tick, micros, info, hidden, weights, old):
    (we, be, wr, br, gains, shifts) = weights
    _, rows, width = hidden.shape
    ff = we.shape[1]
    steps = ff // FFBLOCK
    first = old is None
    slot = lambda info: fwd_micro(info, tick, micros)
    one = lambda *shape: pl.BlockSpec(shape, lambda g, info: (0,) * len(shape))
    in_specs = [
        pl.BlockSpec((None, rows, width), lambda g, i: (slot(i), 0, 0)),
        pl.BlockSpec((width, FFBLOCK), lambda g, i: (0, g)),
        pl.BlockSpec((1, FFBLOCK), lambda g, i: (0, g)),
        pl.BlockSpec((FFBLOCK, width), lambda g, i: (g, 0)),
        one(1, width),
        one(1, width),
        one(1, width),
    ]
    args = [hidden, we, be, wr, br, gains[1:2], shifts[1:2]]
    shapes = [
        ((micros, rows, ff), BF, (None, rows, FFBLOCK), lambda g, i: (slot(i), 0, g)),
        ((micros, rows, ff), BF, (None, rows, FFBLOCK), lambda g, i: (slot(i), 0, g)),
        ((micros, rows, width), BF, (None, rows, width), lambda g, i: (slot(i), 0, 0)),
        ((micros, rows, width), BF, (None, rows, width), lambda g, i: (slot(i), 0, 0)),
        ((micros, rows, 1), F32, (None, rows, 1), lambda g, i: (slot(i), 0, 0)),
        ((micros, 8, width), F32, (None, 8, width), lambda g, i: (slot(i), 0, 0)),
        ((rows, width), BF, (rows, width), lambda g, i: (0, 0)),
    ]
    return call(
        functools.partial(ffn_fwd_body, tick, micros, first),
        steps, info, args, in_specs, shapes, old,
        [pltpu.VMEM((rows, width), F32)],
        flops=4 * rows * width * ff,
    )


def column_sum(value):
    return jnp.sum(value, axis=0, keepdims=True)


def norm_rows_back(grad_out, n, inv, gain):
    grad_unit = grad_out * gain
    mean_grad = jnp.mean(grad_unit, axis=1, keepdims=True)
    mean_along = jnp.mean(grad_unit * n, axis=1, keepdims=True)
    return inv * (grad_unit - mean_grad - n * mean_along)


def loss_parts(info, micro, micros, grad_scale, out_b, wc):
    ends = ends_of(info, micro)
    embedded = dot_nn(out_b, wc)
    inv_norm = lax.rsqrt(jnp.sum(embedded * embedded, axis=1, keepdims=True) + UNIT_EPSILON)
    unit = embedded * inv_norm
    unit_b = unit.astype(BF)
    queries, passages = unit_b[:QROWS], unit_b[QROWS:]
    scaled = dot_nt(queries, passages) / SMOOTHING
    owner = passage_of(lax.broadcasted_iota(jnp.int32, (1, PSLOTS), 1), ends)
    top = jnp.max(jnp.where(owner < NP, scaled, NEG), axis=1, keepdims=True)
    terms = jnp.exp(scaled - top)
    lane = lax.broadcasted_iota(jnp.int32, (1, 128), 1)
    totals = jnp.ones((QROWS, 128), F32)
    lengths = jnp.ones((1, 128), F32)
    for j in range(NP):
        total = jnp.sum(jnp.where(owner == j, terms, 0.0), axis=1, keepdims=True)
        totals = jnp.where(lane == j, total, totals)
        lengths = jnp.where(lane == j, info[1 + micro * NP + j].astype(F32), lengths)
    smooth = SMOOTHING * (jnp.log(totals) + top - jnp.log(lengths))
    grouped = jnp.sum(smooth.reshape(NQ, QLEN, 128), axis=1, keepdims=True)
    scores = LOGIT_SCALE * grouped
    scores = jnp.where(lane[None] < NP, scores, NEG)
    score_max = jnp.max(scores, axis=2, keepdims=True)
    score_exp = jnp.exp(scores - score_max)
    score_total = jnp.sum(score_exp, axis=2, keepdims=True)
    query = lax.broadcasted_iota(jnp.int32, (NQ, 1, 128), 0)
    chosen = jnp.zeros((NQ, 1, 128), jnp.int32)
    for i in range(NQ):
        chosen = jnp.where(query == i, info[1 + micros * NP + micro * NQ + i], chosen)
    onehot = (chosen == lane[None]).astype(F32)
    own_score = jnp.sum(jnp.where(chosen == lane[None], scores, 0.0), axis=2, keepdims=True)
    losses = jnp.log(score_total) + score_max - own_score
    loss = jnp.sum(losses, axis=0)
    grad_scores = (score_exp / score_total - onehot) * grad_scale
    grad_smooth = jnp.broadcast_to(LOGIT_SCALE * grad_scores, (NQ, QLEN, 128)).reshape(QROWS, 128)
    share = grad_smooth / totals
    weight = jnp.zeros((QROWS, PSLOTS), F32)
    for j in range(NP):
        weight = jnp.where(owner == j, share[:, j : j + 1], weight)
    grad_similar = jnp.where(owner < NP, terms * weight, 0.0).astype(BF)
    grad_unit = jnp.concatenate([dot_nn(grad_similar, passages), dot_tn(grad_similar, queries)])
    grad_embed = inv_norm * (grad_unit - unit * jnp.sum(grad_unit * unit, axis=1, keepdims=True))
    return loss, grad_embed.astype(BF)


def ffn_bwd_body(tick, micros, grad_scale, first_tick, info, out_all, wc, rec, n2, inv2, gain2, slope, wr, we, n1, inv1, gain1, *rest):
    rest = rest[6:] if not first_tick else rest
    two_out, inner_out, one_out, emb_out, small_out, ff_out, resid_out, acc, resid, grad = rest
    j = pl.program_id(0)
    micro = bwd_micro(info, tick, micros)

    @pl.when(j == 0)
    def _():
        small_out[...] = jnp.zeros(small_out.shape, F32)

        @pl.when(info[0] == 1)
        def _():
            loss, grad_embed = loss_parts(info, micro, micros, grad_scale, out_all[...], wc[...])
            emb_out[...] = grad_embed
            grad[...] = dot_nt(grad_embed, wc[...])
            small_out[6:7, 0:128] = jnp.broadcast_to(loss, (1, 128))

        @pl.when(info[0] == 0)
        def _():
            emb_out[...] = jnp.zeros(emb_out.shape, BF)
            grad[...] = rec[...].astype(F32)

        upstream = grad[...]
        n = n2[...].astype(F32)
        small_out[0:1, :] = column_sum(upstream * n)
        small_out[1:2, :] = column_sum(upstream)
        d_two = norm_rows_back(upstream, n, inv2[...], gain2[...])
        resid[...] = d_two
        d_two_b = d_two.astype(BF)
        two_out[...] = d_two_b
        small_out[2:3, :] = column_sum(d_two_b.astype(F32))

    rows = two_out.shape[0]
    step = 128
    total = jnp.zeros((1, FFBLOCK), F32)
    for r in range(rows // step):
        at = slice(r * step, r * step + step)
        d_act = dot_nt(two_out[at], wr[...])
        d_inner = (d_act * slope[at].astype(F32)).astype(BF)
        inner_out[at] = d_inner
        total = total + column_sum(d_inner.astype(F32))
        part = dot_nt(d_inner, we[...])

        @pl.when(j == 0)
        def _():
            acc[at] = part

        @pl.when(j > 0)
        def _():
            acc[at] += part
    ff_out[0:1, :] = total

    @pl.when(j == pl.num_programs(0) - 1)
    def _():
        upstream = resid[...] + acc[...]
        n = n1[...].astype(F32)
        small_out[3:4, :] = column_sum(upstream * n)
        small_out[4:5, :] = column_sum(upstream)
        d_one = norm_rows_back(upstream, n, inv1[...], gain1[...])
        resid_out[...] = d_one
        d_one_b = d_one.astype(BF)
        one_out[...] = d_one_b
        small_out[5:6, :] = column_sum(d_one_b.astype(F32))


def ffn_backward(tick, micros, grad_scale, info, received, kept, weights, old):
    (out_all, n2, inv2, slope, n1, inv1) = kept
    (wc, gains, wr, we) = weights
    _, rows, width = out_all.shape
    ff = we.shape[1]
    steps = ff // FFBLOCK
    first = old is None
    slot = lambda info: bwd_micro(info, tick, micros)
    one = lambda *shape: pl.BlockSpec(shape, lambda g, info: (0,) * len(shape))
    at_slot = lambda *shape: pl.BlockSpec((None,) + shape, lambda g, i: (slot(i), 0, 0))
    in_specs = [
        at_slot(rows, width),
        one(*wc.shape),
        one(rows, width),
        at_slot(rows, width),
        at_slot(rows, 1),
        one(1, width),
        pl.BlockSpec((None, rows, FFBLOCK), lambda g, i: (slot(i), 0, g)),
        pl.BlockSpec((FFBLOCK, width), lambda g, i: (g, 0)),
        pl.BlockSpec((width, FFBLOCK), lambda g, i: (0, g)),
        at_slot(rows, width),
        at_slot(rows, 1),
        one(1, width),
    ]
    args = [out_all, wc, received, n2, inv2, gains[1:2], slope, wr, we, n1, inv1, gains[0:1]]
    emb = wc.shape[1]
    shapes = [
        ((micros, rows, width), BF, (None, rows, width), lambda g, i: (slot(i), 0, 0)),
        ((micros, rows, ff), BF, (None, rows, FFBLOCK), lambda g, i: (slot(i), 0, g)),
        ((micros, rows, width), BF, (None, rows, width), lambda g, i: (slot(i), 0, 0)),
        ((micros, rows, emb), BF, (None, rows, emb), lambda g, i: (slot(i), 0, 0)),
        ((micros, 8, width), F32, (None, 8, width), lambda g, i: (slot(i), 0, 0)),
        ((micros, 8, ff), F32, (None, 8, FFBLOCK), lambda g, i: (slot(i), 0, g)),
        ((rows, width), F32, (rows, width), lambda g, i: (0, 0)),
    ]
    return call(
        functools.partial(ffn_bwd_body, tick, micros, grad_scale, first),
        steps, info, args, in_specs, shapes, old,
        [pltpu.VMEM((rows, width), F32), pltpu.VMEM((rows, width), F32), pltpu.VMEM((rows, width), F32)],
        flops=4 * rows * width * ff,
    )


def attn_bwd_body(tick, micros, first_tick, info, resid, one_b, joined, lse, ctx, wm, wq, wk, wv, *rest):
    rest = rest[4:] if not first_tick else rest
    dq_out, dk_out, dv_out, sum_out, send_out, acc, bias, dctx, delta, ktr, dqtr, pbuf, sbuf = rest
    g = pl.program_id(0)
    micro = bwd_micro(info, tick, micros)

    @pl.when(g == 0)
    def _():
        fill_masks(info, micro, bias)

    dctx32 = dot_nt(one_b[...], wm[...])
    dctx[...] = dctx32.astype(BF)
    along = dctx[...].astype(F32) * ctx[...].astype(F32)
    pick = lax.broadcasted_iota(jnp.int32, (8, SLAB), 0) == lax.broadcasted_iota(jnp.int32, (8, SLAB), 1) // HEAD_DIM
    delta[...] = lax.dot_general(
        pick.astype(F32), along, (((1,), (1,)), ((), ())),
        precision=lax.Precision.HIGHEST, preferred_element_type=F32,
    )
    ktr[...] = jnp.transpose(joined[:, SLAB : 2 * SLAB])
    qbias = query_bias()
    for pair in range(SLAB // 128):
        lo = pair * 128
        qs = joined[:, lo : lo + 128] * BF(HEAD_DIM**-0.5)
        ks = joined[:, SLAB + lo : SLAB + lo + 128]
        vs = joined[:, 2 * SLAB + lo : 2 * SLAB + lo + 128]
        do = dctx[:, lo : lo + 128]
        qms = []
        dos = []
        pq = []
        sq = []
        for h in range(2):
            head = pair * 2 + h
            qm = half_lanes(qs, h)
            dm = half_lanes(do, h)
            qms.append(qm)
            dos.append(dm)
            kh = slice(head * HEAD_DIM, head * HEAD_DIM + HEAD_DIM)
            st = dot_nt(ks[:QROWS], qm[:QROWS]) + qbias
            p = jnp.exp(st - lse[head : head + 1, 0:QROWS])
            dp = dot_nt(vs[:QROWS], dm[:QROWS])
            ds = (p * (dp - delta[head : head + 1, 0:QROWS])).astype(BF)
            pq.append(p.astype(BF))
            sq.append(ds)
            dqtr[kh, 0:QROWS] = dot_nn(ktr[kh, 0:QROWS], ds)
            for c in range(PSLOTS // 256):
                at = slice(QROWS + c * 256, QROWS + c * 256 + 256)
                into = slice(h * PSLOTS + c * 256, h * PSLOTS + c * 256 + 256)
                st = dot_nt(ks[QROWS:], qm[at]) + bias[:, c * 256 : c * 256 + 256]
                p = jnp.exp(st - lse[head : head + 1, at])
                dp = dot_nt(vs[QROWS:], dm[at])
                ds = (p * (dp - delta[head : head + 1, at])).astype(BF)
                pbuf[:, into] = p.astype(BF)
                sbuf[:, into] = ds
                dqtr[kh, at] = dot_nn(ktr[kh, QROWS:], ds)
        both_q = jnp.concatenate(qms)
        rows = qs.shape[0]
        q_heads = jnp.concatenate([qms[0][:QROWS], qms[1][:QROWS]])
        d_heads = jnp.concatenate([dos[0][:QROWS], dos[1][:QROWS]])
        dk_out[0:QROWS, lo : lo + 128] = dot_nn(jnp.concatenate(sq, axis=1), q_heads).astype(BF)
        dv_out[0:QROWS, lo : lo + 128] = dot_nn(jnp.concatenate(pq, axis=1), d_heads).astype(BF)
        q_heads = jnp.concatenate([qms[0][QROWS:], qms[1][QROWS:]])
        d_heads = jnp.concatenate([dos[0][QROWS:], dos[1][QROWS:]])
        dk_out[QROWS:rows, lo : lo + 128] = dot_nn(sbuf[...], q_heads).astype(BF)
        dv_out[QROWS:rows, lo : lo + 128] = dot_nn(pbuf[...], d_heads).astype(BF)
    dq = (jnp.transpose(dqtr[...]) * HEAD_DIM**-0.5).astype(BF)
    dq_out[...] = dq
    dk = dk_out[...]
    dv = dv_out[...]
    sum_out[0:1, 0:SLAB] = column_sum(dq.astype(F32))
    sum_out[0:1, SLAB : 2 * SLAB] = column_sum(dv.astype(F32))
    part = dot_nt(dq, wq[...]) + dot_nt(dk, wk[...]) + dot_nt(dv, wv[...])

    @pl.when(g == 0)
    def _():
        acc[...] = part

    @pl.when(g > 0)
    def _():
        acc[...] += part

    @pl.when(g == pl.num_programs(0) - 1)
    def _():
        send_out[...] = (resid[...] + acc[...]).astype(BF)


def attn_backward(tick, micros, info, resid, one_all, kept, weights, old):
    (joined, lse, ctx) = kept
    (wa, wm) = weights
    _, rows, width = one_all.shape
    steps = width // SLAB
    first = old is None
    slot = lambda info: bwd_micro(info, tick, micros)
    one = lambda *shape: pl.BlockSpec(shape, lambda g, info: (0,) * len(shape))
    in_specs = [
        one(rows, width),
        pl.BlockSpec((None, rows, width), lambda g, i: (slot(i), 0, 0)),
        pl.BlockSpec((None, None, rows, 3 * SLAB), lambda g, i: (slot(i), g, 0, 0)),
        pl.BlockSpec((None, None, 8, rows), lambda g, i: (slot(i), g, 0, 0)),
        pl.BlockSpec((None, rows, SLAB), lambda g, i: (slot(i), 0, g)),
        pl.BlockSpec((SLAB, width), lambda g, i: (g, 0)),
        pl.BlockSpec((width, SLAB), lambda g, i: (0, g)),
        pl.BlockSpec((width, SLAB), lambda g, i: (0, steps + g)),
        pl.BlockSpec((width, SLAB), lambda g, i: (0, 2 * steps + g)),
    ]
    args = [resid, one_all, joined, lse, ctx, wm, wa, wa, wa]
    slab = ((micros, rows, width), BF, (None, rows, SLAB), lambda g, i: (slot(i), 0, g))
    shapes = [
        slab,
        slab,
        slab,
        ((micros, steps, 8, 2 * SLAB), F32, (None, None, 8, 2 * SLAB), lambda g, i: (slot(i), g, 0, 0)),
        ((rows, width), BF, (rows, width), lambda g, i: (0, 0)),
    ]
    return call(
        functools.partial(attn_bwd_body, tick, micros, first),
        steps, info, args, in_specs, shapes, old,
        [
            pltpu.VMEM((rows, width), F32),
            pltpu.VMEM((PSLOTS, PSLOTS), F32),
            pltpu.VMEM((rows, SLAB), BF),
            pltpu.VMEM((8, rows), F32),
            pltpu.VMEM((SLAB, rows), BF),
            pltpu.VMEM((SLAB, rows), F32),
            pltpu.VMEM((PSLOTS, 2 * PSLOTS), BF),
            pltpu.VMEM((PSLOTS, 2 * PSLOTS), BF),
        ],
        flops=2 * rows * width * width * 4 + 10 * 12 * 64 * rows * rows,
    )


def mesh_bits():
    place = lax.axis_index("dp")
    bits = []
    bit = 1
    while bit < lax.axis_size("dp"):
        bits.append((bit, (place // bit) % 2))
        bit *= 2
    return bits


def grad_rows_body(info, left, right, first_out, second_out):
    step = pl.program_id(0)
    value = dot_nn(jnp.transpose(left[...]), right[...]).astype(BF)

    @pl.when(step < 2)
    def _():
        first_out[...] = value

    @pl.when(step >= 2)
    def _():
        second_out[...] = value


def grad_rows(half, left, right):
    tall, wide = left.shape[1], right.shape[1]
    block = tall // 8
    out = jax.ShapeDtypeStruct((tall // 4, wide), BF)
    return pl.pallas_call(
        grad_rows_body,
        out_shape=[out, out],
        grid_spec=pltpu.PrefetchScalarGridSpec(
            num_scalar_prefetch=1,
            grid=(4,),
            in_specs=[
                pl.BlockSpec((left.shape[0], block), lambda s, h: (0, h[0] * 4 + s)),
                pl.BlockSpec(right.shape, lambda s, h: (0, 0)),
            ],
            out_specs=[
                pl.BlockSpec((block, wide), lambda s, h: (jnp.minimum(s, 1), 0)),
                pl.BlockSpec((block, wide), lambda s, h: (jnp.maximum(s - 2, 0), 0)),
            ],
        ),
        compiler_params=pltpu.CompilerParams(vmem_limit_bytes=VMEM_LIMIT),
        cost_estimate=pl.CostEstimate(flops=left.shape[0] * tall * wide, bytes_accessed=8_000_000, transcendentals=0),
    )(half, left, right)


def grad_columns_body(info, left, right, first_out, second_out, turned):
    step = pl.program_id(0)

    @pl.when(step == 0)
    def _():
        turned[...] = jnp.transpose(left[...])

    value = dot_nn(turned[...], right[...]).astype(BF)

    @pl.when(step < 2)
    def _():
        first_out[...] = value

    @pl.when(step >= 2)
    def _():
        second_out[...] = value


def grad_columns(half, left, right):
    tall, wide = left.shape[1], right.shape[1]
    block = wide // 4
    out = jax.ShapeDtypeStruct((tall // 2, wide // 2), BF)
    return pl.pallas_call(
        grad_columns_body,
        out_shape=[out, out],
        grid_spec=pltpu.PrefetchScalarGridSpec(
            num_scalar_prefetch=1,
            grid=(4,),
            in_specs=[
                pl.BlockSpec((left.shape[0], tall // 2), lambda s, h: (0, h[0])),
                pl.BlockSpec((right.shape[0], block), lambda s, h: (0, s)),
            ],
            out_specs=[
                pl.BlockSpec((tall // 2, block), lambda s, h: (0, jnp.minimum(s, 1))),
                pl.BlockSpec((tall // 2, block), lambda s, h: (0, jnp.maximum(s - 2, 0))),
            ],
            scratch_shapes=[pltpu.VMEM((tall // 2, left.shape[0]), BF)],
        ),
        compiler_params=pltpu.CompilerParams(vmem_limit_bytes=VMEM_LIMIT),
        cost_estimate=pl.CostEstimate(flops=left.shape[0] * tall * wide, bytes_accessed=8_000_000, transcendentals=0),
    )(half, left, right)


def grad_rest_body(info, inputs, context, d_query, d_key, d_value, d_one, first_out, second_out):
    width = d_one.shape[1]
    turned = jnp.transpose(inputs[...])
    first_out[:, :width] = dot_nn(turned, d_query[...]).astype(BF)
    first_out[:, width:] = dot_nn(turned, d_key[...]).astype(BF)
    second_out[:, :width] = dot_nn(turned, d_value[...]).astype(BF)
    second_out[:, width:] = dot_nn(jnp.transpose(context[...]), d_one[...]).astype(BF)


def grad_rest(half, inputs, context, d_query, d_key, d_value, d_one):
    width = inputs.shape[1]
    out = jax.ShapeDtypeStruct((width // 2, 2 * width), BF)
    side = pl.BlockSpec((inputs.shape[0], width // 2), lambda s, h: (0, h[0]))
    full = pl.BlockSpec(d_one.shape, lambda s, h: (0, 0))
    whole = pl.BlockSpec((width // 2, 2 * width), lambda s, h: (0, 0))
    return pl.pallas_call(
        grad_rest_body,
        out_shape=[out, out],
        grid_spec=pltpu.PrefetchScalarGridSpec(
            num_scalar_prefetch=1,
            grid=(1,),
            in_specs=[side, side, full, full, full, full],
            out_specs=[whole, whole],
        ),
        compiler_params=pltpu.CompilerParams(vmem_limit_bytes=VMEM_LIMIT),
        cost_estimate=pl.CostEstimate(flops=inputs.shape[0] * 4 * width * width, bytes_accessed=12_000_000, transcendentals=0),
    )(half, inputs, context, d_query, d_key, d_value, d_one)


def widen_body(info, own_a, own_b, other_a, other_b, *outs):
    step = pl.program_id(0)
    for s, (a, b) in enumerate(((own_a, own_b), (other_a, other_b))):

        @pl.when(step == s)
        def _(a=a, b=b):
            parts = (a[...].astype(F32), b[...].astype(F32))
            if len(outs) == 2:
                third = outs[1].shape[1]
                outs[0][:, : 2 * third] = parts[0]
                outs[0][:, 2 * third :] = parts[1][:, :third]
                outs[1][...] = parts[1][:, third:]
            elif outs[0].shape[1] == parts[0].shape[1]:
                outs[0][: parts[0].shape[0]] = parts[0]
                outs[0][parts[0].shape[0] :] = parts[1]
            else:
                outs[0][:, : parts[0].shape[1]] = parts[0]
                outs[0][:, parts[0].shape[1] :] = parts[1]


def widened(core, own, other, out_shapes):
    small = own[0].shape
    piece_spec = pl.BlockSpec(small, lambda s, h: (0, 0))
    return pl.pallas_call(
        widen_body,
        out_shape=[jax.ShapeDtypeStruct(shape, F32) for shape in out_shapes],
        grid_spec=pltpu.PrefetchScalarGridSpec(
            num_scalar_prefetch=1,
            grid=(2,),
            in_specs=[piece_spec] * 4,
            out_specs=[
                pl.BlockSpec((shape[0] // 2, shape[1]), lambda s, h: (jnp.where(s == 0, h[0], 1 - h[0]), 0))
                for shape in out_shapes
            ],
        ),
        compiler_params=pltpu.CompilerParams(vmem_limit_bytes=VMEM_LIMIT),
        cost_estimate=pl.CostEstimate(flops=0, bytes_accessed=14_000_000, transcendentals=0),
    )(core, *own, *other)


def passed_along(array, axis, by):
    count = lax.axis_size(axis)
    pairs = [(i, i + by) for i in range(count) if 0 <= i + by < count]
    return lax.ppermute(array, axis, pairs)


def flatten_rows(leaf):
    return leaf.reshape(-1, leaf.shape[-1])


def swapped(array, bit, axis="dp"):
    count = lax.axis_size(axis)
    return lax.ppermute(array, axis, [(i, i ^ bit) for i in range(count)])


def piece(array, index):
    return lax.dynamic_index_in_dim(array, index, 0, keepdims=False)


def sum_low(kept, got):
    return (kept.astype(F32) + got.astype(F32)).astype(BF)


def halved(array, bit):
    step, mine = bit
    halves = array.reshape(2, array.shape[0] // 2, array.shape[1])
    got = swapped(piece(halves, 1 - mine), step)
    return sum_low(piece(halves, mine), got)


def doubled(array, bit):
    step, mine = bit
    got = swapped(array, step)
    both = jnp.zeros((2,) + array.shape, array.dtype)
    both = lax.dynamic_update_index_in_dim(both, array, mine, 0)
    both = lax.dynamic_update_index_in_dim(both, got, 1 - mine, 0)
    return flatten_rows(both)


def summed_halves(sent, kept, bits, orders):
    own, other = [], []
    for send, keep, order in zip(sent, kept, orders):
        total = sum_low(keep, swapped(send, 1))
        for place in order:
            total = halved(total, bits[place])
        for place in reversed(order):
            total = doubled(total, bits[place])
        own.append(total)
        other.append(swapped(total, 1))
    return own, other


def all_summed(array, bits):
    for step, _ in bits:
        array = (array.astype(F32) + swapped(array, step).astype(F32)).astype(array.dtype)
    return array


def shards(
    hidden_in,
    attend_weight,
    attend_bias,
    mixing_weight,
    mixing_bias,
    norm_gain,
    norm_shift,
    expand_weight,
    expand_bias,
    reduce_weight,
    reduce_bias,
    colbert_weight,
    pass_lengths,
    positives,
):
    section_id = lax.axis_index("pipe")
    data_count = lax.axis_size("dp")
    micros = pass_lengths.shape[0]
    rows = hidden_in.shape[0] // micros
    width = hidden_in.shape[1]
    grad_scale = 1.0 / (data_count * micros * NQ)
    wa, wm, we, wr = attend_weight[0], mixing_weight[0], expand_weight[0], reduce_weight[0]
    gains, shifts = norm_gain[0], norm_shift[0]
    info = jnp.concatenate(
        [section_id.astype(jnp.int32)[None], pass_lengths.reshape(-1), positives.reshape(-1)]
    )
    bits = mesh_bits()
    core = bits[0][1].astype(jnp.int32)[None]
    along_x_first = list(range(1, len(bits)))
    along_z_first = [2, 1] + list(range(3, len(bits)))
    orders = (along_x_first, along_z_first)
    attn_weights = (wa, attend_bias, wm, mixing_bias, gains, shifts)
    ffn_weights = (we, expand_bias, wr, reduce_bias, gains, shifts)
    received = jnp.zeros((rows, width), BF)
    attn, ffn = None, None
    for tick in range(micros + 1):
        attn = attn_forward(tick, micros, info, hidden_in, received, attn_weights, attn)
        ffn = ffn_forward(tick, micros, info, attn[4], ffn_weights, ffn and ffn[:6])
        if tick < micros:
            received = passed_along(ffn[6], "pipe", 1)
    inputs, joined, lse, context, hidden, unit_one, inv_one, squares_one = attn
    active, slope, outputs, unit_two, inv_two, squares_two, _ = ffn
    squares = jnp.stack(
        [
            jnp.sum(squares_one[:, 0], axis=1),
            jnp.sum(squares_one[:, 1], axis=1),
            jnp.sum(squares_two[:, 0], axis=1),
        ],
        axis=1,
    )
    received = jnp.zeros((rows, width), BF)
    ffn_back, attn_back = None, None
    for tick in range(micros + 1):
        ffn_back = ffn_backward(
            tick, micros, grad_scale, info, received,
            (outputs, unit_two, inv_two, slope, unit_one, inv_one),
            (colbert_weight, gains, wr, we), ffn_back and ffn_back[:6],
        )
        if tick == micros - 1:
            colbert = dot_tn(flatten_rows(outputs), flatten_rows(ffn_back[3])).astype(BF)
            colbert = jnp.where(section_id == 1, colbert, swapped(colbert, 1, "pipe"))
            colbert_sum = all_summed(colbert, bits).astype(F32)
            facts = jnp.concatenate([squares, ffn_back[4][:, 6, 0:1]], axis=1)
            theirs = swapped(facts, 1, "pipe")
            first = jnp.where(section_id == 0, facts, theirs)
            second = jnp.where(section_id == 0, theirs, facts)
        if tick == micros:
            d_two, d_inner = flatten_rows(ffn_back[0]), flatten_rows(ffn_back[1])
            left = flatten_rows(active)
            sent_reduce, kept_reduce = (grad_rows(half, left, d_two) for half in (1 - core, core))
            left = flatten_rows(hidden)
            sent_expand, kept_expand = (grad_columns(half, left, d_inner) for half in (1 - core, core))
        attn_back = attn_backward(
            tick, micros, info, ffn_back[6], ffn_back[2], (joined, lse, context), (wa, wm),
            attn_back and attn_back[:4],
        )
        if tick < micros:
            received = passed_along(attn_back[4], "pipe", -1)
    small, small_ff = ffn_back[4], ffn_back[5]
    d_query, d_key, d_value, joined_sums, _ = attn_back
    sides = [flatten_rows(a) for a in (inputs, context, d_query, d_key, d_value, ffn_back[2])]
    sent_rest, kept_rest = (grad_rest(half, *sides) for half in (1 - core, core))
    small_sum = jnp.sum(small, axis=0)
    joined_sum = jnp.sum(joined_sums[:, :, 0], axis=0)
    attend_sum = jnp.concatenate(
        [joined_sum[:, :SLAB].reshape(-1), joined_sum[:, SLAB:].reshape(-1)]
    )
    vector = jnp.concatenate(
        [small_sum[:6], attend_sum.reshape(2, width), jnp.sum(small_ff[:, 0], axis=0).reshape(-1, width)]
    )
    vector = all_summed(vector, bits)
    halves = summed_halves(sent_reduce, kept_reduce, bits, orders)
    [big_reduce] = widened(core, *halves, [wr.shape])
    halves = summed_halves(sent_expand, kept_expand, bits, orders)
    [big_expand] = widened(core, *halves, [we.shape])
    halves = summed_halves(sent_rest, kept_rest, bits, orders)
    big_attend, big_mixing = widened(core, *halves, [wa.shape, wm.shape])
    counted = (QROWS + jnp.sum(pass_lengths, axis=1)).astype(F32)
    stats = jnp.stack([first[:, :3], second[:, :3]], axis=1)
    stats = jnp.sqrt(stats / (counted[:, None, None] * width))
    return (
        big_attend[None],
        vector[6:8].reshape(1, -1),
        big_mixing[None],
        vector[5][None],
        jnp.stack([vector[3], vector[0]])[None],
        jnp.stack([vector[4], vector[1]])[None],
        big_expand[None],
        vector[8:].reshape(1, -1),
        big_reduce[None],
        vector[2][None],
        colbert_sum,
        second[:, 3] / NQ,
        stats,
    )


def solution(mesh):
    placed = (
        P("dp", None),
        P("pipe", None, None),
        P("pipe", None),
        P("pipe", None, None),
        P("pipe", None),
        P("pipe", None, None),
        P("pipe", None, None),
        P("pipe", None, None),
        P("pipe", None),
        P("pipe", None, None),
        P("pipe", None),
        P(),
        P("dp", None),
        P("dp", None),
    )
    return jax.shard_map(
        shards,
        mesh=mesh,
        in_specs=placed,
        out_specs=(
            P("pipe", None, None),
            P("pipe", None),
            P("pipe", None, None),
            P("pipe", None),
            P("pipe", None, None),
            P("pipe", None, None),
            P("pipe", None, None),
            P("pipe", None),
            P("pipe", None, None),
            P("pipe", None),
            P(),
            P("dp"),
            P("dp", None, None),
        ),
        check_vma=False,
    )
```

```python
import functools
import jax
import jax.numpy as jnp
from jax import lax
from jax.experimental import pallas as pl
from jax.experimental.pallas import tpu as pltpu
from jax.sharding import PartitionSpec as P

HEAD_DIM = 64
QLEN = 32
NQ = 4
NP = 4
PSLOTS = 512
LAYER_EPSILON = 1e-12
UNIT_EPSILON = 1e-06
SMOOTHING = 0.05
LOGIT_SCALE = 4.0
ROOT_HALF = 0.7071067811865476
NORMAL_PEAK = 0.3989422804014327
BF = jnp.bfloat16
F32 = jnp.float32
QROWS = NQ * QLEN
SLAB = 256
FFBLOCK = 768
VMEM_LIMIT = 56 * 1024 * 1024
NEG = -1e30
FLOPS_FFN = 12_000_000_000
FLOPS_ATTN = 20_000_000_000


def dot_nn(a, b):
    return jnp.dot(a, b, preferred_element_type=F32)


def dot_nt(a, b):
    return lax.dot_general(a, b, (((1,), (1,)), ((), ())), preferred_element_type=F32)


def dot_tn(a, b):
    return lax.dot_general(a, b, (((0,), (0,)), ((), ())), preferred_element_type=F32)


def gelu_pair(u):
    phi = 0.5 + 0.5 * lax.erf(u * ROOT_HALF)
    return u * phi, phi + NORMAL_PEAK * u * jnp.exp(-0.5 * u * u)


def norm_rows(resid):
    centre = resid - jnp.mean(resid, axis=1, keepdims=True)
    inv = lax.rsqrt(jnp.mean(centre * centre, axis=1, keepdims=True) + LAYER_EPSILON)
    return centre * inv, inv


def ends_of(info, micro):
    base = 1 + micro * NP
    ends = []
    total = jnp.int32(0)
    for j in range(NP):
        total = total + info[base + j]
        ends.append(total)
    return ends


def passage_of(place, ends):
    out = jnp.zeros(place.shape, jnp.int32)
    for end in ends:
        out = out + jnp.where(place >= end, 1, 0)
    return out


def when_live(info, section, body):
    pl.when(info[0] == section)(body)


def slot_of(info, section, micro, spare):
    return jnp.where(info[0] == section, micro, spare)


def step_of(info, section, step):
    return jnp.where(info[0] == section, step, 0)


def fill_codes(info, micro, query_code, key_code):
    rows = query_code.shape[0]
    ends = [QROWS + end for end in ends_of(info, micro)]
    place = lax.broadcasted_iota(jnp.int32, (rows, 1), 0)
    segment = jnp.where(place < QROWS, place // QLEN, NQ + passage_of(place, ends))
    lane = lax.broadcasted_iota(jnp.int32, (1, 128), 1) % HEAD_DIM
    query_code[...] = jnp.where(segment == lane, 1.0, 0.0).astype(BF)
    key_code[...] = jnp.where((segment == lane) | (lane > NQ + NP), 0.0, NEG).astype(BF)


def usable_rows(info, micro, rows):
    ends = ends_of(info, micro)
    place = lax.broadcasted_iota(jnp.int32, (rows, 1), 0)
    return (place < QROWS + ends[-1]).astype(F32)


def head_lanes(value, h, others):
    lane = lax.broadcasted_iota(jnp.int32, (1, 128), 1) // HEAD_DIM
    return jnp.where(lane == h, value, others)


def live_only(body, section, micro):
    def kernel(info, *refs):
        when_live(info, section, lambda: body(micro, info, *refs))

    return kernel


def attn_fwd_live(micro, info, hid, wq, wk, wv, bq, bv, wm, bm, gain, shift, *rest):
    x_out, joined_out, lse_out, ctx_out, hid_out, n_out, inv_out, sq_out, acc, qcode, kcode, otr, vtr = rest[-13:]
    g = pl.program_id(0)
    rows = hid.shape[0]

    @pl.when(g == 0)
    def _():
        x_out[...] = hid[...]
        fill_codes(info, micro, qcode, kcode)
        acc[...] = jnp.zeros(acc.shape, F32)

    x = hid[...]
    qkv = dot_nn(x, jnp.concatenate([wq[...], wk[...], wv[...]], axis=1))
    q = (qkv[:, :SLAB] + bq[...]).astype(BF)
    joined_out[:, 0:SLAB] = q
    k = qkv[:, SLAB : 2 * SLAB].astype(BF)
    joined_out[:, SLAB : 2 * SLAB] = k
    v = (qkv[:, 2 * SLAB :] + bv[...]).astype(BF)
    joined_out[:, 2 * SLAB : 3 * SLAB] = v
    vtr[...] = jnp.transpose(v)
    parts = (slice(0, QROWS), slice(QROWS, rows))
    for pair in range(SLAB // 128):
        cols = slice(pair * 128, pair * 128 + 128)
        qs = joined_out[:, cols] * BF(HEAD_DIM**-0.5)
        ks = joined_out[:, SLAB + pair * 128 : SLAB + pair * 128 + 128]
        for h in range(2):
            head = pair * 2 + h
            vh = slice(head * HEAD_DIM, head * HEAD_DIM + HEAD_DIM)
            qh = head_lanes(qs, h, qcode[...])
            kh = head_lanes(ks, h, kcode[...])
            for at in parts:
                st = dot_nt(kh[at], qh[at])
                top = jnp.max(st, axis=0, keepdims=True)
                p = jnp.exp(st - top)
                total = jnp.sum(p, axis=0, keepdims=True)
                lse_out[head : head + 1, at] = top + jnp.log(total)
                otr[vh, at] = dot_nn(vtr[vh, at], p.astype(BF)) * (1.0 / total)
    ctx = jnp.transpose(otr[...]).astype(BF)
    ctx_out[...] = ctx
    acc[...] += dot_nn(ctx, wm[...])

    @pl.when(g == pl.num_programs(0) - 1)
    def _():
        b1 = acc[...] + bm[...]
        x32 = hid[...].astype(F32)
        n, inv = norm_rows(x32 + b1)
        hid_out[...] = (n * gain[...] + shift[...]).astype(BF)
        n_out[...] = n.astype(BF)
        inv_out[...] = inv
        mask = usable_rows(info, micro, rows)
        sq_out[0:1, :] = jnp.sum(mask * x32 * x32, axis=0, keepdims=True)
        sq_out[1:2, :] = jnp.sum(mask * b1 * b1, axis=0, keepdims=True)


def attn_forward(phase, micros, info, source, weights, old):
    (wa, ba, wm, bm, gains, shifts) = weights
    section, micro = phase // micros, phase % micros
    width = source.shape[1]
    rows = source.shape[0] // micros if section == 0 else source.shape[0]
    place = micro if section == 0 else 0
    steps = width // SLAB
    slot = lambda i: slot_of(i, section, micro, micros)
    at = lambda g, i: step_of(i, section, g)
    one = lambda *shape: pl.BlockSpec(shape, lambda g, i: (0,) * len(shape))
    in_specs = [
        pl.BlockSpec((rows, width), lambda g, i: (place, 0)),
        pl.BlockSpec((width, SLAB), lambda g, i: (0, at(g, i))),
        pl.BlockSpec((width, SLAB), lambda g, i: (0, steps + at(g, i))),
        pl.BlockSpec((width, SLAB), lambda g, i: (0, 2 * steps + at(g, i))),
        pl.BlockSpec((1, SLAB), lambda g, i: (0, at(g, i))),
        pl.BlockSpec((1, SLAB), lambda g, i: (0, steps + at(g, i))),
        pl.BlockSpec((SLAB, width), lambda g, i: (at(g, i), 0)),
        one(1, width),
        one(1, width),
        one(1, width),
    ]
    args = [source, wa, wa, wa, ba, ba, wm, bm, gains[0:1], shifts[0:1]]
    slots = micros + 1
    rows_at = lambda shape, kind: ((slots,) + shape, kind, (None,) + shape, lambda g, i: (slot(i), 0, 0))
    shapes = [
        rows_at((rows, width), BF),
        ((slots, steps, rows, 3 * SLAB), BF, (None, None, rows, 3 * SLAB), lambda g, i: (slot(i), at(g, i), 0, 0)),
        ((slots, steps, 8, rows), F32, (None, None, 8, rows), lambda g, i: (slot(i), at(g, i), 0, 0)),
        ((slots, rows, width), BF, (None, rows, SLAB), lambda g, i: (slot(i), 0, at(g, i))),
        rows_at((rows, width), BF),
        rows_at((rows, width), BF),
        rows_at((rows, 1), F32),
        rows_at((8, width), F32),
    ]
    return call(
        live_only(attn_fwd_live, section, micro),
        steps, info, args, in_specs, shapes, old,
        [
            pltpu.VMEM((rows, width), F32),
            pltpu.VMEM((rows, 128), BF),
            pltpu.VMEM((rows, 128), BF),
            pltpu.VMEM((SLAB, rows), F32),
            pltpu.VMEM((SLAB, rows), BF),
        ],
        flops=FLOPS_ATTN,
    )


def call(body, steps, info, args, in_specs, shapes, old, scratch, flops):
    aliases = {}
    if old is not None:
        in_specs = in_specs + [pl.BlockSpec(memory_space=pl.ANY)] * len(old)
        aliases = {1 + len(args) + i: i for i in range(len(old))}
        args = args + list(old)
    return pl.pallas_call(
        body,
        out_shape=[jax.ShapeDtypeStruct(s[0], s[1]) for s in shapes],
        grid_spec=pltpu.PrefetchScalarGridSpec(
            num_scalar_prefetch=1,
            grid=(steps,),
            in_specs=in_specs,
            out_specs=[pl.BlockSpec(s[2], s[3]) for s in shapes],
            scratch_shapes=scratch,
        ),
        input_output_aliases=aliases,
        compiler_params=pltpu.CompilerParams(
            dimension_semantics=("arbitrary",), vmem_limit_bytes=VMEM_LIMIT
        ),
        cost_estimate=pl.CostEstimate(flops=flops, bytes_accessed=20_000_000, transcendentals=0),
    )(info, *args)


def ffn_fwd_live(micro, info, hid, we, be, wr, br, gain, shift, *rest):
    act_out, slope_out, out_all, n_out, inv_out, sq_out, send_out, acc = rest[-8:]
    j = pl.program_id(0)
    rows = hid.shape[0]

    @pl.when(j == 0)
    def _():
        acc[...] = jnp.zeros(acc.shape, F32)

    inner = dot_nn(hid[...], we[...]) + be[...]
    active, slope = gelu_pair(inner)
    active = active.astype(BF)
    act_out[...] = active
    slope_out[...] = slope.astype(BF)
    acc[...] += dot_nn(active, wr[...])

    @pl.when(j == pl.num_programs(0) - 1)
    def _():
        b2 = acc[...] + br[...]
        n, inv = norm_rows(hid[...].astype(F32) + b2)
        out = (n * gain[...] + shift[...]).astype(BF)
        out_all[...] = out
        send_out[...] = out
        n_out[...] = n.astype(BF)
        inv_out[...] = inv
        mask = usable_rows(info, micro, rows)
        sq_out[0:1, :] = jnp.sum(mask * b2 * b2, axis=0, keepdims=True)


def ffn_forward(phase, micros, info, hidden, weights, old):
    (we, be, wr, br, gains, shifts) = weights
    section, micro = phase // micros, phase % micros
    slots, rows, width = hidden.shape
    ff = we.shape[1]
    steps = ff // FFBLOCK
    slot = lambda i: slot_of(i, section, micro, micros)
    at = lambda g, i: step_of(i, section, g)
    one = lambda *shape: pl.BlockSpec(shape, lambda g, i: (0,) * len(shape))
    in_specs = [
        pl.BlockSpec((None, rows, width), lambda g, i: (slot(i), 0, 0)),
        pl.BlockSpec((width, FFBLOCK), lambda g, i: (0, at(g, i))),
        pl.BlockSpec((1, FFBLOCK), lambda g, i: (0, at(g, i))),
        pl.BlockSpec((FFBLOCK, width), lambda g, i: (at(g, i), 0)),
        one(1, width),
        one(1, width),
        one(1, width),
    ]
    args = [hidden, we, be, wr, br, gains[1:2], shifts[1:2]]
    rows_at = lambda shape, kind: ((slots,) + shape, kind, (None,) + shape, lambda g, i: (slot(i), 0, 0))
    wide = ((slots, rows, ff), BF, (None, rows, FFBLOCK), lambda g, i: (slot(i), 0, at(g, i)))
    shapes = [
        wide,
        wide,
        rows_at((rows, width), BF),
        rows_at((rows, width), BF),
        rows_at((rows, 1), F32),
        rows_at((8, width), F32),
        ((rows, width), BF, (rows, width), lambda g, i: (0, 0)),
    ]
    return call(
        live_only(ffn_fwd_live, section, micro),
        steps, info, args, in_specs, shapes, old,
        [pltpu.VMEM((rows, width), F32)],
        flops=FLOPS_FFN,
    )


def column_sum(value):
    return jnp.sum(value, axis=0, keepdims=True)


def norm_rows_back(grad_out, n, inv, gain):
    grad_unit = grad_out * gain
    mean_grad = jnp.mean(grad_unit, axis=1, keepdims=True)
    mean_along = jnp.mean(grad_unit * n, axis=1, keepdims=True)
    return inv * (grad_unit - mean_grad - n * mean_along)


def loss_parts(info, micro, micros, grad_scale, out_b, wc):
    ends = ends_of(info, micro)
    embedded = dot_nn(out_b, wc)
    inv_norm = lax.rsqrt(jnp.sum(embedded * embedded, axis=1, keepdims=True) + UNIT_EPSILON)
    unit = embedded * inv_norm
    unit_b = unit.astype(BF)
    queries, passages = unit_b[:QROWS], unit_b[QROWS:]
    scaled = dot_nt(queries, passages) / SMOOTHING
    owner = passage_of(lax.broadcasted_iota(jnp.int32, (1, PSLOTS), 1), ends)
    top = jnp.max(jnp.where(owner < NP, scaled, NEG), axis=1, keepdims=True)
    terms = jnp.exp(scaled - top)
    lane = lax.broadcasted_iota(jnp.int32, (1, 128), 1)
    totals = jnp.ones((QROWS, 128), F32)
    lengths = jnp.ones((1, 128), F32)
    for j in range(NP):
        total = jnp.sum(jnp.where(owner == j, terms, 0.0), axis=1, keepdims=True)
        totals = jnp.where(lane == j, total, totals)
        lengths = jnp.where(lane == j, info[1 + micro * NP + j].astype(F32), lengths)
    smooth = SMOOTHING * (jnp.log(totals) + top - jnp.log(lengths))
    grouped = jnp.sum(smooth.reshape(NQ, QLEN, 128), axis=1, keepdims=True)
    scores = LOGIT_SCALE * grouped
    scores = jnp.where(lane[None] < NP, scores, NEG)
    score_max = jnp.max(scores, axis=2, keepdims=True)
    score_exp = jnp.exp(scores - score_max)
    score_total = jnp.sum(score_exp, axis=2, keepdims=True)
    query = lax.broadcasted_iota(jnp.int32, (NQ, 1, 128), 0)
    chosen = jnp.zeros((NQ, 1, 128), jnp.int32)
    for i in range(NQ):
        chosen = jnp.where(query == i, info[1 + micros * NP + micro * NQ + i], chosen)
    onehot = (chosen == lane[None]).astype(F32)
    own_score = jnp.sum(jnp.where(chosen == lane[None], scores, 0.0), axis=2, keepdims=True)
    losses = jnp.log(score_total) + score_max - own_score
    loss = jnp.sum(losses, axis=0)
    grad_scores = (score_exp / score_total - onehot) * grad_scale
    grad_smooth = jnp.broadcast_to(LOGIT_SCALE * grad_scores, (NQ, QLEN, 128)).reshape(QROWS, 128)
    share = grad_smooth / totals
    weight = jnp.zeros((QROWS, PSLOTS), F32)
    for j in range(NP):
        weight = jnp.where(owner == j, share[:, j : j + 1], weight)
    grad_similar = jnp.where(owner < NP, terms * weight, 0.0).astype(BF)
    grad_unit = jnp.concatenate([dot_nn(grad_similar, passages), dot_tn(grad_similar, queries)])
    grad_embed = inv_norm * (grad_unit - unit * jnp.sum(grad_unit * unit, axis=1, keepdims=True))
    return loss, grad_embed.astype(BF)


def ffn_bwd_live(with_loss, micros, grad_scale, micro, info, *refs):
    if with_loss:
        out_all, wc = refs[:2]
    else:
        rec = refs[0]
    n2, inv2, gain2, slope, wr, we, n1, inv1, gain1 = refs[2 if with_loss else 1 :][:9]
    two_out, inner_out, one_out, emb_out, small_out, ff_out, resid_out, acc, resid = refs[-9:]
    j = pl.program_id(0)

    @pl.when(j == 0)
    def _():
        small_out[...] = jnp.zeros(small_out.shape, F32)
        if with_loss:
            loss, grad_embed = loss_parts(info, micro, micros, grad_scale, out_all[...], wc[...])
            emb_out[...] = grad_embed
            upstream = dot_nt(grad_embed, wc[...])
            small_out[6:7, 0:128] = jnp.broadcast_to(loss, (1, 128))
        else:
            upstream = rec[...].astype(F32)
        acc[...] = jnp.zeros(acc.shape, F32)
        n = n2[...].astype(F32)
        small_out[0:1, :] = column_sum(upstream * n)
        small_out[1:2, :] = column_sum(upstream)
        d_two = norm_rows_back(upstream, n, inv2[...], gain2[...])
        resid[...] = d_two
        d_two_b = d_two.astype(BF)
        two_out[...] = d_two_b
        small_out[2:3, :] = column_sum(d_two_b.astype(F32))

    d_act = dot_nt(two_out[...], wr[...])
    d_inner = (d_act * slope[...].astype(F32)).astype(BF)
    inner_out[...] = d_inner
    ff_out[0:1, :] = column_sum(d_inner.astype(F32))
    acc[...] += dot_nt(d_inner, we[...])

    @pl.when(j == pl.num_programs(0) - 1)
    def _():
        upstream = resid[...] + acc[...]
        n = n1[...].astype(F32)
        small_out[3:4, :] = column_sum(upstream * n)
        small_out[4:5, :] = column_sum(upstream)
        d_one = norm_rows_back(upstream, n, inv1[...], gain1[...])
        resid_out[...] = d_one
        d_one_b = d_one.astype(BF)
        one_out[...] = d_one_b
        small_out[5:6, :] = column_sum(d_one_b.astype(F32))


def ffn_backward(phase, micros, grad_scale, info, received, kept, weights, old):
    (out_all, n2, inv2, slope, n1, inv1) = kept
    (wc, gains, wr, we) = weights
    section, micro = 1 - phase // micros, phase % micros
    slots, rows, width = out_all.shape
    ff = we.shape[1]
    steps = ff // FFBLOCK
    slot = lambda i: slot_of(i, section, micro, micros)
    at = lambda g, i: step_of(i, section, g)
    one = lambda *shape: pl.BlockSpec(shape, lambda g, i: (0,) * len(shape))
    at_slot = lambda *shape: pl.BlockSpec((None,) + shape, lambda g, i: (slot(i), 0, 0))
    if section == 1:
        in_specs = [at_slot(rows, width), one(*wc.shape)]
        args = [out_all, wc]
    else:
        in_specs = [one(rows, width)]
        args = [received]
    in_specs += [
        at_slot(rows, width),
        at_slot(rows, 1),
        one(1, width),
        pl.BlockSpec((None, rows, FFBLOCK), lambda g, i: (slot(i), 0, at(g, i))),
        pl.BlockSpec((FFBLOCK, width), lambda g, i: (at(g, i), 0)),
        pl.BlockSpec((width, FFBLOCK), lambda g, i: (0, at(g, i))),
        at_slot(rows, width),
        at_slot(rows, 1),
        one(1, width),
    ]
    args += [n2, inv2, gains[1:2], slope, wr, we, n1, inv1, gains[0:1]]
    rows_at = lambda shape, kind: ((slots,) + shape, kind, (None,) + shape, lambda g, i: (slot(i), 0, 0))
    shapes = [
        rows_at((rows, width), BF),
        ((slots, rows, ff), BF, (None, rows, FFBLOCK), lambda g, i: (slot(i), 0, at(g, i))),
        rows_at((rows, width), BF),
        rows_at((rows, wc.shape[1]), BF),
        rows_at((8, width), F32),
        ((slots, 8, ff), F32, (None, 8, FFBLOCK), lambda g, i: (slot(i), 0, at(g, i))),
        ((rows, width), F32, (rows, width), lambda g, i: (0, 0)),
    ]
    return call(
        live_only(functools.partial(ffn_bwd_live, section == 1, micros, grad_scale), section, micro),
        steps, info, args, in_specs, shapes, old,
        [pltpu.VMEM((rows, width), F32), pltpu.VMEM((rows, width), F32)],
        flops=FLOPS_FFN,
    )


def attn_bwd_live(with_send, micro, info, one_b, joined, lse, ctx, wm, *rest):
    qcode, kcode, dctx, delta, ktr, dqtr = rest[-6:]
    if with_send:
        resid, wq, wk, wv = rest[:4]
        dq_out, dk_out, dv_out, sum_out, send_out, acc = rest[-12:-6]
    else:
        dq_out, dk_out, dv_out, sum_out = rest[-10:-6]
    g = pl.program_id(0)

    @pl.when(g == 0)
    def _():
        fill_codes(info, micro, qcode, kcode)
        if with_send:
            acc[...] = jnp.zeros(acc.shape, F32)

    dctx32 = dot_nt(one_b[...], wm[...])
    dctx[...] = dctx32.astype(BF)
    along = dctx[...].astype(F32) * ctx[...].astype(F32)
    pick = lax.broadcasted_iota(jnp.int32, (8, SLAB), 0) == lax.broadcasted_iota(jnp.int32, (8, SLAB), 1) // HEAD_DIM
    delta[...] = lax.dot_general(
        pick.astype(F32), along, (((1,), (1,)), ((), ())),
        precision=lax.Precision.HIGHEST, preferred_element_type=F32,
    )
    ktr[...] = jnp.transpose(joined[:, SLAB : 2 * SLAB])
    rows = one_b.shape[0]
    parts = (slice(0, QROWS), slice(QROWS, rows))
    for pair in range(SLAB // 128):
        lo = pair * 128
        qs = joined[:, lo : lo + 128] * BF(HEAD_DIM**-0.5)
        ks = joined[:, SLAB + lo : SLAB + lo + 128]
        vs = joined[:, 2 * SLAB + lo : 2 * SLAB + lo + 128]
        do = dctx[:, lo : lo + 128]
        qms = [head_lanes(qs, h, jnp.zeros_like(qs)) for h in range(2)]
        dms = [head_lanes(do, h, jnp.zeros_like(do)) for h in range(2)]
        ps, dss = ([], []), ([], [])
        for h in range(2):
            head = pair * 2 + h
            hh = slice(head * HEAD_DIM, head * HEAD_DIM + HEAD_DIM)
            qh = head_lanes(qs, h, qcode[...])
            kh = head_lanes(ks, h, kcode[...])
            for i, at in enumerate(parts):
                p = jnp.exp(dot_nt(kh[at], qh[at]) - lse[head : head + 1, at])
                dp = dot_nt(vs[at], dms[h][at])
                ds = (p * (dp - delta[head : head + 1, at])).astype(BF)
                ps[i].append(p.astype(BF))
                dss[i].append(ds)
                dqtr[hh, at] = dot_nn(ktr[hh, at], ds)
        for i, at in enumerate(parts):
            q_heads = jnp.concatenate([qm[at] for qm in qms])
            d_heads = jnp.concatenate([dm[at] for dm in dms])
            dk_out[at, lo : lo + 128] = dot_nn(jnp.concatenate(dss[i], axis=1), q_heads).astype(BF)
            dv_out[at, lo : lo + 128] = dot_nn(jnp.concatenate(ps[i], axis=1), d_heads).astype(BF)
    dq = (jnp.transpose(dqtr[...]) * HEAD_DIM**-0.5).astype(BF)
    dq_out[...] = dq
    dk = dk_out[...]
    dv = dv_out[...]
    sum_out[0:1, 0:SLAB] = column_sum(dq.astype(F32))
    sum_out[0:1, SLAB : 2 * SLAB] = column_sum(dv.astype(F32))
    if not with_send:
        return
    acc[...] += dot_nt(
        jnp.concatenate([dq, dk, dv], axis=1), jnp.concatenate([wq[...], wk[...], wv[...]], axis=1)
    )

    @pl.when(g == pl.num_programs(0) - 1)
    def _():
        send_out[...] = (resid[...] + acc[...]).astype(BF)


def attn_backward(phase, micros, info, resid, one_all, kept, weights, old, slabs=None):
    (joined, lse, ctx) = kept
    (wa, wm) = weights
    section, micro = 1 - phase // micros, phase % micros
    slots, rows, width = one_all.shape
    count = width // SLAB
    slabs = slabs or range(count)
    with_send = section == 1
    slot = lambda i: slot_of(i, section, micro, micros)
    at = lambda g, i: step_of(i, section, slabs[0] + g)
    in_specs = [
        pl.BlockSpec((None, rows, width), lambda g, i: (slot(i), 0, 0)),
        pl.BlockSpec((None, None, rows, 3 * SLAB), lambda g, i: (slot(i), at(g, i), 0, 0)),
        pl.BlockSpec((None, None, 8, rows), lambda g, i: (slot(i), at(g, i), 0, 0)),
        pl.BlockSpec((None, rows, SLAB), lambda g, i: (slot(i), 0, at(g, i))),
        pl.BlockSpec((SLAB, width), lambda g, i: (at(g, i), 0)),
    ]
    args = [one_all, joined, lse, ctx, wm]
    slab = ((slots, rows, width), BF, (None, rows, SLAB), lambda g, i: (slot(i), 0, at(g, i)))
    shapes = [
        slab,
        slab,
        slab,
        ((slots, count, 8, 2 * SLAB), F32, (None, None, 8, 2 * SLAB), lambda g, i: (slot(i), at(g, i), 0, 0)),
    ]
    scratch = [
        pltpu.VMEM((rows, 128), BF),
        pltpu.VMEM((rows, 128), BF),
        pltpu.VMEM((rows, SLAB), BF),
        pltpu.VMEM((8, rows), F32),
        pltpu.VMEM((SLAB, rows), BF),
        pltpu.VMEM((SLAB, rows), F32),
    ]
    if with_send:
        in_specs += [
            pl.BlockSpec((rows, width), lambda g, i: (0, 0)),
            pl.BlockSpec((width, SLAB), lambda g, i: (0, at(g, i))),
            pl.BlockSpec((width, SLAB), lambda g, i: (0, count + at(g, i))),
            pl.BlockSpec((width, SLAB), lambda g, i: (0, 2 * count + at(g, i))),
        ]
        args += [resid, wa, wa, wa]
        shapes += [((rows, width), BF, (rows, width), lambda g, i: (0, 0))]
        scratch = [pltpu.VMEM((rows, width), F32)] + scratch
    return call(
        live_only(functools.partial(attn_bwd_live, with_send), section, micro),
        len(slabs), info, args, in_specs, shapes, old, scratch,
        flops=FLOPS_ATTN * len(slabs) // count,
    )


def mesh_bits():
    place = lax.axis_index("dp")
    bits = []
    bit = 1
    while bit < lax.axis_size("dp"):
        bits.append((bit, (place // bit) % 2))
        bit *= 2
    return bits


def grad_rows_body(info, left, right, first_out, second_out):
    step = pl.program_id(0)
    value = dot_nn(jnp.transpose(left[...]), right[...]).astype(BF)

    @pl.when(step < 2)
    def _():
        first_out[...] = value

    @pl.when(step >= 2)
    def _():
        second_out[...] = value


def grad_rows(tokens, half, left, right):
    tall, wide = left.shape[1], right.shape[1]
    block = tall // 8
    out = jax.ShapeDtypeStruct((tall // 4, wide), BF)
    return pl.pallas_call(
        grad_rows_body,
        out_shape=[out, out],
        grid_spec=pltpu.PrefetchScalarGridSpec(
            num_scalar_prefetch=1,
            grid=(4,),
            in_specs=[
                pl.BlockSpec((tokens, block), lambda s, h: (0, h[0] * 4 + s)),
                pl.BlockSpec((tokens, wide), lambda s, h: (0, 0)),
            ],
            out_specs=[
                pl.BlockSpec((block, wide), lambda s, h: (jnp.minimum(s, 1), 0)),
                pl.BlockSpec((block, wide), lambda s, h: (jnp.maximum(s - 2, 0), 0)),
            ],
        ),
        compiler_params=pltpu.CompilerParams(vmem_limit_bytes=VMEM_LIMIT),
        cost_estimate=pl.CostEstimate(flops=tokens * tall * wide, bytes_accessed=8_000_000, transcendentals=0),
    )(half, left, right)


def grad_columns_body(info, left, right, first_out, second_out, turned):
    step = pl.program_id(0)

    @pl.when(step == 0)
    def _():
        turned[...] = jnp.transpose(left[...])

    value = dot_nn(turned[...], right[...]).astype(BF)

    @pl.when(step < 2)
    def _():
        first_out[...] = value

    @pl.when(step >= 2)
    def _():
        second_out[...] = value


def grad_columns(tokens, half, left, right):
    tall, wide = left.shape[1], right.shape[1]
    block = wide // 4
    out = jax.ShapeDtypeStruct((tall // 2, wide // 2), BF)
    return pl.pallas_call(
        grad_columns_body,
        out_shape=[out, out],
        grid_spec=pltpu.PrefetchScalarGridSpec(
            num_scalar_prefetch=1,
            grid=(4,),
            in_specs=[
                pl.BlockSpec((tokens, tall // 2), lambda s, h: (0, h[0])),
                pl.BlockSpec((tokens, block), lambda s, h: (0, s)),
            ],
            out_specs=[
                pl.BlockSpec((tall // 2, block), lambda s, h: (0, jnp.minimum(s, 1))),
                pl.BlockSpec((tall // 2, block), lambda s, h: (0, jnp.maximum(s - 2, 0))),
            ],
            scratch_shapes=[pltpu.VMEM((tall // 2, tokens), BF)],
        ),
        compiler_params=pltpu.CompilerParams(vmem_limit_bytes=VMEM_LIMIT),
        cost_estimate=pl.CostEstimate(flops=tokens * tall * wide, bytes_accessed=8_000_000, transcendentals=0),
    )(half, left, right)


def grad_rest_body(with_context, info, inputs, *refs):
    step = pl.program_id(0)
    sent, kept = refs[-2:]
    turned = jnp.transpose(inputs[...])
    parts = []
    if with_context:
        context, d_one = refs[:2]
        parts.append(dot_nn(jnp.transpose(context[...]), d_one[...]).astype(BF))
        refs = refs[2:]
    parts += [dot_nn(turned, right[...]).astype(BF) for right in refs[:-2]]
    for s, out in enumerate((sent, kept)):

        @pl.when(step == s)
        def _(out=out):
            at = 0
            for part in parts:
                out[:, at : at + part.shape[1]] = part
                at += part.shape[1]


def grad_rest(tokens, core, inputs, joined_grads, slabs, context=None, d_one=None):
    width = inputs.shape[1]
    side = pl.BlockSpec((tokens, width // 2), lambda s, h: (0, jnp.where(s == 0, 1 - h[0], h[0])))
    in_specs, args = [side], [inputs]
    columns = 0
    if context is not None:
        in_specs += [side, pl.BlockSpec((tokens, width), lambda s, h: (0, 0))]
        args += [context, d_one]
        columns += width
    for slab in slabs:
        in_specs += [pl.BlockSpec((tokens, SLAB), lambda s, h, slab=slab: (0, slab))] * 3
        args += joined_grads
        columns += 3 * SLAB
    out = jax.ShapeDtypeStruct((width // 2, columns), BF)
    whole = pl.BlockSpec(out.shape, lambda s, h: (0, 0))
    return pl.pallas_call(
        functools.partial(grad_rest_body, context is not None),
        out_shape=[out, out],
        grid_spec=pltpu.PrefetchScalarGridSpec(
            num_scalar_prefetch=1,
            grid=(2,),
            in_specs=in_specs,
            out_specs=[whole, whole],
        ),
        compiler_params=pltpu.CompilerParams(vmem_limit_bytes=VMEM_LIMIT),
        cost_estimate=pl.CostEstimate(flops=2 * tokens * columns * width, bytes_accessed=12_000_000, transcendentals=0),
    )(core, *args)


def widen_body(info, own_a, own_b, other_a, other_b, *outs):
    step = pl.program_id(0)
    for s, (a, b) in enumerate(((own_a, own_b), (other_a, other_b))):

        @pl.when(step == s)
        def _(a=a, b=b):
            parts = (a[...].astype(F32), b[...].astype(F32))
            if len(outs) == 2:
                width = outs[1].shape[1]
                outs[1][...] = parts[0][:, :width]
                slabs = [parts[0][:, width:]] + [
                    parts[1][:, at : at + 3 * SLAB] for at in range(0, parts[1].shape[1], 3 * SLAB)
                ]
                for g, slab in enumerate(slabs):
                    for kind in range(3):
                        at = kind * width + g * SLAB
                        outs[0][:, at : at + SLAB] = slab[:, kind * SLAB : kind * SLAB + SLAB]
            elif outs[0].shape[1] == parts[0].shape[1]:
                outs[0][: parts[0].shape[0]] = parts[0]
                outs[0][parts[0].shape[0] :] = parts[1]
            else:
                outs[0][:, : parts[0].shape[1]] = parts[0]
                outs[0][:, parts[0].shape[1] :] = parts[1]


def widened(core, own, other, out_shapes):
    small = own[0].shape
    piece_spec = pl.BlockSpec(small, lambda s, h: (0, 0))
    return pl.pallas_call(
        widen_body,
        out_shape=[jax.ShapeDtypeStruct(shape, F32) for shape in out_shapes],
        grid_spec=pltpu.PrefetchScalarGridSpec(
            num_scalar_prefetch=1,
            grid=(2,),
            in_specs=[piece_spec] * 4,
            out_specs=[
                pl.BlockSpec((shape[0] // 2, shape[1]), lambda s, h: (jnp.where(s == 0, h[0], 1 - h[0]), 0))
                for shape in out_shapes
            ],
        ),
        compiler_params=pltpu.CompilerParams(vmem_limit_bytes=VMEM_LIMIT),
        cost_estimate=pl.CostEstimate(flops=0, bytes_accessed=14_000_000, transcendentals=0),
    )(core, *own, *other)


def passed_along(array, axis, by):
    count = lax.axis_size(axis)
    pairs = [(i, i + by) for i in range(count) if 0 <= i + by < count]
    return lax.ppermute(array, axis, pairs)


def tied(array, *others):
    return lax.optimization_barrier((array, *others))[0]


def flatten_rows(leaf):
    return leaf.reshape(-1, leaf.shape[-1])


def swapped(array, bit, axis="dp"):
    count = lax.axis_size(axis)
    return lax.ppermute(array, axis, [(i, i ^ bit) for i in range(count)])


def piece(array, index):
    return lax.dynamic_index_in_dim(array, index, 0, keepdims=False)


def sum_low(kept, got):
    return (kept.astype(F32) + got.astype(F32)).astype(BF)


def halved(array, bit):
    step, mine = bit
    halves = array.reshape(2, array.shape[0] // 2, array.shape[1])
    got = swapped(piece(halves, 1 - mine), step)
    return sum_low(piece(halves, mine), got)


def doubled(array, bit):
    step, mine = bit
    got = swapped(array, step)
    both = jnp.zeros((2,) + array.shape, array.dtype)
    both = lax.dynamic_update_index_in_dim(both, array, mine, 0)
    both = lax.dynamic_update_index_in_dim(both, got, 1 - mine, 0)
    return flatten_rows(both)


class Piece:
    def __init__(self, sent, kept, bits, order):
        self.value = sum_low(kept, swapped(sent, 1))
        self.steps = [(halved, bits[place]) for place in order]
        self.steps += [(doubled, bits[place]) for place in reversed(order)]

    def advance(self):
        step, bit = self.steps.pop(0)
        self.value = step(self.value, bit)

    def finish(self):
        while self.steps:
            self.advance()
        return self.value, swapped(self.value, 1)


def advanced(*pieces):
    for one in pieces:
        one.advance()
    return tuple(one.value for one in pieces)


def all_summed(array, bits):
    for step, _ in bits:
        array = (array.astype(F32) + swapped(array, step).astype(F32)).astype(array.dtype)
    return array


def shards(
    hidden_in,
    attend_weight,
    attend_bias,
    mixing_weight,
    mixing_bias,
    norm_gain,
    norm_shift,
    expand_weight,
    expand_bias,
    reduce_weight,
    reduce_bias,
    colbert_weight,
    pass_lengths,
    positives,
):
    section_id = lax.axis_index("pipe")
    data_count = lax.axis_size("dp")
    micros = pass_lengths.shape[0]
    rows = hidden_in.shape[0] // micros
    width = hidden_in.shape[1]
    grad_scale = 1.0 / (data_count * micros * NQ)
    wa, wm, we, wr = attend_weight[0], mixing_weight[0], expand_weight[0], reduce_weight[0]
    gains, shifts = norm_gain[0], norm_shift[0]
    info = jnp.concatenate(
        [section_id.astype(jnp.int32)[None], pass_lengths.reshape(-1), positives.reshape(-1)]
    )
    bits = mesh_bits()
    core = bits[0][1].astype(jnp.int32)[None]
    along_x_first = list(range(1, len(bits)))
    along_z_first = [2, 1] + list(range(3, len(bits)))
    orders = (along_x_first, along_z_first)
    attn_weights = (wa, attend_bias, wm, mixing_bias, gains, shifts)
    ffn_weights = (we, expand_bias, wr, reduce_bias, gains, shifts)
    state = {"attn": None, "ffn": None, "attn_back": None, "ffn_back": None}
    arriving, returning = {}, {}

    def forward(phase, after=()):
        source = hidden_in if phase < micros else arriving[phase - micros]
        source = tied(source, *after)
        attn = attn_forward(phase, micros, info, source, attn_weights, state["attn"])
        old = state["ffn"]
        ffn = ffn_forward(phase, micros, info, attn[4], ffn_weights, old and old[:6])
        state["attn"], state["ffn"] = attn, ffn
        if phase < micros:
            arriving[phase] = passed_along(ffn[6], "pipe", 1)

    def backward_ffn(phase, after=()):
        attn, ffn, old = state["attn"], state["ffn"], state["ffn_back"]
        received = None if phase < micros else tied(returning[phase - micros], *after)
        state["ffn_back"] = ffn_backward(
            phase, micros, grad_scale, info, received,
            (ffn[2], ffn[3], ffn[4], ffn[1], attn[5], attn[6]),
            (colbert_weight, gains, wr, we), old and old[:6],
        )

    def backward_attn(phase, after=(), slabs=None):
        attn, old, ffn_back = state["attn"], state["attn_back"], state["ffn_back"]
        attn_back = attn_backward(
            phase, micros, tied(info, *after), ffn_back[6], ffn_back[2], (attn[1], attn[2], attn[3]), (wa, wm),
            old and old[:4], slabs,
        )
        state["attn_back"] = attn_back
        if phase < micros:
            returning[phase] = passed_along(attn_back[4], "pipe", -1)

    for phase in range(micros):
        forward(phase)
    done = ()
    for phase in range(micros):
        forward(micros + phase, done)
        backward_ffn(phase)
        backward_attn(phase)
        done = (state["attn_back"][3],)
    for phase in range(micros, 2 * micros - 1):
        backward_ffn(phase, done)
        backward_attn(phase)
        done = (state["attn_back"][3],)
    inputs, joined, lse, context, hidden, unit_one, inv_one, squares_one = state["attn"]
    active, slope, outputs, unit_two, inv_two, squares_two, _ = state["ffn"]
    embeds, losses = state["ffn_back"][3], state["ffn_back"][4]
    squares = jnp.stack(
        [
            jnp.sum(squares_one[:micros, 0], axis=1),
            jnp.sum(squares_one[:micros, 1], axis=1),
            jnp.sum(squares_two[:micros, 0], axis=1),
        ],
        axis=1,
    )
    colbert = dot_tn(flatten_rows(outputs[:micros]), flatten_rows(embeds[:micros])).astype(BF)
    facts = jnp.concatenate([squares, losses[:micros, 6, 0:1]], axis=1)
    backward_ffn(2 * micros - 1, done + (colbert, facts))
    colbert = jnp.where(section_id == 1, colbert, swapped(colbert, 1, "pipe"))
    colbert_sum = all_summed(colbert, bits).astype(F32)
    theirs = swapped(facts, 1, "pipe")
    first = jnp.where(section_id == 0, facts, theirs)
    second = jnp.where(section_id == 0, theirs, facts)
    ffn_back = state["ffn_back"]
    tokens = micros * rows
    last = 2 * micros - 1
    d_two, d_inner = flatten_rows(ffn_back[0]), flatten_rows(ffn_back[1])
    left = flatten_rows(active)
    sent, kept = (grad_rows(tokens, half, left, d_two) for half in (1 - core, core))
    pieces = [Piece(s, k, bits, order) for s, k, order in zip(sent, kept, orders)]
    of_reduce = tuple(one.value for one in pieces)
    left = flatten_rows(hidden)
    sent = grad_columns(tokens, 1 - core, left, d_inner)
    kept = grad_columns(tokens, tied(core, *of_reduce), left, d_inner)
    pieces += [Piece(s, k, bits, order) for s, k, order in zip(sent, kept, orders)]
    of_expand = tuple(one.value for one in pieces[2:])
    backward_attn(last, of_expand, (0,))
    x_rows, context_rows, one_rows = (flatten_rows(a) for a in (inputs, context, ffn_back[2]))
    joined_grads = [flatten_rows(a) for a in state["attn_back"][:3]]
    after = advanced(*pieces[:2])
    sent, kept = grad_rest(tokens, tied(core, *after), x_rows, joined_grads, (0,), context_rows, one_rows)
    after = advanced(*pieces[:4])
    backward_attn(last, after + (kept,), tuple(range(1, width // SLAB)))
    pieces += [Piece(sent, kept, bits, orders[0])]
    after = advanced(*pieces[:4])
    joined_grads = [flatten_rows(a) for a in state["attn_back"][:3]]
    sent, kept = grad_rest(tokens, tied(core, *after), x_rows, joined_grads, tuple(range(1, width // SLAB)))
    pieces += [Piece(sent, kept, bits, orders[1])]
    attn_back = state["attn_back"]
    small, small_ff = ffn_back[4], ffn_back[5]
    joined_sums = attn_back[3]
    small_sum = jnp.sum(small[:micros], axis=0)
    joined_sum = jnp.sum(joined_sums[:micros, :, 0], axis=0)
    attend_sum = jnp.concatenate(
        [joined_sum[:, :SLAB].reshape(-1), joined_sum[:, SLAB:].reshape(-1)]
    )
    vector = jnp.concatenate(
        [small_sum[:6], attend_sum.reshape(2, width), jnp.sum(small_ff[:micros, 0], axis=0).reshape(-1, width)]
    )
    vector = all_summed(vector, bits)
    halves = [one.finish() for one in pieces]
    own, other = [h[0] for h in halves], [h[1] for h in halves]
    [big_reduce] = widened(core, own[:2], other[:2], [wr.shape])
    [big_expand] = widened(core, own[2:4], other[2:4], [we.shape])
    big_attend, big_mixing = widened(core, own[4:], other[4:], [wa.shape, wm.shape])
    counted = (QROWS + jnp.sum(pass_lengths, axis=1)).astype(F32)
    stats = jnp.stack([first[:, :3], second[:, :3]], axis=1)
    stats = jnp.sqrt(stats / (counted[:, None, None] * width))
    return (
        big_attend[None],
        vector[6:8].reshape(1, -1),
        big_mixing[None],
        vector[5][None],
        jnp.stack([vector[3], vector[0]])[None],
        jnp.stack([vector[4], vector[1]])[None],
        big_expand[None],
        vector[8:].reshape(1, -1),
        big_reduce[None],
        vector[2][None],
        colbert_sum,
        second[:, 3] / NQ,
        stats,
    )


def solution(mesh):
    placed = (
        P("dp", None),
        P("pipe", None, None),
        P("pipe", None),
        P("pipe", None, None),
        P("pipe", None),
        P("pipe", None, None),
        P("pipe", None, None),
        P("pipe", None, None),
        P("pipe", None),
        P("pipe", None, None),
        P("pipe", None),
        P(),
        P("dp", None),
        P("dp", None),
    )
    return jax.shard_map(
        shards,
        mesh=mesh,
        in_specs=placed,
        out_specs=(
            P("pipe", None, None),
            P("pipe", None),
            P("pipe", None, None),
            P("pipe", None),
            P("pipe", None, None),
            P("pipe", None, None),
            P("pipe", None, None),
            P("pipe", None),
            P("pipe", None, None),
            P("pipe", None),
            P(),
            P("dp"),
            P("dp", None, None),
        ),
        check_vma=False,
    )
```

```python
import functools
import jax
import jax.numpy as jnp
from jax import lax
from jax.experimental import pallas as pl
from jax.experimental.pallas import tpu as pltpu
from jax.sharding import PartitionSpec as P

HEAD_DIM = 64
QLEN = 32
NQ = 4
NP = 4
PSLOTS = 512
LAYER_EPSILON = 1e-12
UNIT_EPSILON = 1e-06
SMOOTHING = 0.05
LOGIT_SCALE = 4.0
ROOT_HALF = 0.7071067811865476
NORMAL_PEAK = 0.3989422804014327
BF = jnp.bfloat16
F32 = jnp.float32
QROWS = NQ * QLEN
SLAB = 256
FFBLOCK = 768
VMEM_LIMIT = 56 * 1024 * 1024
NEG = -1e30
GRAD_STEPS = 2
SMALL_VMEM = 26 * 1024 * 1024
FLOPS_FFN = 12_000_000_000
FLOPS_ATTN = 20_000_000_000


def dot_nn(a, b):
    return jnp.dot(a, b, preferred_element_type=F32)


def dot_nt(a, b):
    return lax.dot_general(a, b, (((1,), (1,)), ((), ())), preferred_element_type=F32)


def dot_tn(a, b):
    return lax.dot_general(a, b, (((0,), (0,)), ((), ())), preferred_element_type=F32)


def gelu_pair(u):
    phi = 0.5 + 0.5 * lax.erf(u * ROOT_HALF)
    return u * phi, phi + NORMAL_PEAK * u * jnp.exp(-0.5 * u * u)


def norm_rows(resid):
    centre = resid - jnp.mean(resid, axis=1, keepdims=True)
    inv = lax.rsqrt(jnp.mean(centre * centre, axis=1, keepdims=True) + LAYER_EPSILON)
    return centre * inv, inv


def ends_of(info, micro):
    base = 1 + micro * NP
    ends = []
    total = jnp.int32(0)
    for j in range(NP):
        total = total + info[base + j]
        ends.append(total)
    return ends


def passage_of(place, ends):
    out = jnp.zeros(place.shape, jnp.int32)
    for end in ends:
        out = out + jnp.where(place >= end, 1, 0)
    return out


def when_live(info, section, body):
    pl.when(info[0] == section)(body)


def slot_of(info, section, micro, spare):
    return jnp.where(info[0] == section, micro, spare)


def step_of(info, section, step):
    return jnp.where(info[0] == section, step, 0)


def fill_codes(info, micro, query_code, key_code):
    rows = query_code.shape[0]
    ends = [QROWS + end for end in ends_of(info, micro)]
    place = lax.broadcasted_iota(jnp.int32, (rows, 1), 0)
    segment = jnp.where(place < QROWS, place // QLEN, NQ + passage_of(place, ends))
    lane = lax.broadcasted_iota(jnp.int32, (1, 128), 1) % HEAD_DIM
    query_code[...] = jnp.where(segment == lane, 1.0, 0.0).astype(BF)
    key_code[...] = jnp.where((segment == lane) | (lane > NQ + NP), 0.0, NEG).astype(BF)


def usable_rows(info, micro, rows):
    ends = ends_of(info, micro)
    place = lax.broadcasted_iota(jnp.int32, (rows, 1), 0)
    return (place < QROWS + ends[-1]).astype(F32)


def head_lanes(value, h, others):
    lane = lax.broadcasted_iota(jnp.int32, (1, 128), 1) // HEAD_DIM
    return jnp.where(lane == h, value, others)


def live_only(body, section, micro):
    def kernel(info, *refs):
        when_live(info, section, lambda: body(micro, info, *refs))

    return kernel


def attn_fwd_live(micro, info, hid, wq, wk, wv, bq, bv, wm, bm, gain, shift, *rest):
    x_out, joined_out, lse_out, ctx_out, hid_out, n_out, inv_out, sq_out, acc, qcode, kcode, otr, vtr = rest[-13:]
    g = pl.program_id(0)
    rows = hid.shape[0]

    @pl.when(g == 0)
    def _():
        x_out[...] = hid[...]
        fill_codes(info, micro, qcode, kcode)
        acc[...] = jnp.zeros(acc.shape, F32)

    x = hid[...]
    qkv = dot_nn(x, jnp.concatenate([wq[...], wk[...], wv[...]], axis=1))
    q = (qkv[:, :SLAB] + bq[...]).astype(BF)
    joined_out[:, 0:SLAB] = q
    k = qkv[:, SLAB : 2 * SLAB].astype(BF)
    joined_out[:, SLAB : 2 * SLAB] = k
    v = (qkv[:, 2 * SLAB :] + bv[...]).astype(BF)
    joined_out[:, 2 * SLAB : 3 * SLAB] = v
    vtr[...] = jnp.transpose(v)
    parts = (slice(0, QROWS), slice(QROWS, rows))
    for pair in range(SLAB // 128):
        cols = slice(pair * 128, pair * 128 + 128)
        qs = joined_out[:, cols] * BF(HEAD_DIM**-0.5)
        ks = joined_out[:, SLAB + pair * 128 : SLAB + pair * 128 + 128]
        for h in range(2):
            head = pair * 2 + h
            vh = slice(head * HEAD_DIM, head * HEAD_DIM + HEAD_DIM)
            qh = head_lanes(qs, h, qcode[...])
            kh = head_lanes(ks, h, kcode[...])
            for at in parts:
                st = dot_nt(kh[at], qh[at])
                top = jnp.max(st, axis=0, keepdims=True)
                p = jnp.exp(st - top)
                total = jnp.sum(p, axis=0, keepdims=True)
                lse_out[head : head + 1, at] = top + jnp.log(total)
                otr[vh, at] = dot_nn(vtr[vh, at], p.astype(BF)) * (1.0 / total)
    ctx = jnp.transpose(otr[...]).astype(BF)
    ctx_out[...] = ctx
    acc[...] += dot_nn(ctx, wm[...])

    @pl.when(g == pl.num_programs(0) - 1)
    def _():
        b1 = acc[...] + bm[...]
        x32 = hid[...].astype(F32)
        n, inv = norm_rows(x32 + b1)
        hid_out[...] = (n * gain[...] + shift[...]).astype(BF)
        n_out[...] = n.astype(BF)
        inv_out[...] = inv
        mask = usable_rows(info, micro, rows)
        sq_out[0:1, :] = jnp.sum(mask * x32 * x32, axis=0, keepdims=True)
        sq_out[1:2, :] = jnp.sum(mask * b1 * b1, axis=0, keepdims=True)


def attn_forward(phase, micros, info, source, weights, old):
    (wa, ba, wm, bm, gains, shifts) = weights
    section, micro = phase // micros, phase % micros
    width = source.shape[1]
    rows = source.shape[0] // micros if section == 0 else source.shape[0]
    place = micro if section == 0 else 0
    steps = width // SLAB
    slot = lambda i: slot_of(i, section, micro, micros)
    at = lambda g, i: step_of(i, section, g)
    one = lambda *shape: pl.BlockSpec(shape, lambda g, i: (0,) * len(shape))
    in_specs = [
        pl.BlockSpec((rows, width), lambda g, i: (place, 0)),
        pl.BlockSpec((width, SLAB), lambda g, i: (0, at(g, i))),
        pl.BlockSpec((width, SLAB), lambda g, i: (0, steps + at(g, i))),
        pl.BlockSpec((width, SLAB), lambda g, i: (0, 2 * steps + at(g, i))),
        pl.BlockSpec((1, SLAB), lambda g, i: (0, at(g, i))),
        pl.BlockSpec((1, SLAB), lambda g, i: (0, steps + at(g, i))),
        pl.BlockSpec((SLAB, width), lambda g, i: (at(g, i), 0)),
        one(1, width),
        one(1, width),
        one(1, width),
    ]
    args = [source, wa, wa, wa, ba, ba, wm, bm, gains[0:1], shifts[0:1]]
    slots = micros + 1
    rows_at = lambda shape, kind: ((slots,) + shape, kind, (None,) + shape, lambda g, i: (slot(i), 0, 0))
    shapes = [
        rows_at((rows, width), BF),
        ((slots, steps, rows, 3 * SLAB), BF, (None, None, rows, 3 * SLAB), lambda g, i: (slot(i), at(g, i), 0, 0)),
        ((slots, steps, 8, rows), F32, (None, None, 8, rows), lambda g, i: (slot(i), at(g, i), 0, 0)),
        ((slots, rows, width), BF, (None, rows, SLAB), lambda g, i: (slot(i), 0, at(g, i))),
        rows_at((rows, width), BF),
        rows_at((rows, width), BF),
        rows_at((rows, 1), F32),
        rows_at((8, width), F32),
    ]
    return call(
        live_only(attn_fwd_live, section, micro),
        steps, info, args, in_specs, shapes, old,
        [
            pltpu.VMEM((rows, width), F32),
            pltpu.VMEM((rows, 128), BF),
            pltpu.VMEM((rows, 128), BF),
            pltpu.VMEM((SLAB, rows), F32),
            pltpu.VMEM((SLAB, rows), BF),
        ],
        flops=FLOPS_ATTN,
    )


def call(body, steps, info, args, in_specs, shapes, old, scratch, flops, limit=VMEM_LIMIT):
    aliases = {}
    if old is not None:
        in_specs = in_specs + [pl.BlockSpec(memory_space=pl.ANY)] * len(old)
        aliases = {1 + len(args) + i: i for i in range(len(old))}
        args = args + list(old)
    return pl.pallas_call(
        body,
        out_shape=[jax.ShapeDtypeStruct(s[0], s[1]) for s in shapes],
        grid_spec=pltpu.PrefetchScalarGridSpec(
            num_scalar_prefetch=1,
            grid=(steps,),
            in_specs=in_specs,
            out_specs=[pl.BlockSpec(s[2], s[3]) for s in shapes],
            scratch_shapes=scratch,
        ),
        input_output_aliases=aliases,
        compiler_params=pltpu.CompilerParams(
            dimension_semantics=("arbitrary",), vmem_limit_bytes=limit
        ),
        cost_estimate=pl.CostEstimate(flops=flops, bytes_accessed=min(20_000_000, flops // 600), transcendentals=0),
    )(info, *args)


def ffn_fwd_live(micro, info, hid, we, be, wr, br, gain, shift, *rest):
    act_out, slope_out, out_all, n_out, inv_out, sq_out, send_out, acc = rest[-8:]
    j = pl.program_id(0)
    rows = hid.shape[0]

    @pl.when(j == 0)
    def _():
        acc[...] = jnp.zeros(acc.shape, F32)

    inner = dot_nn(hid[...], we[...]) + be[...]
    active, slope = gelu_pair(inner)
    active = active.astype(BF)
    act_out[...] = active
    slope_out[...] = slope.astype(BF)
    acc[...] += dot_nn(active, wr[...])

    @pl.when(j == pl.num_programs(0) - 1)
    def _():
        b2 = acc[...] + br[...]
        n, inv = norm_rows(hid[...].astype(F32) + b2)
        out = (n * gain[...] + shift[...]).astype(BF)
        out_all[...] = out
        send_out[...] = out
        n_out[...] = n.astype(BF)
        inv_out[...] = inv
        mask = usable_rows(info, micro, rows)
        sq_out[0:1, :] = jnp.sum(mask * b2 * b2, axis=0, keepdims=True)


def ffn_forward(phase, micros, info, hidden, weights, old):
    (we, be, wr, br, gains, shifts) = weights
    section, micro = phase // micros, phase % micros
    slots, rows, width = hidden.shape
    ff = we.shape[1]
    steps = ff // FFBLOCK
    slot = lambda i: slot_of(i, section, micro, micros)
    at = lambda g, i: step_of(i, section, g)
    one = lambda *shape: pl.BlockSpec(shape, lambda g, i: (0,) * len(shape))
    in_specs = [
        pl.BlockSpec((None, rows, width), lambda g, i: (slot(i), 0, 0)),
        pl.BlockSpec((width, FFBLOCK), lambda g, i: (0, at(g, i))),
        pl.BlockSpec((1, FFBLOCK), lambda g, i: (0, at(g, i))),
        pl.BlockSpec((FFBLOCK, width), lambda g, i: (at(g, i), 0)),
        one(1, width),
        one(1, width),
        one(1, width),
    ]
    args = [hidden, we, be, wr, br, gains[1:2], shifts[1:2]]
    rows_at = lambda shape, kind: ((slots,) + shape, kind, (None,) + shape, lambda g, i: (slot(i), 0, 0))
    wide = ((slots, rows, ff), BF, (None, rows, FFBLOCK), lambda g, i: (slot(i), 0, at(g, i)))
    shapes = [
        wide,
        wide,
        rows_at((rows, width), BF),
        rows_at((rows, width), BF),
        rows_at((rows, 1), F32),
        rows_at((8, width), F32),
        ((rows, width), BF, (rows, width), lambda g, i: (0, 0)),
    ]
    return call(
        live_only(ffn_fwd_live, section, micro),
        steps, info, args, in_specs, shapes, old,
        [pltpu.VMEM((rows, width), F32)],
        flops=FLOPS_FFN,
    )


def column_sum(value):
    return jnp.sum(value, axis=0, keepdims=True)


def norm_rows_back(grad_out, n, inv, gain):
    grad_unit = grad_out * gain
    mean_grad = jnp.mean(grad_unit, axis=1, keepdims=True)
    mean_along = jnp.mean(grad_unit * n, axis=1, keepdims=True)
    return inv * (grad_unit - mean_grad - n * mean_along)


def loss_parts(info, micro, micros, grad_scale, out_b, wc):
    ends = ends_of(info, micro)
    embedded = dot_nn(out_b, wc)
    inv_norm = lax.rsqrt(jnp.sum(embedded * embedded, axis=1, keepdims=True) + UNIT_EPSILON)
    unit = embedded * inv_norm
    unit_b = unit.astype(BF)
    queries, passages = unit_b[:QROWS], unit_b[QROWS:]
    scaled = dot_nt(queries, passages) / SMOOTHING
    owner = passage_of(lax.broadcasted_iota(jnp.int32, (1, PSLOTS), 1), ends)
    top = jnp.max(jnp.where(owner < NP, scaled, NEG), axis=1, keepdims=True)
    terms = jnp.exp(scaled - top)
    lane = lax.broadcasted_iota(jnp.int32, (1, 128), 1)
    totals = jnp.ones((QROWS, 128), F32)
    lengths = jnp.ones((1, 128), F32)
    for j in range(NP):
        total = jnp.sum(jnp.where(owner == j, terms, 0.0), axis=1, keepdims=True)
        totals = jnp.where(lane == j, total, totals)
        lengths = jnp.where(lane == j, info[1 + micro * NP + j].astype(F32), lengths)
    smooth = SMOOTHING * (jnp.log(totals) + top - jnp.log(lengths))
    grouped = jnp.sum(smooth.reshape(NQ, QLEN, 128), axis=1, keepdims=True)
    scores = LOGIT_SCALE * grouped
    scores = jnp.where(lane[None] < NP, scores, NEG)
    score_max = jnp.max(scores, axis=2, keepdims=True)
    score_exp = jnp.exp(scores - score_max)
    score_total = jnp.sum(score_exp, axis=2, keepdims=True)
    query = lax.broadcasted_iota(jnp.int32, (NQ, 1, 128), 0)
    chosen = jnp.zeros((NQ, 1, 128), jnp.int32)
    for i in range(NQ):
        chosen = jnp.where(query == i, info[1 + micros * NP + micro * NQ + i], chosen)
    onehot = (chosen == lane[None]).astype(F32)
    own_score = jnp.sum(jnp.where(chosen == lane[None], scores, 0.0), axis=2, keepdims=True)
    losses = jnp.log(score_total) + score_max - own_score
    loss = jnp.sum(losses, axis=0)
    grad_scores = (score_exp / score_total - onehot) * grad_scale
    grad_smooth = jnp.broadcast_to(LOGIT_SCALE * grad_scores, (NQ, QLEN, 128)).reshape(QROWS, 128)
    share = grad_smooth / totals
    weight = jnp.zeros((QROWS, PSLOTS), F32)
    for j in range(NP):
        weight = jnp.where(owner == j, share[:, j : j + 1], weight)
    grad_similar = jnp.where(owner < NP, terms * weight, 0.0).astype(BF)
    grad_unit = jnp.concatenate([dot_nn(grad_similar, passages), dot_tn(grad_similar, queries)])
    grad_embed = inv_norm * (grad_unit - unit * jnp.sum(grad_unit * unit, axis=1, keepdims=True))
    return loss, grad_embed.astype(BF)


def ffn_bwd_live(with_loss, micros, grad_scale, micro, info, *refs):
    if with_loss:
        out_all, wc = refs[:2]
    else:
        rec = refs[0]
    n2, inv2, gain2, slope, wr, we, n1, inv1, gain1 = refs[2 if with_loss else 1 :][:9]
    two_out, inner_out, one_out, emb_out, small_out, ff_out, resid_out, acc, resid = refs[-9:]
    j = pl.program_id(0)

    @pl.when(j == 0)
    def _():
        small_out[...] = jnp.zeros(small_out.shape, F32)
        if with_loss:
            loss, grad_embed = loss_parts(info, micro, micros, grad_scale, out_all[...], wc[...])
            emb_out[...] = grad_embed
            upstream = dot_nt(grad_embed, wc[...])
            small_out[6:7, 0:128] = jnp.broadcast_to(loss, (1, 128))
        else:
            upstream = rec[...].astype(F32)
        acc[...] = jnp.zeros(acc.shape, F32)
        n = n2[...].astype(F32)
        small_out[0:1, :] = column_sum(upstream * n)
        small_out[1:2, :] = column_sum(upstream)
        d_two = norm_rows_back(upstream, n, inv2[...], gain2[...])
        resid[...] = d_two
        d_two_b = d_two.astype(BF)
        two_out[...] = d_two_b
        small_out[2:3, :] = column_sum(d_two_b.astype(F32))

    d_act = dot_nt(two_out[...], wr[...])
    d_inner = (d_act * slope[...].astype(F32)).astype(BF)
    inner_out[...] = d_inner
    ff_out[0:1, :] = column_sum(d_inner.astype(F32))
    acc[...] += dot_nt(d_inner, we[...])

    @pl.when(j == pl.num_programs(0) - 1)
    def _():
        upstream = resid[...] + acc[...]
        n = n1[...].astype(F32)
        small_out[3:4, :] = column_sum(upstream * n)
        small_out[4:5, :] = column_sum(upstream)
        d_one = norm_rows_back(upstream, n, inv1[...], gain1[...])
        resid_out[...] = d_one
        d_one_b = d_one.astype(BF)
        one_out[...] = d_one_b
        small_out[5:6, :] = column_sum(d_one_b.astype(F32))


def ffn_backward(phase, micros, grad_scale, info, received, kept, weights, old):
    (out_all, n2, inv2, slope, n1, inv1) = kept
    (wc, gains, wr, we) = weights
    section, micro = 1 - phase // micros, phase % micros
    slots, rows, width = out_all.shape
    ff = we.shape[1]
    steps = ff // FFBLOCK
    slot = lambda i: slot_of(i, section, micro, micros)
    at = lambda g, i: step_of(i, section, g)
    one = lambda *shape: pl.BlockSpec(shape, lambda g, i: (0,) * len(shape))
    at_slot = lambda *shape: pl.BlockSpec((None,) + shape, lambda g, i: (slot(i), 0, 0))
    if section == 1:
        in_specs = [at_slot(rows, width), one(*wc.shape)]
        args = [out_all, wc]
    else:
        in_specs = [one(rows, width)]
        args = [received]
    in_specs += [
        at_slot(rows, width),
        at_slot(rows, 1),
        one(1, width),
        pl.BlockSpec((None, rows, FFBLOCK), lambda g, i: (slot(i), 0, at(g, i))),
        pl.BlockSpec((FFBLOCK, width), lambda g, i: (at(g, i), 0)),
        pl.BlockSpec((width, FFBLOCK), lambda g, i: (0, at(g, i))),
        at_slot(rows, width),
        at_slot(rows, 1),
        one(1, width),
    ]
    args += [n2, inv2, gains[1:2], slope, wr, we, n1, inv1, gains[0:1]]
    rows_at = lambda shape, kind: ((slots,) + shape, kind, (None,) + shape, lambda g, i: (slot(i), 0, 0))
    shapes = [
        rows_at((rows, width), BF),
        ((slots, rows, ff), BF, (None, rows, FFBLOCK), lambda g, i: (slot(i), 0, at(g, i))),
        rows_at((rows, width), BF),
        rows_at((rows, wc.shape[1]), BF),
        rows_at((8, width), F32),
        ((slots, 8, ff), F32, (None, 8, FFBLOCK), lambda g, i: (slot(i), 0, at(g, i))),
        ((rows, width), F32, (rows, width), lambda g, i: (0, 0)),
    ]
    return call(
        live_only(functools.partial(ffn_bwd_live, section == 1, micros, grad_scale), section, micro),
        steps, info, args, in_specs, shapes, old,
        [pltpu.VMEM((rows, width), F32), pltpu.VMEM((rows, width), F32)],
        flops=FLOPS_FFN,
    )


def attn_bwd_live(with_send, micro, info, one_b, joined, lse, ctx, wm, *rest):
    qcode, kcode, dctx, delta, ktr, dqtr = rest[-6:]
    if with_send:
        resid, wq, wk, wv = rest[:4]
        dq_out, dk_out, dv_out, sum_out, send_out, acc = rest[-12:-6]
    else:
        dq_out, dk_out, dv_out, sum_out = rest[-10:-6]
    g = pl.program_id(0)

    @pl.when(g == 0)
    def _():
        fill_codes(info, micro, qcode, kcode)
        if with_send:
            acc[...] = jnp.zeros(acc.shape, F32)

    dctx32 = dot_nt(one_b[...], wm[...])
    dctx[...] = dctx32.astype(BF)
    along = dctx[...].astype(F32) * ctx[...].astype(F32)
    pick = lax.broadcasted_iota(jnp.int32, (8, SLAB), 0) == lax.broadcasted_iota(jnp.int32, (8, SLAB), 1) // HEAD_DIM
    delta[...] = lax.dot_general(
        pick.astype(F32), along, (((1,), (1,)), ((), ())),
        precision=lax.Precision.HIGHEST, preferred_element_type=F32,
    )
    ktr[...] = jnp.transpose(joined[:, SLAB : 2 * SLAB])
    rows = one_b.shape[0]
    parts = (slice(0, QROWS), slice(QROWS, rows))
    for pair in range(SLAB // 128):
        lo = pair * 128
        qs = joined[:, lo : lo + 128] * BF(HEAD_DIM**-0.5)
        ks = joined[:, SLAB + lo : SLAB + lo + 128]
        vs = joined[:, 2 * SLAB + lo : 2 * SLAB + lo + 128]
        do = dctx[:, lo : lo + 128]
        qms = [head_lanes(qs, h, jnp.zeros_like(qs)) for h in range(2)]
        dms = [head_lanes(do, h, jnp.zeros_like(do)) for h in range(2)]
        ps, dss = ([], []), ([], [])
        for h in range(2):
            head = pair * 2 + h
            hh = slice(head * HEAD_DIM, head * HEAD_DIM + HEAD_DIM)
            qh = head_lanes(qs, h, qcode[...])
            kh = head_lanes(ks, h, kcode[...])
            for i, at in enumerate(parts):
                p = jnp.exp(dot_nt(kh[at], qh[at]) - lse[head : head + 1, at])
                dp = dot_nt(vs[at], dms[h][at])
                ds = (p * (dp - delta[head : head + 1, at])).astype(BF)
                ps[i].append(p.astype(BF))
                dss[i].append(ds)
                dqtr[hh, at] = dot_nn(ktr[hh, at], ds)
        for i, at in enumerate(parts):
            q_heads = jnp.concatenate([qm[at] for qm in qms])
            d_heads = jnp.concatenate([dm[at] for dm in dms])
            dk_out[at, lo : lo + 128] = dot_nn(jnp.concatenate(dss[i], axis=1), q_heads).astype(BF)
            dv_out[at, lo : lo + 128] = dot_nn(jnp.concatenate(ps[i], axis=1), d_heads).astype(BF)
    dq = (jnp.transpose(dqtr[...]) * HEAD_DIM**-0.5).astype(BF)
    dq_out[...] = dq
    dk = dk_out[...]
    dv = dv_out[...]
    sum_out[0:1, 0:SLAB] = column_sum(dq.astype(F32))
    sum_out[0:1, SLAB : 2 * SLAB] = column_sum(dv.astype(F32))
    if not with_send:
        return
    acc[...] += dot_nt(
        jnp.concatenate([dq, dk, dv], axis=1), jnp.concatenate([wq[...], wk[...], wv[...]], axis=1)
    )

    @pl.when(g == pl.num_programs(0) - 1)
    def _():
        send_out[...] = (resid[...] + acc[...]).astype(BF)


def attn_backward(phase, micros, info, resid, one_all, kept, weights, old, slabs=None):
    (joined, lse, ctx) = kept
    (wa, wm) = weights
    section, micro = 1 - phase // micros, phase % micros
    slots, rows, width = one_all.shape
    count = width // SLAB
    slabs = slabs or range(count)
    with_send = section == 1
    slot = lambda i: slot_of(i, section, micro, micros)
    at = lambda g, i: step_of(i, section, slabs[0] + g)
    in_specs = [
        pl.BlockSpec((None, rows, width), lambda g, i: (slot(i), 0, 0)),
        pl.BlockSpec((None, None, rows, 3 * SLAB), lambda g, i: (slot(i), at(g, i), 0, 0)),
        pl.BlockSpec((None, None, 8, rows), lambda g, i: (slot(i), at(g, i), 0, 0)),
        pl.BlockSpec((None, rows, SLAB), lambda g, i: (slot(i), 0, at(g, i))),
        pl.BlockSpec((SLAB, width), lambda g, i: (at(g, i), 0)),
    ]
    args = [one_all, joined, lse, ctx, wm]
    slab = ((slots, rows, width), BF, (None, rows, SLAB), lambda g, i: (slot(i), 0, at(g, i)))
    shapes = [
        slab,
        slab,
        slab,
        ((slots, count, 8, 2 * SLAB), F32, (None, None, 8, 2 * SLAB), lambda g, i: (slot(i), at(g, i), 0, 0)),
    ]
    scratch = [
        pltpu.VMEM((rows, 128), BF),
        pltpu.VMEM((rows, 128), BF),
        pltpu.VMEM((rows, SLAB), BF),
        pltpu.VMEM((8, rows), F32),
        pltpu.VMEM((SLAB, rows), BF),
        pltpu.VMEM((SLAB, rows), F32),
    ]
    if with_send:
        in_specs += [
            pl.BlockSpec((rows, width), lambda g, i: (0, 0)),
            pl.BlockSpec((width, SLAB), lambda g, i: (0, at(g, i))),
            pl.BlockSpec((width, SLAB), lambda g, i: (0, count + at(g, i))),
            pl.BlockSpec((width, SLAB), lambda g, i: (0, 2 * count + at(g, i))),
        ]
        args += [resid, wa, wa, wa]
        shapes += [((rows, width), BF, (rows, width), lambda g, i: (0, 0))]
        scratch = [pltpu.VMEM((rows, width), F32)] + scratch
    return call(
        live_only(functools.partial(attn_bwd_live, with_send), section, micro),
        len(slabs), info, args, in_specs, shapes, old, scratch,
        flops=FLOPS_ATTN * len(slabs) // count // (1 if with_send else 32),
        limit=VMEM_LIMIT if with_send else SMALL_VMEM,
    )


def mesh_bits():
    place = lax.axis_index("dp")
    bits = []
    bit = 1
    while bit < lax.axis_size("dp"):
        bits.append((bit, (place // bit) % 2))
        bit *= 2
    return bits


def grad_call(body, steps, core, in_specs, args, out_shape, out_specs, flops, limit=SMALL_VMEM):
    return pl.pallas_call(
        body,
        out_shape=out_shape,
        grid_spec=pltpu.PrefetchScalarGridSpec(
            num_scalar_prefetch=1,
            grid=(steps,),
            in_specs=in_specs,
            out_specs=out_specs,
        ),
        compiler_params=pltpu.CompilerParams(vmem_limit_bytes=limit),
        cost_estimate=pl.CostEstimate(flops=flops // 16, bytes_accessed=100_000, transcendentals=0),
    )(core, *args)


def grad_half_body(by_rows, info, left, *refs):
    rights = refs[: 1 if by_rows else 2]
    bases, outs = refs[len(rights) : -2], refs[-2:]
    turned = jnp.transpose(left[...])
    tall = outs[0].shape[0]
    for i, out in enumerate(outs):
        total = dot_nn(turned[i * tall : i * tall + tall], rights[0][...]) if by_rows else dot_nn(turned, rights[i][...])
        if bases:
            total = total + bases[i][...].astype(F32)
        out[...] = total.astype(BF)


def grad_half(rows, micro, core, mine, left, right, by_rows, bases):
    tall, wide = left.shape[1] // 2, right.shape[1]
    steps = GRAD_STEPS
    half_of = lambda h: h[0] if mine else 1 - h[0]
    left_spec = pl.BlockSpec((rows, tall), lambda s, h: (micro, half_of(h)))
    if by_rows:
        shape = (tall // 2, wide)
        rights = [pl.BlockSpec((rows, wide // steps), lambda s, h: (micro, s))]
    else:
        shape = (tall, wide // 2)
        rights = [
            pl.BlockSpec((rows, wide // 2 // steps), lambda s, h, i=i: (micro, i * steps + s)) for i in range(2)
        ]
    spec = pl.BlockSpec((shape[0], shape[1] // steps), lambda s, h: (0, s))
    args = [left] + [right] * len(rights) + list(bases or ())
    in_specs = [left_spec] + rights + ([spec, spec] if bases else [])
    out = jax.ShapeDtypeStruct(shape, BF)
    return grad_call(
        functools.partial(grad_half_body, by_rows), steps, core, in_specs, args,
        [out, out], [spec, spec], 2 * rows * tall * wide, VMEM_LIMIT,
    )


def grad_rest_body(with_context, info, inputs, *refs):
    out = refs[-1]
    turned = jnp.transpose(inputs[...])
    parts = []
    if with_context:
        parts.append(dot_nn(jnp.transpose(refs[0][...]), refs[1][...]))
        refs = refs[2:]
    for at in range(0, len(refs) - 3, 3):
        parts.append(dot_nn(turned, jnp.concatenate([right[...] for right in refs[at : at + 3]], axis=1)))
    at = 0
    for part in parts:
        here = slice(at, at + part.shape[1])
        total = part if refs[-2] is None else part + refs[-2][:, here].astype(F32)
        out[:, here] = total.astype(BF)
        at += part.shape[1]


def grad_rest(rows, micro, core, mine, inputs, joined_grads, slabs, context, d_one, base):
    width = inputs.shape[1]
    side = pl.BlockSpec((rows, width // 2), lambda s, h: (micro, h[0] if mine else 1 - h[0]))
    in_specs, args = [side], [inputs]
    columns = 0
    if context is not None:
        in_specs += [side, pl.BlockSpec((rows, width), lambda s, h: (micro, 0))]
        args += [context, d_one]
        columns += width
    for slab in slabs:
        in_specs += [pl.BlockSpec((rows, SLAB), lambda s, h, slab=slab: (micro, slab))] * 3
        args += joined_grads
        columns += 3 * SLAB
    out = jax.ShapeDtypeStruct((width // 2, columns), BF)
    whole = pl.BlockSpec(out.shape, lambda s, h: (0, 0))
    if base is not None:
        in_specs += [whole]
        args += [base]
    body = functools.partial(grad_rest_body, context is not None)
    return grad_call(
        body if base is not None else lambda *refs: body(*refs[:-1], None, refs[-1]), 1, core, in_specs, args,
        out, whole, rows * columns * width,
    )


def widen_body(info, own_a, own_b, other_a, other_b, *outs):
    step = pl.program_id(0)
    for s, (a, b) in enumerate(((own_a, own_b), (other_a, other_b))):

        @pl.when(step == s)
        def _(a=a, b=b):
            parts = (a[...].astype(F32), b[...].astype(F32))
            if len(outs) == 2:
                width = outs[1].shape[1]
                outs[1][...] = parts[0][:, :width]
                slabs = [parts[0][:, width:]] + [
                    parts[1][:, at : at + 3 * SLAB] for at in range(0, parts[1].shape[1], 3 * SLAB)
                ]
                for g, slab in enumerate(slabs):
                    for kind in range(3):
                        at = kind * width + g * SLAB
                        outs[0][:, at : at + SLAB] = slab[:, kind * SLAB : kind * SLAB + SLAB]
            elif outs[0].shape[1] == parts[0].shape[1]:
                outs[0][: parts[0].shape[0]] = parts[0]
                outs[0][parts[0].shape[0] :] = parts[1]
            else:
                outs[0][:, : parts[0].shape[1]] = parts[0]
                outs[0][:, parts[0].shape[1] :] = parts[1]


def widened(core, own, other, out_shapes):
    small = own[0].shape
    piece_spec = pl.BlockSpec(small, lambda s, h: (0, 0))
    return pl.pallas_call(
        widen_body,
        out_shape=[jax.ShapeDtypeStruct(shape, F32) for shape in out_shapes],
        grid_spec=pltpu.PrefetchScalarGridSpec(
            num_scalar_prefetch=1,
            grid=(2,),
            in_specs=[piece_spec] * 4,
            out_specs=[
                pl.BlockSpec((shape[0] // 2, shape[1]), lambda s, h: (jnp.where(s == 0, h[0], 1 - h[0]), 0))
                for shape in out_shapes
            ],
        ),
        compiler_params=pltpu.CompilerParams(vmem_limit_bytes=SMALL_VMEM),
        cost_estimate=pl.CostEstimate(flops=0, bytes_accessed=14_000_000, transcendentals=0),
    )(core, *own, *other)


EXCHANGE = (
    "SR", "KR", "R0", "SE", "R1", "KE", "E1", "S0", "R0", "E0", "PS", "PK", "R0", "E1", "R1", "P0", "S1",
    "R1", "E1", "R0", "E0", "S2", "P0", "R1", "QS", "R0", "E1", "QK", "Q0", "E0", "R1", "P0", "R0", "E0",
    "Q0", "V", "P0", "E0", "R1", "E1", "Q0", "V", "E0", "P0", "Q0", "Q0", "P0", "V", "R0", "E1", "R1", "Q0",
    "E0", "V", "WR", "E1", "P0", "Q0", "WE", "WP",
)
ORDERS = {"R0": 0, "R1": 0, "E0": 0, "E1": 1, "P0": 0, "Q0": 0}
WIDENED = {"WR": ("R0", "R1"), "WE": ("E0", "E1"), "WP": ("P0", "Q0")}
KERNELS = ("SR", "KR", "SE", "KE", "S0", "PS", "PK", "S1", "S2", "QS", "QK")


def passed_along(array, axis, by):
    count = lax.axis_size(axis)
    pairs = [(i, i + by) for i in range(count) if 0 <= i + by < count]
    return lax.ppermute(array, axis, pairs)


def tied(array, *others):
    return lax.optimization_barrier((array, *others))[0]


def flatten_rows(leaf):
    return leaf.reshape(-1, leaf.shape[-1])


def swapped(array, bit, axis="dp"):
    count = lax.axis_size(axis)
    return lax.ppermute(array, axis, [(i, i ^ bit) for i in range(count)])


def piece(array, index):
    return lax.dynamic_index_in_dim(array, index, 0, keepdims=False)


def sum_low(kept, got):
    return (kept.astype(F32) + got.astype(F32)).astype(BF)


class Sequence:
    def __init__(self):
        self.last = ()

    def after(self, array):
        return tied(array, *self.last)

    def did(self, *arrays):
        self.last = arrays
        return arrays


class Adder:
    def __init__(self, sequence, value, bits):
        self.sequence, self.value = sequence, value
        self.bits = [step for step, _ in bits]
        self.got = swapped(value, self.bits[0])

    def take(self):
        self.bits.pop(0)
        self.value = sum_low(self.sequence.after(self.value), self.got)
        self.sequence.did(self.value)
        if self.bits:
            self.got = swapped(self.value, self.bits[0])


class Piece:
    def __init__(self, sequence, sent, kept, bits, order):
        self.sequence = sequence
        self.value = kept
        self.steps = [(sum_low, None)]
        self.steps += [(halved, bits[place]) for place in order]
        self.steps += [(doubled, bits[place]) for place in reversed(order)]
        self.got = swapped(sent, 1)

    def send(self):
        if not self.steps:
            self.sequence.did(self.value)
            self.got = swapped(self.value, 1)
            return
        step, (bit, mine) = self.steps[0]
        sent = self.value
        if step is halved:
            sent = piece(sent.reshape(2, sent.shape[0] // 2, sent.shape[1]), 1 - mine)
        self.sequence.did(self.value, sent)
        self.got = swapped(sent, bit)

    def take(self):
        step, bit = self.steps.pop(0)
        value = self.sequence.after(self.value)
        self.value = step(value, self.got) if bit is None else step(value, self.got, bit[1])
        self.send()


def halved(array, got, mine):
    halves = array.reshape(2, array.shape[0] // 2, array.shape[1])
    return sum_low(piece(halves, mine), got)


def doubled(array, got, mine):
    both = jnp.zeros((2,) + array.shape, array.dtype)
    both = lax.dynamic_update_index_in_dim(both, array, mine, 0)
    both = lax.dynamic_update_index_in_dim(both, got, 1 - mine, 0)
    return flatten_rows(both)


def exchange_order(digits):
    if digits == 4:
        return EXCHANGE
    rounds = ("R0", "R1", "E0", "E1", "P0", "Q0") * (2 * digits - 1)
    return KERNELS + rounds + ("V",) * digits + tuple(WIDENED)


def ends_of_pieces(pieces):
    return [one.value for one in pieces], [one.got for one in pieces]


def take(*pieces):
    for one in pieces:
        one.take()


def shards(
    hidden_in,
    attend_weight,
    attend_bias,
    mixing_weight,
    mixing_bias,
    norm_gain,
    norm_shift,
    expand_weight,
    expand_bias,
    reduce_weight,
    reduce_bias,
    colbert_weight,
    pass_lengths,
    positives,
):
    section_id = lax.axis_index("pipe")
    data_count = lax.axis_size("dp")
    micros = pass_lengths.shape[0]
    rows = hidden_in.shape[0] // micros
    width = hidden_in.shape[1]
    grad_scale = 1.0 / (data_count * micros * NQ)
    wa, wm, we, wr = attend_weight[0], mixing_weight[0], expand_weight[0], reduce_weight[0]
    gains, shifts = norm_gain[0], norm_shift[0]
    info = jnp.concatenate(
        [section_id.astype(jnp.int32)[None], pass_lengths.reshape(-1), positives.reshape(-1)]
    )
    bits = mesh_bits()
    core = bits[0][1].astype(jnp.int32)[None]
    along_x_first = list(range(1, len(bits)))
    along_z_first = [2, 1] + list(range(3, len(bits)))
    orders = (along_x_first, along_z_first)
    attn_weights = (wa, attend_bias, wm, mixing_bias, gains, shifts)
    ffn_weights = (we, expand_bias, wr, reduce_bias, gains, shifts)
    state = {"attn": None, "ffn": None, "attn_back": None, "ffn_back": None}
    arriving, returning = {}, {}

    def forward(phase, after=()):
        source = hidden_in if phase < micros else arriving[phase - micros]
        source = tied(source, *after)
        attn = attn_forward(phase, micros, info, source, attn_weights, state["attn"])
        old = state["ffn"]
        ffn = ffn_forward(phase, micros, info, attn[4], ffn_weights, old and old[:6])
        state["attn"], state["ffn"] = attn, ffn
        if phase < micros:
            arriving[phase] = passed_along(ffn[6], "pipe", 1)

    def backward_ffn(phase, after=()):
        attn, ffn, old = state["attn"], state["ffn"], state["ffn_back"]
        received = None if phase < micros else tied(returning[phase - micros], *after)
        state["ffn_back"] = ffn_backward(
            phase, micros, grad_scale, info, received,
            (ffn[2], ffn[3], ffn[4], ffn[1], attn[5], attn[6]),
            (colbert_weight, gains, wr, we), old and old[:6],
        )

    def backward_attn(phase, after=(), slabs=None):
        attn, old, ffn_back = state["attn"], state["attn_back"], state["ffn_back"]
        attn_back = attn_backward(
            phase, micros, tied(info, *after), ffn_back[6], ffn_back[2], (attn[1], attn[2], attn[3]), (wa, wm),
            old and old[:4], slabs,
        )
        state["attn_back"] = attn_back
        if phase < micros:
            returning[phase] = passed_along(attn_back[4], "pipe", -1)

    for phase in range(micros):
        forward(phase)
    done = ()
    for phase in range(micros):
        forward(micros + phase, done)
        backward_ffn(phase)
        backward_attn(phase)
        done = (state["attn_back"][3],)
    for phase in range(micros, 2 * micros - 1):
        backward_ffn(phase, done)
        backward_attn(phase)
        done = (state["attn_back"][3],)
    inputs, joined, lse, context, hidden, unit_one, inv_one, squares_one = state["attn"]
    active, slope, outputs, unit_two, inv_two, squares_two, _ = state["ffn"]
    embeds, losses = state["ffn_back"][3], state["ffn_back"][4]
    squares = jnp.stack(
        [
            jnp.sum(squares_one[:micros, 0], axis=1),
            jnp.sum(squares_one[:micros, 1], axis=1),
            jnp.sum(squares_two[:micros, 0], axis=1),
        ],
        axis=1,
    )
    after_back = state["attn_back"][3]
    colbert = dot_tn(
        flatten_rows(outputs[:micros]), flatten_rows(tied(embeds, after_back)[:micros])
    ).astype(BF)
    facts = tied(jnp.concatenate([squares, losses[:micros, 6, 0:1]], axis=1), after_back)
    last = 2 * micros - 1
    slabs = tuple(range(width // SLAB))
    ffn_back, attn_back = state["ffn_back"], state["attn_back"]
    lefts = [flatten_rows(a) for a in (active, hidden, inputs, context)]

    bases = {}
    for micro in range(micros - 1):
        first_core = tied(core, after_back)
        d_two, d_inner, d_one = (flatten_rows(ffn_back[i]) for i in range(3))
        joined_grads = [flatten_rows(a) for a in attn_back[:3]]
        for mine in (0, 1):
            old = bases.get(mine, (None,) * 4)
            bases[mine] = (
                grad_half(rows, micro, first_core, mine, lefts[0], d_two, True, old[0]),
                grad_half(rows, micro, first_core, mine, lefts[1], d_inner, False, old[1]),
                grad_rest(rows, micro, first_core, mine, lefts[2], joined_grads, slabs[:1], lefts[3], d_one, old[2]),
                grad_rest(rows, micro, first_core, mine, lefts[2], joined_grads, slabs[1:], None, None, old[3]),
            )
    backward_ffn(last, (colbert, facts) + tuple(jax.tree.leaves(bases)))
    bases = bases or {0: (None,) * 4, 1: (None,) * 4}
    micro = micros - 1
    ffn_back = state["ffn_back"]
    d_two, d_inner, d_one = (flatten_rows(ffn_back[i]) for i in range(3))
    line = Sequence()

    def half_of(mine, left, right, by_rows, which):
        both = grad_half(rows, micro, line.after(core), mine, left, right, by_rows, bases[mine][which])
        line.did(*both)
        return both

    def rest_half(mine, some, which):
        joined_grads = [flatten_rows(a) for a in state["attn_back"][:3]]
        extra = (lefts[3], d_one) if which == 2 else (None, None)
        [one] = line.did(
            grad_rest(rows, micro, line.after(core), mine, lefts[2], joined_grads, some, *extra, bases[mine][which])
        )
        return one

    def slab_back(slab):
        backward_attn(last, line.last, (slab,))
        line.did(*state["attn_back"])

    made, pieces, widths = {}, {}, {}

    def run_kernel(name):
        made[name] = {
            "SR": lambda: half_of(0, lefts[0], d_two, True, 0),
            "KR": lambda: half_of(1, lefts[0], d_two, True, 0),
            "SE": lambda: half_of(0, lefts[1], d_inner, False, 1),
            "KE": lambda: half_of(1, lefts[1], d_inner, False, 1),
            "PS": lambda: [rest_half(0, slabs[:1], 2)],
            "PK": lambda: [rest_half(1, slabs[:1], 2)],
            "QS": lambda: [rest_half(0, slabs[1:], 3)],
            "QK": lambda: [rest_half(1, slabs[1:], 3)],
            "S0": lambda: slab_back(slabs[0]),
            "S1": lambda: slab_back(slabs[1]),
            "S2": lambda: [slab_back(slab) for slab in slabs[2:]],
        }[name]()

    def small_sums():
        small, small_ff, joined_sums = ffn_back[4], ffn_back[5], state["attn_back"][3]
        small_sum = jnp.sum(small[:micros], axis=0)
        joined_sum = jnp.sum(joined_sums[:micros, :, 0], axis=0)
        attend_sum = jnp.concatenate(
            [joined_sum[:, :SLAB].reshape(-1), joined_sum[:, SLAB:].reshape(-1)]
        )
        of_colbert = tied(colbert, *line.last)
        of_colbert = jnp.where(section_id == 1, of_colbert, passed_along(of_colbert, "pipe", -1))
        parts = [
            small_sum[:6],
            attend_sum.reshape(2, width),
            jnp.sum(small_ff[:micros, 0], axis=0).reshape(-1, width),
            of_colbert.astype(F32).reshape(-1, width),
        ]
        return jnp.concatenate(parts).astype(BF)

    senders = {"SR": ("R", "KR", 2), "SE": ("E", "KE", 2), "PS": ("P", "PK", 1), "QS": ("Q", "QK", 1)}
    for step in exchange_order(len(bits)):
        if step in pieces:
            pieces[step].take()
        elif step[0] == "W":
            widths[step] = widened(
                line.after(core), *ends_of_pieces([pieces[one] for one in WIDENED[step]]),
                {"WR": [wr.shape], "WE": [we.shape], "WP": [wa.shape, wm.shape]}[step],
            )
            line.did(*widths[step])
        else:
            run_kernel(step)
            for send, (name, keep, count) in senders.items():
                if keep == step:
                    for i, (s, k) in enumerate(zip(made[send], made[keep])):
                        one = name + str(i)
                        pieces[one] = Piece(line, s, k, bits, orders[ORDERS[one]])
            if step == "QK":
                mine = line.after(facts)
                made["up"], made["down"] = passed_along(mine, "pipe", 1), passed_along(mine, "pipe", -1)
                pieces["V"] = Adder(line, small_sums(), bits)
    first = jnp.where(section_id == 0, facts, made["up"])
    second = jnp.where(section_id == 0, made["down"], facts)
    [big_reduce], [big_expand], (big_attend, big_mixing) = (widths[one] for one in ("WR", "WE", "WP"))
    vector = pieces["V"].value
    vector = vector.astype(F32)
    colbert_sum = vector[8 + we.shape[1] // width :].reshape(colbert_weight.shape)
    counted = (QROWS + jnp.sum(pass_lengths, axis=1)).astype(F32)
    stats = jnp.stack([first[:, :3], second[:, :3]], axis=1)
    stats = jnp.sqrt(stats / (counted[:, None, None] * width))
    return (
        big_attend[None],
        vector[6:8].reshape(1, -1),
        big_mixing[None],
        vector[5][None],
        jnp.stack([vector[3], vector[0]])[None],
        jnp.stack([vector[4], vector[1]])[None],
        big_expand[None],
        vector[8 : 8 + we.shape[1] // width].reshape(1, -1),
        big_reduce[None],
        vector[2][None],
        colbert_sum,
        second[:, 3] / NQ,
        stats,
    )


def solution(mesh):
    placed = (
        P("dp", None),
        P("pipe", None, None),
        P("pipe", None),
        P("pipe", None, None),
        P("pipe", None),
        P("pipe", None, None),
        P("pipe", None, None),
        P("pipe", None, None),
        P("pipe", None),
        P("pipe", None, None),
        P("pipe", None),
        P(),
        P("dp", None),
        P("dp", None),
    )
    return jax.shard_map(
        shards,
        mesh=mesh,
        in_specs=placed,
        out_specs=(
            P("pipe", None, None),
            P("pipe", None),
            P("pipe", None, None),
            P("pipe", None),
            P("pipe", None, None),
            P("pipe", None, None),
            P("pipe", None, None),
            P("pipe", None),
            P("pipe", None, None),
            P("pipe", None),
            P(),
            P("dp"),
            P("dp", None, None),
        ),
        check_vma=False,
    )
```

```python
import functools
import jax
import jax.numpy as jnp
from jax import lax
from jax.experimental import pallas as pl
from jax.experimental.pallas import tpu as pltpu
from jax.sharding import PartitionSpec as P

HEAD_DIM = 64
QLEN = 32
NQ = 4
NP = 4
PSLOTS = 512
LAYER_EPSILON = 1e-12
UNIT_EPSILON = 1e-06
SMOOTHING = 0.05
LOGIT_SCALE = 4.0
ROOT_HALF = 0.7071067811865476
NORMAL_PEAK = 0.3989422804014327
BF = jnp.bfloat16
F32 = jnp.float32
QROWS = NQ * QLEN
SLAB = 256
FFBLOCK = 1536
VMEM_LIMIT = 56 * 1024 * 1024
NEG = -1e30
GRAD_STEPS = 2
SMALL_VMEM = 26 * 1024 * 1024
SLAB_VMEM = VMEM_LIMIT
FLOPS_FFN = 12_000_000_000
FLOPS_ATTN = 20_000_000_000


def dot_nn(a, b):
    return jnp.dot(a, b, preferred_element_type=F32)


def dot_nt(a, b):
    return lax.dot_general(a, b, (((1,), (1,)), ((), ())), preferred_element_type=F32)


def dot_tn(a, b):
    return lax.dot_general(a, b, (((0,), (0,)), ((), ())), preferred_element_type=F32)


def gelu_pair(u):
    phi = 0.5 + 0.5 * lax.erf(u * ROOT_HALF)
    return u * phi, phi + NORMAL_PEAK * u * jnp.exp(-0.5 * u * u)


def norm_rows(resid):
    centre = resid - jnp.mean(resid, axis=1, keepdims=True)
    inv = lax.rsqrt(jnp.mean(centre * centre, axis=1, keepdims=True) + LAYER_EPSILON)
    return centre * inv, inv


def ends_of(info, micro):
    base = 1 + micro * NP
    ends = []
    total = jnp.int32(0)
    for j in range(NP):
        total = total + info[base + j]
        ends.append(total)
    return ends


def passage_of(place, ends):
    out = jnp.zeros(place.shape, jnp.int32)
    for end in ends:
        out = out + jnp.where(place >= end, 1, 0)
    return out


def when_live(info, section, body):
    pl.when(info[0] == section)(body)


def slot_of(info, section, micro, spare):
    return jnp.where(info[0] == section, micro, spare)


def step_of(info, section, step):
    return jnp.where(info[0] == section, step, 0)


def fill_codes(info, micro, query_code, key_code):
    rows = query_code.shape[0]
    ends = [QROWS + end for end in ends_of(info, micro)]
    place = lax.broadcasted_iota(jnp.int32, (rows, 1), 0)
    segment = jnp.where(place < QROWS, place // QLEN, NQ + passage_of(place, ends))
    lane = lax.broadcasted_iota(jnp.int32, (1, 128), 1) % HEAD_DIM
    query_code[...] = jnp.where(segment == lane, 1.0, 0.0).astype(BF)
    key_code[...] = jnp.where((segment == lane) | (lane > NQ + NP), 0.0, NEG).astype(BF)


def usable_rows(info, micro, rows):
    ends = ends_of(info, micro)
    place = lax.broadcasted_iota(jnp.int32, (rows, 1), 0)
    return (place < QROWS + ends[-1]).astype(F32)


def head_lanes(value, h, others):
    lane = lax.broadcasted_iota(jnp.int32, (1, 128), 1) // HEAD_DIM
    return jnp.where(lane == h, value, others)


def live_only(body, section, micro):
    def kernel(info, *refs):
        when_live(info, section, lambda: body(micro, info, *refs))

    return kernel


def attn_fwd_live(g, count, micro, info, hid, wq, wk, wv, bq, bv, wm, bm, gain, shift, *rest):
    x_out, joined_out, lse_out, ctx_out, hid_out, n_out, inv_out, sq_out, acc, qcode, kcode, otr, vtr = rest
    rows = hid.shape[0]

    @pl.when(g == 0)
    def _():
        x_out[...] = hid[...]
        fill_codes(info, micro, qcode, kcode)
        acc[...] = jnp.zeros(acc.shape, F32)

    x = hid[...]
    qkv = dot_nn(x, jnp.concatenate([wq[...], wk[...], wv[...]], axis=1))
    q = (qkv[:, :SLAB] + bq[...]).astype(BF)
    joined_out[:, 0:SLAB] = q
    k = qkv[:, SLAB : 2 * SLAB].astype(BF)
    joined_out[:, SLAB : 2 * SLAB] = k
    v = (qkv[:, 2 * SLAB :] + bv[...]).astype(BF)
    joined_out[:, 2 * SLAB : 3 * SLAB] = v
    vtr[...] = jnp.transpose(v)
    parts = (slice(0, QROWS), slice(QROWS, rows))
    for pair in range(SLAB // 128):
        cols = slice(pair * 128, pair * 128 + 128)
        qs = joined_out[:, cols] * BF(HEAD_DIM**-0.5)
        ks = joined_out[:, SLAB + pair * 128 : SLAB + pair * 128 + 128]
        for h in range(2):
            head = pair * 2 + h
            vh = slice(head * HEAD_DIM, head * HEAD_DIM + HEAD_DIM)
            qh = head_lanes(qs, h, qcode[...])
            kh = head_lanes(ks, h, kcode[...])
            for at in parts:
                st = dot_nt(kh[at], qh[at])
                top = jnp.max(st, axis=0, keepdims=True)
                p = jnp.exp(st - top)
                total = jnp.sum(p, axis=0, keepdims=True)
                lse_out[head : head + 1, at] = top + jnp.log(total)
                otr[vh, at] = dot_nn(vtr[vh, at], p.astype(BF)) * (1.0 / total)
    ctx = jnp.transpose(otr[...]).astype(BF)
    ctx_out[...] = ctx
    acc[...] += dot_nn(ctx, wm[...])

    @pl.when(g == count - 1)
    def _():
        b1 = acc[...] + bm[...]
        x32 = hid[...].astype(F32)
        n, inv = norm_rows(x32 + b1)
        hid_out[...] = (n * gain[...] + shift[...]).astype(BF)
        n_out[...] = n.astype(BF)
        inv_out[...] = inv
        mask = usable_rows(info, micro, rows)
        sq_out[0:1, :] = jnp.sum(mask * x32 * x32, axis=0, keepdims=True)
        sq_out[1:2, :] = jnp.sum(mask * b1 * b1, axis=0, keepdims=True)


def call(body, steps, info, args, in_specs, shapes, old, scratch, flops, limit=VMEM_LIMIT):
    aliases = {}
    if old is not None:
        in_specs = in_specs + [pl.BlockSpec(memory_space=pl.ANY)] * len(old)
        aliases = {1 + len(args) + i: i for i in range(len(old))}
        args = args + list(old)
    return pl.pallas_call(
        body,
        out_shape=[jax.ShapeDtypeStruct(s[0], s[1]) for s in shapes],
        grid_spec=pltpu.PrefetchScalarGridSpec(
            num_scalar_prefetch=1,
            grid=(steps,),
            in_specs=in_specs,
            out_specs=[pl.BlockSpec(s[2], s[3]) for s in shapes],
            scratch_shapes=scratch,
        ),
        input_output_aliases=aliases,
        compiler_params=pltpu.CompilerParams(
            dimension_semantics=("arbitrary",), vmem_limit_bytes=limit
        ),
        cost_estimate=pl.CostEstimate(flops=flops, bytes_accessed=min(20_000_000, flops // 600), transcendentals=0),
    )(info, *args)


def ffn_fwd_live(j, count, micro, info, hid, we, be, wr, br, gain, shift, *rest):
    act_out, slope_out, out_all, n_out, inv_out, sq_out, send_out, acc = rest
    rows = hid.shape[0]

    @pl.when(j == 0)
    def _():
        acc[...] = jnp.zeros(acc.shape, F32)

    inner = dot_nn(hid[...], we[...]) + be[...]
    active, slope = gelu_pair(inner)
    active = active.astype(BF)
    act_out[...] = active
    slope_out[...] = slope.astype(BF)
    acc[...] += dot_nn(active, wr[...])

    @pl.when(j == count - 1)
    def _():
        b2 = acc[...] + br[...]
        n, inv = norm_rows(hid[...].astype(F32) + b2)
        out = (n * gain[...] + shift[...]).astype(BF)
        out_all[...] = out
        send_out[...] = out
        n_out[...] = n.astype(BF)
        inv_out[...] = inv
        mask = usable_rows(info, micro, rows)
        sq_out[0:1, :] = jnp.sum(mask * b2 * b2, axis=0, keepdims=True)


def layer_fwd_live(first, second, micro, info, *refs):
    attn_in, ffn_in = refs[:10], refs[10:16]
    attn_out, ffn_out = refs[-20:-12], refs[-12:-5]
    acc, qcode, kcode, otr, vtr = refs[-5:]
    g = pl.program_id(0)

    @pl.when(g < first)
    def _():
        attn_fwd_live(g, first, micro, info, *attn_in, *attn_out, acc, qcode, kcode, otr, vtr)

    @pl.when(g >= first)
    def _():
        ffn_fwd_live(g - first, second, micro, info, attn_out[4], *ffn_in, *ffn_out, acc)


def layer_forward(phase, micros, info, source, weights, old):
    (wa, ba, wm, bm, we, be, wr, br, gains, shifts) = weights
    section, micro = phase // micros, phase % micros
    width, ff = we.shape
    rows = source.shape[0] // micros if section == 0 else source.shape[0]
    place = micro if section == 0 else 0
    first, second = width // SLAB, ff // FFBLOCK
    slot = lambda i: slot_of(i, section, micro, micros)
    at = lambda g, i: step_of(i, section, jnp.minimum(g, first - 1))
    on = lambda g, i: step_of(i, section, jnp.maximum(g - first, 0))
    one = lambda *shape: pl.BlockSpec(shape, lambda g, i: (0,) * len(shape))
    in_specs = [
        pl.BlockSpec((rows, width), lambda g, i: (place, 0)),
        pl.BlockSpec((width, SLAB), lambda g, i: (0, at(g, i))),
        pl.BlockSpec((width, SLAB), lambda g, i: (0, first + at(g, i))),
        pl.BlockSpec((width, SLAB), lambda g, i: (0, 2 * first + at(g, i))),
        pl.BlockSpec((1, SLAB), lambda g, i: (0, at(g, i))),
        pl.BlockSpec((1, SLAB), lambda g, i: (0, first + at(g, i))),
        pl.BlockSpec((SLAB, width), lambda g, i: (at(g, i), 0)),
        one(1, width),
        one(1, width),
        one(1, width),
        pl.BlockSpec((width, FFBLOCK), lambda g, i: (0, on(g, i))),
        pl.BlockSpec((1, FFBLOCK), lambda g, i: (0, on(g, i))),
        pl.BlockSpec((FFBLOCK, width), lambda g, i: (on(g, i), 0)),
        one(1, width),
        one(1, width),
        one(1, width),
    ]
    args = [source, wa, wa, wa, ba, ba, wm, bm, gains[0:1], shifts[0:1]]
    args += [we, be, wr, br, gains[1:2], shifts[1:2]]
    slots = micros + 1
    rows_at = lambda shape, kind: ((slots,) + shape, kind, (None,) + shape, lambda g, i: (slot(i), 0, 0))
    wide = ((slots, rows, ff), BF, (None, rows, FFBLOCK), lambda g, i: (slot(i), 0, on(g, i)))
    shapes = [
        rows_at((rows, width), BF),
        ((slots, first, rows, 3 * SLAB), BF, (None, None, rows, 3 * SLAB), lambda g, i: (slot(i), at(g, i), 0, 0)),
        ((slots, first, 8, rows), F32, (None, None, 8, rows), lambda g, i: (slot(i), at(g, i), 0, 0)),
        ((slots, rows, width), BF, (None, rows, SLAB), lambda g, i: (slot(i), 0, at(g, i))),
        rows_at((rows, width), BF),
        rows_at((rows, width), BF),
        rows_at((rows, 1), F32),
        rows_at((8, width), F32),
        wide,
        wide,
        rows_at((rows, width), BF),
        rows_at((rows, width), BF),
        rows_at((rows, 1), F32),
        rows_at((8, width), F32),
        ((rows, width), BF, (rows, width), lambda g, i: (0, 0)),
    ]
    return call(
        live_only(functools.partial(layer_fwd_live, first, second), section, micro),
        first + second, info, args, in_specs, shapes, old,
        [
            pltpu.VMEM((rows, width), F32),
            pltpu.VMEM((rows, 128), BF),
            pltpu.VMEM((rows, 128), BF),
            pltpu.VMEM((SLAB, rows), F32),
            pltpu.VMEM((SLAB, rows), BF),
        ],
        flops=FLOPS_FFN + FLOPS_ATTN,
    )


def column_sum(value):
    return jnp.sum(value, axis=0, keepdims=True)


def norm_rows_back(grad_out, n, inv, gain):
    grad_unit = grad_out * gain
    mean_grad = jnp.mean(grad_unit, axis=1, keepdims=True)
    mean_along = jnp.mean(grad_unit * n, axis=1, keepdims=True)
    return inv * (grad_unit - mean_grad - n * mean_along)


def loss_parts(info, micro, micros, grad_scale, out_b, wc):
    ends = ends_of(info, micro)
    embedded = dot_nn(out_b, wc)
    inv_norm = lax.rsqrt(jnp.sum(embedded * embedded, axis=1, keepdims=True) + UNIT_EPSILON)
    unit = embedded * inv_norm
    unit_b = unit.astype(BF)
    queries, passages = unit_b[:QROWS], unit_b[QROWS:]
    scaled = dot_nt(queries, passages) / SMOOTHING
    owner = passage_of(lax.broadcasted_iota(jnp.int32, (1, PSLOTS), 1), ends)
    top = jnp.max(jnp.where(owner < NP, scaled, NEG), axis=1, keepdims=True)
    terms = jnp.exp(scaled - top)
    lane = lax.broadcasted_iota(jnp.int32, (1, 128), 1)
    totals = jnp.ones((QROWS, 128), F32)
    lengths = jnp.ones((1, 128), F32)
    for j in range(NP):
        total = jnp.sum(jnp.where(owner == j, terms, 0.0), axis=1, keepdims=True)
        totals = jnp.where(lane == j, total, totals)
        lengths = jnp.where(lane == j, info[1 + micro * NP + j].astype(F32), lengths)
    smooth = SMOOTHING * (jnp.log(totals) + top - jnp.log(lengths))
    grouped = jnp.sum(smooth.reshape(NQ, QLEN, 128), axis=1, keepdims=True)
    scores = LOGIT_SCALE * grouped
    scores = jnp.where(lane[None] < NP, scores, NEG)
    score_max = jnp.max(scores, axis=2, keepdims=True)
    score_exp = jnp.exp(scores - score_max)
    score_total = jnp.sum(score_exp, axis=2, keepdims=True)
    query = lax.broadcasted_iota(jnp.int32, (NQ, 1, 128), 0)
    chosen = jnp.zeros((NQ, 1, 128), jnp.int32)
    for i in range(NQ):
        chosen = jnp.where(query == i, info[1 + micros * NP + micro * NQ + i], chosen)
    onehot = (chosen == lane[None]).astype(F32)
    own_score = jnp.sum(jnp.where(chosen == lane[None], scores, 0.0), axis=2, keepdims=True)
    losses = jnp.log(score_total) + score_max - own_score
    loss = jnp.sum(losses, axis=0)
    grad_scores = (score_exp / score_total - onehot) * grad_scale
    grad_smooth = jnp.broadcast_to(LOGIT_SCALE * grad_scores, (NQ, QLEN, 128)).reshape(QROWS, 128)
    share = grad_smooth / totals
    weight = jnp.zeros((QROWS, PSLOTS), F32)
    for j in range(NP):
        weight = jnp.where(owner == j, share[:, j : j + 1], weight)
    grad_similar = jnp.where(owner < NP, terms * weight, 0.0).astype(BF)
    grad_unit = jnp.concatenate([dot_nn(grad_similar, passages), dot_tn(grad_similar, queries)])
    grad_embed = inv_norm * (grad_unit - unit * jnp.sum(grad_unit * unit, axis=1, keepdims=True))
    return loss, grad_embed.astype(BF)


def ffn_bwd_live(j, count, with_loss, micros, grad_scale, micro, info, *refs):
    if with_loss:
        out_all, wc = refs[:2]
    else:
        rec = refs[0]
    n2, inv2, gain2, slope, wr, we, n1, inv1, gain1 = refs[2 if with_loss else 1 :][:9]
    two_out, inner_out, one_out, emb_out, small_out, ff_out, acc, resid = refs[-8:]

    @pl.when(j == 0)
    def _():
        small_out[...] = jnp.zeros(small_out.shape, F32)
        if with_loss:
            loss, grad_embed = loss_parts(info, micro, micros, grad_scale, out_all[...], wc[...])
            emb_out[...] = grad_embed
            upstream = dot_nt(grad_embed, wc[...])
            small_out[6:7, 0:128] = jnp.broadcast_to(loss, (1, 128))
        else:
            upstream = rec[...].astype(F32)
        acc[...] = jnp.zeros(acc.shape, F32)
        n = n2[...].astype(F32)
        small_out[0:1, :] = column_sum(upstream * n)
        small_out[1:2, :] = column_sum(upstream)
        d_two = norm_rows_back(upstream, n, inv2[...], gain2[...])
        resid[...] = d_two
        d_two_b = d_two.astype(BF)
        two_out[...] = d_two_b
        small_out[2:3, :] = column_sum(d_two_b.astype(F32))

    d_act = dot_nt(two_out[...], wr[...])
    d_inner = (d_act * slope[...].astype(F32)).astype(BF)
    inner_out[...] = d_inner
    ff_out[0:1, :] = column_sum(d_inner.astype(F32))
    acc[...] += dot_nt(d_inner, we[...])

    @pl.when(j == count - 1)
    def _():
        upstream = resid[...] + acc[...]
        n = n1[...].astype(F32)
        small_out[3:4, :] = column_sum(upstream * n)
        small_out[4:5, :] = column_sum(upstream)
        d_one = norm_rows_back(upstream, n, inv1[...], gain1[...])
        resid[...] = d_one
        d_one_b = d_one.astype(BF)
        one_out[...] = d_one_b
        small_out[5:6, :] = column_sum(d_one_b.astype(F32))


def ffn_bwd_parts(section, micro, micros, received, kept, weights, step):
    (out_all, n2, inv2, slope, n1, inv1) = kept
    (wc, gains, wr, we) = weights
    slots, rows, width = out_all.shape
    ff = we.shape[1]
    slot = lambda i: slot_of(i, section, micro, micros)
    at = lambda g, i: step_of(i, section, step(g))
    one = lambda *shape: pl.BlockSpec(shape, lambda g, i: (0,) * len(shape))
    at_slot = lambda *shape: pl.BlockSpec((None,) + shape, lambda g, i: (slot(i), 0, 0))
    if section == 1:
        in_specs = [at_slot(rows, width), one(*wc.shape)]
        args = [out_all, wc]
    else:
        in_specs = [one(rows, width)]
        args = [received]
    in_specs += [
        at_slot(rows, width),
        at_slot(rows, 1),
        one(1, width),
        pl.BlockSpec((None, rows, FFBLOCK), lambda g, i: (slot(i), 0, at(g, i))),
        pl.BlockSpec((FFBLOCK, width), lambda g, i: (at(g, i), 0)),
        pl.BlockSpec((width, FFBLOCK), lambda g, i: (0, at(g, i))),
        at_slot(rows, width),
        at_slot(rows, 1),
        one(1, width),
    ]
    args += [n2, inv2, gains[1:2], slope, wr, we, n1, inv1, gains[0:1]]
    rows_at = lambda shape, kind: ((slots,) + shape, kind, (None,) + shape, lambda g, i: (slot(i), 0, 0))
    shapes = [
        rows_at((rows, width), BF),
        ((slots, rows, ff), BF, (None, rows, FFBLOCK), lambda g, i: (slot(i), 0, at(g, i))),
        rows_at((rows, width), BF),
        rows_at((rows, wc.shape[1]), BF),
        rows_at((8, width), F32),
        ((slots, 8, ff), F32, (None, 8, FFBLOCK), lambda g, i: (slot(i), 0, at(g, i))),
    ]
    return in_specs, args, shapes, [pltpu.VMEM((rows, width), F32), pltpu.VMEM((rows, width), F32)]


def ffn_backward(phase, micros, grad_scale, info, received, kept, weights, old):
    section, micro = 1 - phase // micros, phase % micros
    in_specs, args, shapes, scratch = ffn_bwd_parts(section, micro, micros, received, kept, weights, lambda g: g)
    steps = weights[3].shape[1] // FFBLOCK

    def body(micro, info, *refs):
        ffn_bwd_live(pl.program_id(0), steps, section == 1, micros, grad_scale, micro, info, *refs)

    return call(
        live_only(body, section, micro), steps, info, args, in_specs, shapes, old, scratch, flops=FLOPS_FFN
    )


def attn_bwd_live(g, count, with_send, micro, info, one_b, joined, lse, ctx, wm, *rest):
    qcode, kcode, dctx, delta, ktr, dqtr = rest[-6:]
    if with_send:
        wq, wk, wv, resid, acc = rest[:5]
        dq_out, dk_out, dv_out, sum_out, send_out = rest[-11:-6]
    else:
        dq_out, dk_out, dv_out, sum_out = rest[-10:-6]

    @pl.when(g == 0)
    def _():
        fill_codes(info, micro, qcode, kcode)
        if with_send:
            acc[...] = jnp.zeros(acc.shape, F32)

    dctx32 = dot_nt(one_b[...], wm[...])
    dctx[...] = dctx32.astype(BF)
    along = dctx[...].astype(F32) * ctx[...].astype(F32)
    pick = lax.broadcasted_iota(jnp.int32, (8, SLAB), 0) == lax.broadcasted_iota(jnp.int32, (8, SLAB), 1) // HEAD_DIM
    delta[...] = lax.dot_general(
        pick.astype(F32), along, (((1,), (1,)), ((), ())),
        precision=lax.Precision.HIGHEST, preferred_element_type=F32,
    )
    ktr[...] = jnp.transpose(joined[:, SLAB : 2 * SLAB])
    rows = one_b.shape[0]
    parts = (slice(0, QROWS), slice(QROWS, rows))
    for pair in range(SLAB // 128):
        lo = pair * 128
        qs = joined[:, lo : lo + 128] * BF(HEAD_DIM**-0.5)
        ks = joined[:, SLAB + lo : SLAB + lo + 128]
        vs = joined[:, 2 * SLAB + lo : 2 * SLAB + lo + 128]
        do = dctx[:, lo : lo + 128]
        qms = [head_lanes(qs, h, jnp.zeros_like(qs)) for h in range(2)]
        dms = [head_lanes(do, h, jnp.zeros_like(do)) for h in range(2)]
        ps, dss = ([], []), ([], [])
        for h in range(2):
            head = pair * 2 + h
            hh = slice(head * HEAD_DIM, head * HEAD_DIM + HEAD_DIM)
            qh = head_lanes(qs, h, qcode[...])
            kh = head_lanes(ks, h, kcode[...])
            for i, at in enumerate(parts):
                p = jnp.exp(dot_nt(kh[at], qh[at]) - lse[head : head + 1, at])
                dp = dot_nt(vs[at], dms[h][at])
                ds = (p * (dp - delta[head : head + 1, at])).astype(BF)
                ps[i].append(p.astype(BF))
                dss[i].append(ds)
                dqtr[hh, at] = dot_nn(ktr[hh, at], ds)
        for i, at in enumerate(parts):
            q_heads = jnp.concatenate([qm[at] for qm in qms])
            d_heads = jnp.concatenate([dm[at] for dm in dms])
            dk_out[at, lo : lo + 128] = dot_nn(jnp.concatenate(dss[i], axis=1), q_heads).astype(BF)
            dv_out[at, lo : lo + 128] = dot_nn(jnp.concatenate(ps[i], axis=1), d_heads).astype(BF)
    dq = (jnp.transpose(dqtr[...]) * HEAD_DIM**-0.5).astype(BF)
    dq_out[...] = dq
    dk = dk_out[...]
    dv = dv_out[...]
    sum_out[0:1, 0:SLAB] = column_sum(dq.astype(F32))
    sum_out[0:1, SLAB : 2 * SLAB] = column_sum(dv.astype(F32))
    if not with_send:
        return
    acc[...] += dot_nt(
        jnp.concatenate([dq, dk, dv], axis=1), jnp.concatenate([wq[...], wk[...], wv[...]], axis=1)
    )

    @pl.when(g == count - 1)
    def _():
        send_out[...] = (resid[...] + acc[...]).astype(BF)


def attn_bwd_parts(section, micro, micros, shape, kept, weights, step):
    (joined, lse, ctx) = kept
    (wa, wm) = weights
    slots, rows, width = shape
    count = width // SLAB
    slot = lambda i: slot_of(i, section, micro, micros)
    at = lambda g, i: step_of(i, section, step(g))
    in_specs = [
        pl.BlockSpec((None, None, rows, 3 * SLAB), lambda g, i: (slot(i), at(g, i), 0, 0)),
        pl.BlockSpec((None, None, 8, rows), lambda g, i: (slot(i), at(g, i), 0, 0)),
        pl.BlockSpec((None, rows, SLAB), lambda g, i: (slot(i), 0, at(g, i))),
        pl.BlockSpec((SLAB, width), lambda g, i: (at(g, i), 0)),
    ]
    args = [joined, lse, ctx, wm]
    slab = ((slots, rows, width), BF, (None, rows, SLAB), lambda g, i: (slot(i), 0, at(g, i)))
    shapes = [
        slab,
        slab,
        slab,
        ((slots, count, 8, 2 * SLAB), F32, (None, None, 8, 2 * SLAB), lambda g, i: (slot(i), at(g, i), 0, 0)),
    ]
    scratch = [
        pltpu.VMEM((rows, 128), BF),
        pltpu.VMEM((rows, 128), BF),
        pltpu.VMEM((rows, SLAB), BF),
        pltpu.VMEM((8, rows), F32),
        pltpu.VMEM((SLAB, rows), BF),
        pltpu.VMEM((SLAB, rows), F32),
    ]
    return in_specs, args, shapes, scratch


def attn_backward(phase, micros, info, one_all, kept, weights, old, slabs):
    section, micro = 1 - phase // micros, phase % micros
    slots, rows, width = one_all.shape
    in_specs, args, shapes, scratch = attn_bwd_parts(
        section, micro, micros, one_all.shape, kept, weights, lambda g: slabs[0] + g
    )
    in_specs = [pl.BlockSpec((None, rows, width), lambda g, i: (slot_of(i, section, micro, micros), 0, 0))] + in_specs

    def body(micro, info, *refs):
        attn_bwd_live(pl.program_id(0), len(slabs), False, micro, info, *refs)

    return call(
        live_only(body, section, micro), len(slabs), info, [one_all] + args, in_specs, shapes, old, scratch,
        flops=FLOPS_ATTN * len(slabs) * SLAB // width // 32, limit=SLAB_VMEM,
    )


def layer_backward(phase, micros, grad_scale, info, received, ffn_kept, attn_kept, weights, old):
    (wc, gains, wr, we, wa, wm) = weights
    section, micro = 1 - phase // micros, phase % micros
    shape = ffn_kept[0].shape
    _, rows, width = shape
    first, second = we.shape[1] // FFBLOCK, width // SLAB
    in_specs, args, shapes, scratch = ffn_bwd_parts(
        section, micro, micros, received, ffn_kept, (wc, gains, wr, we), lambda g: jnp.minimum(g, first - 1)
    )
    step = lambda g: jnp.maximum(g - first, 0)
    more = attn_bwd_parts(section, micro, micros, shape, attn_kept, (wa, wm), step)
    count = len(args)
    in_specs, args, shapes, scratch = in_specs + more[0], args + more[1], shapes + more[2], scratch + more[3]
    sends = section == 1
    if sends:
        at = lambda g, i: step_of(i, section, step(g))
        in_specs += [
            pl.BlockSpec((width, SLAB), lambda g, i, k=k: (0, k * second + at(g, i))) for k in range(3)
        ]
        args += [wa, wa, wa]
        shapes += [((rows, width), BF, (rows, width), lambda g, i: (0, 0))]

    def body(micro, info, *refs):
        ffn_in, attn_in = refs[:count], refs[count : count + 4]
        ins_q = refs[count + 4 : count + 7]
        inner = refs[-6:]
        acc, resid = refs[-8:-6]
        ends = 11 if sends else 10
        outs = refs[-8 - ends : -8]
        g = pl.program_id(0)

        @pl.when(g < first)
        def _():
            ffn_bwd_live(g, first, sends, micros, grad_scale, micro, info, *ffn_in, *outs[:6], acc, resid)

        @pl.when(g >= first)
        def _():
            extra = ins_q + (resid, acc) if sends else ()
            attn_bwd_live(g - first, second, sends, micro, info, outs[2], *attn_in, *extra, *outs[6:], *inner)

    return call(
        live_only(body, section, micro), first + second, info, args, in_specs, shapes, old, scratch,
        flops=FLOPS_FFN + FLOPS_ATTN,
    )


def mesh_bits():
    place = lax.axis_index("dp")
    bits = []
    bit = 1
    while bit < lax.axis_size("dp"):
        bits.append((bit, (place // bit) % 2))
        bit *= 2
    return bits


def grad_call(body, steps, core, in_specs, args, out_shape, out_specs, flops, limit=VMEM_LIMIT):
    return pl.pallas_call(
        body,
        out_shape=out_shape,
        grid_spec=pltpu.PrefetchScalarGridSpec(
            num_scalar_prefetch=1,
            grid=(steps,),
            in_specs=in_specs,
            out_specs=out_specs,
        ),
        compiler_params=pltpu.CompilerParams(vmem_limit_bytes=limit),
        cost_estimate=pl.CostEstimate(flops=flops // 16, bytes_accessed=100_000, transcendentals=0),
    )(core, *args)


def grad_half_body(info, left, right, *refs):
    total = dot_nn(jnp.transpose(left[...]), right[...])
    if len(refs) > 1:
        total = total + refs[0][...].astype(F32)
    refs[-1][...] = total.astype(BF)


def grad_half(rows, micro, core, mine, left, right, base):
    tall, wide = left.shape[1] // 2, right.shape[1]
    block = wide // GRAD_STEPS
    spec = pl.BlockSpec((tall, block), lambda s, h: (0, s))
    in_specs = [
        pl.BlockSpec((rows, tall), lambda s, h: (micro, h[0] if mine else 1 - h[0])),
        pl.BlockSpec((rows, block), lambda s, h: (micro, s)),
    ]
    args = [left, right]
    if base is not None:
        in_specs += [spec]
        args += [base]
    return grad_call(
        grad_half_body, GRAD_STEPS, core, in_specs, args,
        jax.ShapeDtypeStruct((tall, wide), BF), spec, 2 * rows * tall * wide, VMEM_LIMIT,
    )


def grad_rest_body(with_context, info, inputs, *refs):
    out = refs[-1]
    turned = jnp.transpose(inputs[...])
    parts = []
    if with_context:
        parts.append(dot_nn(jnp.transpose(refs[0][...]), refs[1][...]))
        refs = refs[2:]
    for at in range(0, len(refs) - 3, 3):
        parts.append(dot_nn(turned, jnp.concatenate([right[...] for right in refs[at : at + 3]], axis=1)))
    at = 0
    for part in parts:
        here = slice(at, at + part.shape[1])
        total = part if refs[-2] is None else part + refs[-2][:, here].astype(F32)
        out[:, here] = total.astype(BF)
        at += part.shape[1]


def grad_rest(rows, micro, core, mine, inputs, joined_grads, slabs, context, d_one, base):
    width = inputs.shape[1]
    side = pl.BlockSpec((rows, width // 2), lambda s, h: (micro, h[0] if mine else 1 - h[0]))
    in_specs, args = [side], [inputs]
    columns = 0
    if context is not None:
        in_specs += [side, pl.BlockSpec((rows, width), lambda s, h: (micro, 0))]
        args += [context, d_one]
        columns += width
    for slab in slabs:
        in_specs += [pl.BlockSpec((rows, SLAB), lambda s, h, slab=slab: (micro, slab))] * 3
        args += joined_grads
        columns += 3 * SLAB
    out = jax.ShapeDtypeStruct((width // 2, columns), BF)
    whole = pl.BlockSpec(out.shape, lambda s, h: (0, 0))
    if base is not None:
        in_specs += [whole]
        args += [base]
    body = functools.partial(grad_rest_body, context is not None)
    return grad_call(
        body if base is not None else lambda *refs: body(*refs[:-1], None, refs[-1]), 1, core, in_specs, args,
        out, whole, rows * columns * width,
    )


def widen_body(info, *refs):
    step = pl.program_id(0)
    count = 2 if len(refs) == 6 else 1
    outs = refs[2 * count :]
    for s in range(2):

        @pl.when(step == s)
        def _(s=s):
            parts = [ref[...].astype(F32) for ref in refs[s * count : s * count + count]]
            if count == 1:
                outs[0][...] = parts[0]
                return
            width = outs[1].shape[1]
            outs[1][...] = parts[0][:, :width]
            slabs = [parts[0][:, width:]] + [
                parts[1][:, at : at + 3 * SLAB] for at in range(0, parts[1].shape[1], 3 * SLAB)
            ]
            for g, slab in enumerate(slabs):
                for kind in range(3):
                    at = kind * width + g * SLAB
                    outs[0][:, at : at + SLAB] = slab[:, kind * SLAB : kind * SLAB + SLAB]


def widened(core, own, other, out_shapes):
    return pl.pallas_call(
        widen_body,
        out_shape=[jax.ShapeDtypeStruct(shape, F32) for shape in out_shapes],
        grid_spec=pltpu.PrefetchScalarGridSpec(
            num_scalar_prefetch=1,
            grid=(2,),
            in_specs=[pl.BlockSpec(one.shape, lambda s, h: (0, 0)) for one in own + other],
            out_specs=[
                pl.BlockSpec((shape[0] // 2, shape[1]), lambda s, h: (jnp.where(s == 0, h[0], 1 - h[0]), 0))
                for shape in out_shapes
            ],
        ),
        compiler_params=pltpu.CompilerParams(vmem_limit_bytes=SMALL_VMEM),
        cost_estimate=pl.CostEstimate(flops=0, bytes_accessed=14_000_000, transcendentals=0),
    )(core, *own, *other)


EXCHANGE = (
    "SR", "KR", "SE", "R", "KE", "E", "S0", "PS", "PK", "R", "S1", "E", "P", "R", "S2", "E", "QS", "R", "QK",
    "P", "E", "Q", "R", "P", "E", "V", "Q", "P", "R", "V", "E", "Q", "P", "Q", "Q", "R", "P", "V", "Q", "E",
    "WR", "V", "P", "Q", "WE", "WP",
)
ORDERS = {"R": 0, "E": 1, "P": 1, "Q": 0}
WIDENED = {"WR": ("R",), "WE": ("E",), "WP": ("P", "Q")}
KEEPERS = {"KR": ("R", "SR"), "KE": ("E", "SE"), "PK": ("P", "PS"), "QK": ("Q", "QS")}
KERNELS = ("SR", "KR", "SE", "KE", "S0", "PS", "PK", "S1", "S2", "QS", "QK")


def passed_along(array, axis, by):
    count = lax.axis_size(axis)
    pairs = [(i, i + by) for i in range(count) if 0 <= i + by < count]
    return lax.ppermute(array, axis, pairs)


def tied(array, *others):
    return lax.optimization_barrier((array, *others))[0]


def flatten_rows(leaf):
    return leaf.reshape(-1, leaf.shape[-1])


def swapped(array, bit, axis="dp"):
    count = lax.axis_size(axis)
    return lax.ppermute(array, axis, [(i, i ^ bit) for i in range(count)])


def piece(array, index):
    return lax.dynamic_index_in_dim(array, index, 0, keepdims=False)


def sum_low(kept, got):
    return (kept.astype(F32) + got.astype(F32)).astype(BF)


class Sequence:
    def __init__(self):
        self.last = ()

    def after(self, array):
        return tied(array, *self.last)

    def did(self, *arrays):
        self.last = arrays
        return arrays


class Adder:
    def __init__(self, sequence, value, bits):
        self.sequence, self.value = sequence, value
        self.bits = [step for step, _ in bits]
        self.got = swapped(value, self.bits[0])

    def take(self):
        self.bits.pop(0)
        self.value = sum_low(self.sequence.after(self.value), self.got)
        self.sequence.did(self.value)
        if self.bits:
            self.got = swapped(self.value, self.bits[0])


class Piece:
    def __init__(self, sequence, sent, kept, bits, order):
        self.sequence = sequence
        self.value = kept
        self.steps = [(sum_low, None)]
        self.steps += [(halved, bits[place]) for place in order]
        self.steps += [(doubled, bits[place]) for place in reversed(order)]
        self.got = swapped(sent, 1)

    def send(self):
        if not self.steps:
            self.sequence.did(self.value)
            self.got = swapped(self.value, 1)
            return
        step, (bit, mine) = self.steps[0]
        sent = self.value
        if step is halved:
            sent = piece(sent.reshape(2, sent.shape[0] // 2, sent.shape[1]), 1 - mine)
        self.sequence.did(self.value, sent)
        self.got = swapped(sent, bit)

    def take(self):
        step, bit = self.steps.pop(0)
        value = self.sequence.after(self.value)
        self.value = step(value, self.got) if bit is None else step(value, self.got, bit[1])
        self.send()


def halved(array, got, mine):
    halves = array.reshape(2, array.shape[0] // 2, array.shape[1])
    return sum_low(piece(halves, mine), got)


def doubled(array, got, mine):
    both = jnp.zeros((2,) + array.shape, array.dtype)
    both = lax.dynamic_update_index_in_dim(both, array, mine, 0)
    both = lax.dynamic_update_index_in_dim(both, got, 1 - mine, 0)
    return flatten_rows(both)


def exchange_order(digits):
    if digits == 4:
        return EXCHANGE
    rounds = ("R", "E", "P", "Q") * (2 * digits - 1)
    return KERNELS + rounds + ("V",) * digits + tuple(WIDENED)


def ends_of_pieces(pieces):
    return [one.value for one in pieces], [one.got for one in pieces]


def take(*pieces):
    for one in pieces:
        one.take()


def shards(
    hidden_in,
    attend_weight,
    attend_bias,
    mixing_weight,
    mixing_bias,
    norm_gain,
    norm_shift,
    expand_weight,
    expand_bias,
    reduce_weight,
    reduce_bias,
    colbert_weight,
    pass_lengths,
    positives,
):
    section_id = lax.axis_index("pipe")
    data_count = lax.axis_size("dp")
    micros = pass_lengths.shape[0]
    rows = hidden_in.shape[0] // micros
    width = hidden_in.shape[1]
    grad_scale = 1.0 / (data_count * micros * NQ)
    wa, wm, we, wr = attend_weight[0], mixing_weight[0], expand_weight[0], reduce_weight[0]
    gains, shifts = norm_gain[0], norm_shift[0]
    info = jnp.concatenate(
        [section_id.astype(jnp.int32)[None], pass_lengths.reshape(-1), positives.reshape(-1)]
    )
    bits = mesh_bits()
    core = bits[0][1].astype(jnp.int32)[None]
    along_x_first = list(range(1, len(bits)))
    along_z_first = [2, 1] + list(range(3, len(bits)))
    orders = (along_x_first, along_z_first)
    weights = (wa, attend_bias, wm, mixing_bias, we, expand_bias, wr, reduce_bias, gains, shifts)
    state = {"fwd": None, "bwd": None}
    arriving, returning = {}, {}

    def forward(phase, after=()):
        source = hidden_in if phase < micros else arriving[phase - micros]
        old = state["fwd"]
        state["fwd"] = layer_forward(
            phase, micros, info, tied(source, *after), weights, old and old[:14]
        )
        if phase < micros:
            arriving[phase] = passed_along(state["fwd"][14], "pipe", 1)

    def kept():
        fwd = state["fwd"]
        return (fwd[10], fwd[11], fwd[12], fwd[9], fwd[5], fwd[6]), (fwd[1], fwd[2], fwd[3])

    def arrived(phase, after):
        return None if phase < micros else tied(returning[phase - micros], *after)

    def backward(phase, after=()):
        old = state["bwd"]
        state["bwd"] = layer_backward(
            phase, micros, grad_scale, info, arrived(phase, after), *kept(),
            (colbert_weight, gains, wr, we, wa, wm), old and old[:10],
        )
        if phase < micros:
            returning[phase] = passed_along(state["bwd"][10], "pipe", -1)

    def backward_ffn(phase, after=()):
        made = ffn_backward(
            phase, micros, grad_scale, info, arrived(phase, after), kept()[0],
            (colbert_weight, gains, wr, we), state["bwd"][:6],
        )
        state["bwd"] = list(made) + list(state["bwd"][6:10])

    def backward_attn(phase, after, slabs):
        old = state["bwd"]
        made = attn_backward(
            phase, micros, tied(info, *after), old[2], kept()[1], (wa, wm), old[6:10], slabs
        )
        state["bwd"] = list(old[:6]) + list(made)

    for phase in range(micros):
        forward(phase)
    done = ()
    for phase in range(micros):
        forward(micros + phase, done)
        backward(phase)
        done = (state["bwd"][9],)
    fwd = state["fwd"]
    inputs, context, hidden, squares_one = fwd[0], fwd[3], fwd[4], fwd[7]
    active, outputs, squares_two = fwd[8], fwd[10], fwd[13]
    embeds, losses = state["bwd"][3:5]
    squares = jnp.stack(
        [
            jnp.sum(squares_one[:micros, 0], axis=1),
            jnp.sum(squares_one[:micros, 1], axis=1),
            jnp.sum(squares_two[:micros, 0], axis=1),
        ],
        axis=1,
    )
    colbert = dot_tn(flatten_rows(outputs[:micros]), flatten_rows(embeds[:micros])).astype(BF)
    facts = jnp.concatenate([squares, losses[:micros, 6, 0:1]], axis=1)
    facts_down, colbert_down = passed_along(facts, "pipe", -1), passed_along(colbert, "pipe", -1)
    done += (facts, colbert)
    for phase in range(micros, 2 * micros - 1):
        backward(phase, done)
        done = (state["bwd"][9],)
    last = 2 * micros - 1
    after_back = state["bwd"][9]
    slabs = tuple(range(width // SLAB))
    ffn_back, attn_back = state["bwd"][:6], state["bwd"][6:10]
    lefts = [flatten_rows(a) for a in (active, hidden, inputs, context)]

    bases = {}
    for micro in range(micros - 1):
        first_core = tied(core, after_back)
        d_two, d_inner, d_one = (flatten_rows(ffn_back[i]) for i in range(3))
        joined_grads = [flatten_rows(a) for a in attn_back[:3]]
        for mine in (0, 1):
            old = bases.get(mine, (None,) * 4)
            bases[mine] = (
                grad_half(rows, micro, first_core, mine, lefts[0], d_two, old[0]),
                grad_half(rows, micro, first_core, mine, lefts[1], d_inner, old[1]),
                grad_rest(rows, micro, first_core, mine, lefts[2], joined_grads, slabs[:1], lefts[3], d_one, old[2]),
                grad_rest(rows, micro, first_core, mine, lefts[2], joined_grads, slabs[1:], None, None, old[3]),
            )
    backward_ffn(last, (facts_down, colbert_down) + tuple(jax.tree.leaves(bases)))
    bases = bases or {0: (None,) * 4, 1: (None,) * 4}
    micro = micros - 1
    ffn_back = state["bwd"]
    d_two, d_inner, d_one = (flatten_rows(ffn_back[i]) for i in range(3))
    line = Sequence()

    def half_of(mine, left, right, which):
        [one] = line.did(grad_half(rows, micro, line.after(core), mine, left, right, bases[mine][which]))
        return one

    def rest_half(mine, some, which):
        joined_grads = [flatten_rows(a) for a in state["bwd"][6:9]]
        extra = (lefts[3], d_one) if which == 2 else (None, None)
        [one] = line.did(
            grad_rest(rows, micro, line.after(core), mine, lefts[2], joined_grads, some, *extra, bases[mine][which])
        )
        return one

    def slab_back(slab):
        backward_attn(last, line.last, (slab,))
        line.did(*state["bwd"][6:10])

    made, pieces, widths = {}, {}, {}

    def run_kernel(name):
        made[name] = {
            "SR": lambda: half_of(0, lefts[0], d_two, 0),
            "KR": lambda: half_of(1, lefts[0], d_two, 0),
            "SE": lambda: half_of(0, lefts[1], d_inner, 1),
            "KE": lambda: half_of(1, lefts[1], d_inner, 1),
            "PS": lambda: rest_half(0, slabs[:1], 2),
            "PK": lambda: rest_half(1, slabs[:1], 2),
            "QS": lambda: rest_half(0, slabs[1:], 3),
            "QK": lambda: rest_half(1, slabs[1:], 3),
            "S0": lambda: slab_back(slabs[0]),
            "S1": lambda: slab_back(slabs[1]),
            "S2": lambda: [slab_back(slab) for slab in slabs[2:]],
        }[name]()

    def small_sums():
        small, small_ff, joined_sums = ffn_back[4], ffn_back[5], state["bwd"][9]
        small_sum = jnp.sum(small[:micros], axis=0)
        joined_sum = jnp.sum(joined_sums[:micros, :, 0], axis=0)
        attend_sum = jnp.concatenate(
            [joined_sum[:, :SLAB].reshape(-1), joined_sum[:, SLAB:].reshape(-1)]
        )
        of_colbert = jnp.where(section_id == 1, colbert, colbert_down)
        parts = [
            small_sum[:6],
            attend_sum.reshape(2, width),
            jnp.sum(small_ff[:micros, 0], axis=0).reshape(-1, width),
            of_colbert.astype(F32).reshape(-1, width),
        ]
        return jnp.concatenate(parts).astype(BF)

    for step in exchange_order(len(bits)):
        if step == "V" and step not in pieces:
            pieces[step] = Adder(line, small_sums(), bits)
        if step in pieces:
            pieces[step].take()
        elif step[0] == "W":
            if step == "WE":
                made["up"] = passed_along(line.after(facts), "pipe", 1)
            widths[step] = widened(
                line.after(core), *ends_of_pieces([pieces[one] for one in WIDENED[step]]),
                {"WR": [wr.shape], "WE": [we.shape], "WP": [wa.shape, wm.shape]}[step],
            )
            line.did(*widths[step])
        else:
            run_kernel(step)
            if step in KEEPERS:
                name, send = KEEPERS[step]
                pieces[name] = Piece(line, made[send], made[step], bits, orders[ORDERS[name]])
    first = jnp.where(section_id == 0, facts, made["up"])
    second = jnp.where(section_id == 0, facts_down, facts)
    [big_reduce], [big_expand], (big_attend, big_mixing) = (widths[one] for one in ("WR", "WE", "WP"))
    vector = pieces["V"].value
    vector = vector.astype(F32)
    colbert_sum = vector[8 + we.shape[1] // width :].reshape(colbert_weight.shape)
    counted = (QROWS + jnp.sum(pass_lengths, axis=1)).astype(F32)
    stats = jnp.stack([first[:, :3], second[:, :3]], axis=1)
    stats = jnp.sqrt(stats / (counted[:, None, None] * width))
    return (
        big_attend[None],
        vector[6:8].reshape(1, -1),
        big_mixing[None],
        vector[5][None],
        jnp.stack([vector[3], vector[0]])[None],
        jnp.stack([vector[4], vector[1]])[None],
        big_expand[None],
        vector[8 : 8 + we.shape[1] // width].reshape(1, -1),
        big_reduce[None],
        vector[2][None],
        colbert_sum,
        second[:, 3] / NQ,
        stats,
    )


def solution(mesh):
    placed = (
        P("dp", None),
        P("pipe", None, None),
        P("pipe", None),
        P("pipe", None, None),
        P("pipe", None),
        P("pipe", None, None),
        P("pipe", None, None),
        P("pipe", None, None),
        P("pipe", None),
        P("pipe", None, None),
        P("pipe", None),
        P(),
        P("dp", None),
        P("dp", None),
    )
    return jax.shard_map(
        shards,
        mesh=mesh,
        in_specs=placed,
        out_specs=(
            P("pipe", None, None),
            P("pipe", None),
            P("pipe", None, None),
            P("pipe", None),
            P("pipe", None, None),
            P("pipe", None, None),
            P("pipe", None, None),
            P("pipe", None),
            P("pipe", None, None),
            P("pipe", None),
            P(),
            P("dp"),
            P("dp", None, None),
        ),
        check_vma=False,
    )
```

```python
import functools
import jax
import jax.numpy as jnp
from jax import lax
from jax.experimental import pallas as pl
from jax.experimental.pallas import tpu as pltpu
from jax.sharding import PartitionSpec as P

HEAD_DIM = 64
QLEN = 32
NQ = 4
NP = 4
PSLOTS = 512
LAYER_EPSILON = 1e-12
UNIT_EPSILON = 1e-06
SMOOTHING = 0.05
LOGIT_SCALE = 4.0
ROOT_HALF = 0.7071067811865476
NORMAL_PEAK = 0.3989422804014327
BF = jnp.bfloat16
F32 = jnp.float32
QROWS = NQ * QLEN
SLAB = 256
FFBLOCK = 1536
VMEM_LIMIT = 56 * 1024 * 1024
NEG = -1e30
GRAD_STEPS = 2
SMALL_VMEM = 26 * 1024 * 1024
SLAB_VMEM = VMEM_LIMIT
FLOPS_FFN = 12_000_000_000
FLOPS_ATTN = 20_000_000_000


def dot_nn(a, b):
    return jnp.dot(a, b, preferred_element_type=F32)


def dot_nt(a, b):
    return lax.dot_general(a, b, (((1,), (1,)), ((), ())), preferred_element_type=F32)


def dot_tn(a, b):
    return lax.dot_general(a, b, (((0,), (0,)), ((), ())), preferred_element_type=F32)


def gelu_pair(u):
    phi = 0.5 + 0.5 * lax.erf(u * ROOT_HALF)
    return u * phi, phi + NORMAL_PEAK * u * jnp.exp(-0.5 * u * u)


def norm_rows(resid):
    centre = resid - jnp.mean(resid, axis=1, keepdims=True)
    inv = lax.rsqrt(jnp.mean(centre * centre, axis=1, keepdims=True) + LAYER_EPSILON)
    return centre * inv, inv


def ends_of(info, micro):
    base = 1 + micro * NP
    ends = []
    total = jnp.int32(0)
    for j in range(NP):
        total = total + info[base + j]
        ends.append(total)
    return ends


def passage_of(place, ends):
    out = jnp.zeros(place.shape, jnp.int32)
    for end in ends:
        out = out + jnp.where(place >= end, 1, 0)
    return out


def when_live(info, section, body):
    pl.when(info[0] == section)(body)


def slot_of(info, section, micro, spare):
    return jnp.where(info[0] == section, micro, spare)


def step_of(info, section, step):
    return jnp.where(info[0] == section, step, 0)


def fill_codes(info, micro, query_code, key_code):
    rows = query_code.shape[0]
    ends = [QROWS + end for end in ends_of(info, micro)]
    place = lax.broadcasted_iota(jnp.int32, (rows, 1), 0)
    segment = jnp.where(place < QROWS, place // QLEN, NQ + passage_of(place, ends))
    lane = lax.broadcasted_iota(jnp.int32, (1, 128), 1) % HEAD_DIM
    query_code[...] = jnp.where(segment == lane, 1.0, 0.0).astype(BF)
    key_code[...] = jnp.where((segment == lane) | (lane > NQ + NP), 0.0, NEG).astype(BF)


def usable_rows(info, micro, rows):
    ends = ends_of(info, micro)
    place = lax.broadcasted_iota(jnp.int32, (rows, 1), 0)
    return (place < QROWS + ends[-1]).astype(F32)


def head_lanes(value, h, others):
    lane = lax.broadcasted_iota(jnp.int32, (1, 128), 1) // HEAD_DIM
    return jnp.where(lane == h, value, others)


def live_only(body, section, micro):
    def kernel(info, *refs):
        when_live(info, section, lambda: body(micro, info, *refs))

    return kernel


def attn_fwd_live(g, count, micro, info, hid, wq, wk, wv, bq, bv, wm, bm, gain, shift, *rest):
    x_out, joined_out, lse_out, ctx_out, hid_out, n_out, inv_out, sq_out, acc, qcode, kcode, otr, vtr = rest
    rows = hid.shape[0]

    @pl.when(g == 0)
    def _():
        x_out[...] = hid[...]
        fill_codes(info, micro, qcode, kcode)
        acc[...] = jnp.zeros(acc.shape, F32)

    x = hid[...]
    qkv = dot_nn(x, jnp.concatenate([wq[...], wk[...], wv[...]], axis=1))
    q = (qkv[:, :SLAB] + bq[...]).astype(BF)
    joined_out[:, 0:SLAB] = q
    k = qkv[:, SLAB : 2 * SLAB].astype(BF)
    joined_out[:, SLAB : 2 * SLAB] = k
    v = (qkv[:, 2 * SLAB :] + bv[...]).astype(BF)
    joined_out[:, 2 * SLAB : 3 * SLAB] = v
    vtr[...] = jnp.transpose(v)
    parts = (slice(0, QROWS), slice(QROWS, rows))
    for pair in range(SLAB // 128):
        cols = slice(pair * 128, pair * 128 + 128)
        qs = joined_out[:, cols] * BF(HEAD_DIM**-0.5)
        ks = joined_out[:, SLAB + pair * 128 : SLAB + pair * 128 + 128]
        for h in range(2):
            head = pair * 2 + h
            vh = slice(head * HEAD_DIM, head * HEAD_DIM + HEAD_DIM)
            qh = head_lanes(qs, h, qcode[...])
            kh = head_lanes(ks, h, kcode[...])
            for at in parts:
                st = dot_nt(kh[at], qh[at])
                top = jnp.max(st, axis=0, keepdims=True)
                p = jnp.exp(st - top)
                total = jnp.sum(p, axis=0, keepdims=True)
                lse_out[head : head + 1, at] = top + jnp.log(total)
                otr[vh, at] = dot_nn(vtr[vh, at], p.astype(BF)) * (1.0 / total)
    ctx = jnp.transpose(otr[...]).astype(BF)
    ctx_out[...] = ctx
    acc[...] += dot_nn(ctx, wm[...])

    @pl.when(g == count - 1)
    def _():
        b1 = acc[...] + bm[...]
        x32 = hid[...].astype(F32)
        n, inv = norm_rows(x32 + b1)
        hid_out[...] = (n * gain[...] + shift[...]).astype(BF)
        n_out[...] = n.astype(BF)
        inv_out[...] = inv
        mask = usable_rows(info, micro, rows)
        sq_out[0:1, :] = jnp.sum(mask * x32 * x32, axis=0, keepdims=True)
        sq_out[1:2, :] = jnp.sum(mask * b1 * b1, axis=0, keepdims=True)


def call(body, steps, info, args, in_specs, shapes, old, scratch, flops, limit=VMEM_LIMIT):
    aliases = {}
    if old is not None:
        in_specs = in_specs + [pl.BlockSpec(memory_space=pl.ANY)] * len(old)
        aliases = {1 + len(args) + i: i for i in range(len(old))}
        args = args + list(old)
    return pl.pallas_call(
        body,
        out_shape=[jax.ShapeDtypeStruct(s[0], s[1]) for s in shapes],
        grid_spec=pltpu.PrefetchScalarGridSpec(
            num_scalar_prefetch=1,
            grid=(steps,),
            in_specs=in_specs,
            out_specs=[pl.BlockSpec(s[2], s[3]) for s in shapes],
            scratch_shapes=scratch,
        ),
        input_output_aliases=aliases,
        compiler_params=pltpu.CompilerParams(
            dimension_semantics=("arbitrary",), vmem_limit_bytes=limit
        ),
        cost_estimate=pl.CostEstimate(flops=flops, bytes_accessed=min(20_000_000, flops // 600), transcendentals=0),
    )(info, *args)


def ffn_fwd_live(j, count, micro, info, hid, we, be, wr, br, gain, shift, *rest):
    act_out, slope_out, out_all, n_out, inv_out, sq_out, send_out, acc = rest
    rows = hid.shape[0]

    @pl.when(j == 0)
    def _():
        acc[...] = jnp.zeros(acc.shape, F32)

    inner = dot_nn(hid[...], we[...]) + be[...]
    active, slope = gelu_pair(inner)
    active = active.astype(BF)
    act_out[...] = active
    slope_out[...] = slope.astype(BF)
    acc[...] += dot_nn(active, wr[...])

    @pl.when(j == count - 1)
    def _():
        b2 = acc[...] + br[...]
        n, inv = norm_rows(hid[...].astype(F32) + b2)
        out = (n * gain[...] + shift[...]).astype(BF)
        out_all[...] = out
        send_out[...] = out
        n_out[...] = n.astype(BF)
        inv_out[...] = inv
        mask = usable_rows(info, micro, rows)
        sq_out[0:1, :] = jnp.sum(mask * b2 * b2, axis=0, keepdims=True)


def layer_fwd_live(first, second, micro, info, *refs):
    attn_in, ffn_in = refs[:10], refs[10:16]
    attn_out, ffn_out = refs[-20:-12], refs[-12:-5]
    acc, qcode, kcode, otr, vtr = refs[-5:]
    g = pl.program_id(0)

    @pl.when(g < first)
    def _():
        attn_fwd_live(g, first, micro, info, *attn_in, *attn_out, acc, qcode, kcode, otr, vtr)

    @pl.when(g >= first)
    def _():
        ffn_fwd_live(g - first, second, micro, info, attn_out[4], *ffn_in, *ffn_out, acc)


def layer_forward(phase, micros, info, source, weights, old):
    (wa, ba, wm, bm, we, be, wr, br, gains, shifts) = weights
    section, micro = phase // micros, phase % micros
    width, ff = we.shape
    rows = source.shape[0] // micros if section == 0 else source.shape[0]
    place = micro if section == 0 else 0
    first, second = width // SLAB, ff // FFBLOCK
    slot = lambda i: slot_of(i, section, micro, micros)
    at = lambda g, i: step_of(i, section, jnp.minimum(g, first - 1))
    on = lambda g, i: step_of(i, section, jnp.maximum(g - first, 0))
    one = lambda *shape: pl.BlockSpec(shape, lambda g, i: (0,) * len(shape))
    in_specs = [
        pl.BlockSpec((rows, width), lambda g, i: (place, 0)),
        pl.BlockSpec((width, SLAB), lambda g, i: (0, at(g, i))),
        pl.BlockSpec((width, SLAB), lambda g, i: (0, first + at(g, i))),
        pl.BlockSpec((width, SLAB), lambda g, i: (0, 2 * first + at(g, i))),
        pl.BlockSpec((1, SLAB), lambda g, i: (0, at(g, i))),
        pl.BlockSpec((1, SLAB), lambda g, i: (0, first + at(g, i))),
        pl.BlockSpec((SLAB, width), lambda g, i: (at(g, i), 0)),
        one(1, width),
        one(1, width),
        one(1, width),
        pl.BlockSpec((width, FFBLOCK), lambda g, i: (0, on(g, i))),
        pl.BlockSpec((1, FFBLOCK), lambda g, i: (0, on(g, i))),
        pl.BlockSpec((FFBLOCK, width), lambda g, i: (on(g, i), 0)),
        one(1, width),
        one(1, width),
        one(1, width),
    ]
    args = [source, wa, wa, wa, ba, ba, wm, bm, gains[0:1], shifts[0:1]]
    args += [we, be, wr, br, gains[1:2], shifts[1:2]]
    slots = micros + 1
    rows_at = lambda shape, kind: ((slots,) + shape, kind, (None,) + shape, lambda g, i: (slot(i), 0, 0))
    wide = ((slots, rows, ff), BF, (None, rows, FFBLOCK), lambda g, i: (slot(i), 0, on(g, i)))
    shapes = [
        rows_at((rows, width), BF),
        ((slots, first, rows, 3 * SLAB), BF, (None, None, rows, 3 * SLAB), lambda g, i: (slot(i), at(g, i), 0, 0)),
        ((slots, first, 8, rows), F32, (None, None, 8, rows), lambda g, i: (slot(i), at(g, i), 0, 0)),
        ((slots, rows, width), BF, (None, rows, SLAB), lambda g, i: (slot(i), 0, at(g, i))),
        rows_at((rows, width), BF),
        rows_at((rows, width), BF),
        rows_at((rows, 1), F32),
        rows_at((8, width), F32),
        wide,
        wide,
        rows_at((rows, width), BF),
        rows_at((rows, width), BF),
        rows_at((rows, 1), F32),
        rows_at((8, width), F32),
        ((rows, width), BF, (rows, width), lambda g, i: (0, 0)),
    ]
    return call(
        live_only(functools.partial(layer_fwd_live, first, second), section, micro),
        first + second, info, args, in_specs, shapes, old,
        [
            pltpu.VMEM((rows, width), F32),
            pltpu.VMEM((rows, 128), BF),
            pltpu.VMEM((rows, 128), BF),
            pltpu.VMEM((SLAB, rows), F32),
            pltpu.VMEM((SLAB, rows), BF),
        ],
        flops=FLOPS_FFN + FLOPS_ATTN,
    )


def column_sum(value):
    return jnp.sum(value, axis=0, keepdims=True)


def norm_rows_back(grad_out, n, inv, gain):
    grad_unit = grad_out * gain
    mean_grad = jnp.mean(grad_unit, axis=1, keepdims=True)
    mean_along = jnp.mean(grad_unit * n, axis=1, keepdims=True)
    return inv * (grad_unit - mean_grad - n * mean_along)


def loss_parts(info, micro, micros, grad_scale, out_b, wc):
    ends = ends_of(info, micro)
    embedded = dot_nn(out_b, wc)
    inv_norm = lax.rsqrt(jnp.sum(embedded * embedded, axis=1, keepdims=True) + UNIT_EPSILON)
    unit = embedded * inv_norm
    unit_b = unit.astype(BF)
    queries, passages = unit_b[:QROWS], unit_b[QROWS:]
    scaled = dot_nt(queries, passages) / SMOOTHING
    owner = passage_of(lax.broadcasted_iota(jnp.int32, (1, PSLOTS), 1), ends)
    top = jnp.max(jnp.where(owner < NP, scaled, NEG), axis=1, keepdims=True)
    terms = jnp.exp(scaled - top)
    lane = lax.broadcasted_iota(jnp.int32, (1, 128), 1)
    totals = jnp.ones((QROWS, 128), F32)
    lengths = jnp.ones((1, 128), F32)
    for j in range(NP):
        total = jnp.sum(jnp.where(owner == j, terms, 0.0), axis=1, keepdims=True)
        totals = jnp.where(lane == j, total, totals)
        lengths = jnp.where(lane == j, info[1 + micro * NP + j].astype(F32), lengths)
    smooth = SMOOTHING * (jnp.log(totals) + top - jnp.log(lengths))
    grouped = jnp.sum(smooth.reshape(NQ, QLEN, 128), axis=1, keepdims=True)
    scores = LOGIT_SCALE * grouped
    scores = jnp.where(lane[None] < NP, scores, NEG)
    score_max = jnp.max(scores, axis=2, keepdims=True)
    score_exp = jnp.exp(scores - score_max)
    score_total = jnp.sum(score_exp, axis=2, keepdims=True)
    query = lax.broadcasted_iota(jnp.int32, (NQ, 1, 128), 0)
    chosen = jnp.zeros((NQ, 1, 128), jnp.int32)
    for i in range(NQ):
        chosen = jnp.where(query == i, info[1 + micros * NP + micro * NQ + i], chosen)
    onehot = (chosen == lane[None]).astype(F32)
    own_score = jnp.sum(jnp.where(chosen == lane[None], scores, 0.0), axis=2, keepdims=True)
    losses = jnp.log(score_total) + score_max - own_score
    loss = jnp.sum(losses, axis=0)
    grad_scores = (score_exp / score_total - onehot) * grad_scale
    grad_smooth = jnp.broadcast_to(LOGIT_SCALE * grad_scores, (NQ, QLEN, 128)).reshape(QROWS, 128)
    share = grad_smooth / totals
    weight = jnp.zeros((QROWS, PSLOTS), F32)
    for j in range(NP):
        weight = jnp.where(owner == j, share[:, j : j + 1], weight)
    grad_similar = jnp.where(owner < NP, terms * weight, 0.0).astype(BF)
    grad_unit = jnp.concatenate([dot_nn(grad_similar, passages), dot_tn(grad_similar, queries)])
    grad_embed = inv_norm * (grad_unit - unit * jnp.sum(grad_unit * unit, axis=1, keepdims=True))
    return loss, grad_embed.astype(BF)


def ffn_bwd_live(j, count, with_loss, micros, grad_scale, micro, info, *refs):
    if with_loss:
        out_all, wc = refs[:2]
    else:
        rec = refs[0]
    n2, inv2, gain2, slope, wr, we, n1, inv1, gain1 = refs[2 if with_loss else 1 :][:9]
    two_out, inner_out, one_out, emb_out, small_out, ff_out, acc, resid = refs[-8:]

    @pl.when(j == 0)
    def _():
        small_out[...] = jnp.zeros(small_out.shape, F32)
        if with_loss:
            loss, grad_embed = loss_parts(info, micro, micros, grad_scale, out_all[...], wc[...])
            emb_out[...] = grad_embed
            upstream = dot_nt(grad_embed, wc[...])
            small_out[6:7, 0:128] = jnp.broadcast_to(loss, (1, 128))
        else:
            upstream = rec[...].astype(F32)
        acc[...] = jnp.zeros(acc.shape, F32)
        n = n2[...].astype(F32)
        small_out[0:1, :] = column_sum(upstream * n)
        small_out[1:2, :] = column_sum(upstream)
        d_two = norm_rows_back(upstream, n, inv2[...], gain2[...])
        resid[...] = d_two
        d_two_b = d_two.astype(BF)
        two_out[...] = d_two_b
        small_out[2:3, :] = column_sum(d_two_b.astype(F32))

    d_act = dot_nt(two_out[...], wr[...])
    d_inner = (d_act * slope[...].astype(F32)).astype(BF)
    inner_out[...] = d_inner
    ff_out[0:1, :] = column_sum(d_inner.astype(F32))
    acc[...] += dot_nt(d_inner, we[...])

    @pl.when(j == count - 1)
    def _():
        upstream = resid[...] + acc[...]
        n = n1[...].astype(F32)
        small_out[3:4, :] = column_sum(upstream * n)
        small_out[4:5, :] = column_sum(upstream)
        d_one = norm_rows_back(upstream, n, inv1[...], gain1[...])
        resid[...] = d_one
        d_one_b = d_one.astype(BF)
        one_out[...] = d_one_b
        small_out[5:6, :] = column_sum(d_one_b.astype(F32))


def ffn_bwd_parts(section, micro, micros, received, kept, weights, step):
    (out_all, n2, inv2, slope, n1, inv1) = kept
    (wc, gains, wr, we) = weights
    slots, rows, width = out_all.shape
    ff = we.shape[1]
    slot = lambda i: slot_of(i, section, micro, micros)
    at = lambda g, i: step_of(i, section, step(g))
    one = lambda *shape: pl.BlockSpec(shape, lambda g, i: (0,) * len(shape))
    at_slot = lambda *shape: pl.BlockSpec((None,) + shape, lambda g, i: (slot(i), 0, 0))
    if section == 1:
        in_specs = [at_slot(rows, width), one(*wc.shape)]
        args = [out_all, wc]
    else:
        in_specs = [one(rows, width)]
        args = [received]
    in_specs += [
        at_slot(rows, width),
        at_slot(rows, 1),
        one(1, width),
        pl.BlockSpec((None, rows, FFBLOCK), lambda g, i: (slot(i), 0, at(g, i))),
        pl.BlockSpec((FFBLOCK, width), lambda g, i: (at(g, i), 0)),
        pl.BlockSpec((width, FFBLOCK), lambda g, i: (0, at(g, i))),
        at_slot(rows, width),
        at_slot(rows, 1),
        one(1, width),
    ]
    args += [n2, inv2, gains[1:2], slope, wr, we, n1, inv1, gains[0:1]]
    rows_at = lambda shape, kind: ((slots,) + shape, kind, (None,) + shape, lambda g, i: (slot(i), 0, 0))
    shapes = [
        rows_at((rows, width), BF),
        ((slots, rows, ff), BF, (None, rows, FFBLOCK), lambda g, i: (slot(i), 0, at(g, i))),
        rows_at((rows, width), BF),
        rows_at((rows, wc.shape[1]), BF),
        rows_at((8, width), F32),
        ((slots, 8, ff), F32, (None, 8, FFBLOCK), lambda g, i: (slot(i), 0, at(g, i))),
    ]
    return in_specs, args, shapes, [pltpu.VMEM((rows, width), F32), pltpu.VMEM((rows, width), F32)]


def ffn_backward(phase, micros, grad_scale, info, received, kept, weights, old):
    section, micro = 1 - phase // micros, phase % micros
    in_specs, args, shapes, scratch = ffn_bwd_parts(section, micro, micros, received, kept, weights, lambda g: g)
    steps = weights[3].shape[1] // FFBLOCK

    def body(micro, info, *refs):
        ffn_bwd_live(pl.program_id(0), steps, section == 1, micros, grad_scale, micro, info, *refs)

    return call(
        live_only(body, section, micro), steps, info, args, in_specs, shapes, old, scratch, flops=FLOPS_FFN
    )


def attn_bwd_live(g, count, with_send, micro, info, one_b, joined, lse, ctx, wm, *rest):
    qcode, kcode, dctx, delta, ktr, dqtr = rest[-6:]
    if with_send:
        wq, wk, wv, resid, acc = rest[:5]
        dq_out, dk_out, dv_out, sum_out, send_out = rest[-11:-6]
    else:
        dq_out, dk_out, dv_out, sum_out = rest[-10:-6]

    @pl.when(g == 0)
    def _():
        fill_codes(info, micro, qcode, kcode)
        if with_send:
            acc[...] = jnp.zeros(acc.shape, F32)

    dctx32 = dot_nt(one_b[...], wm[...])
    dctx[...] = dctx32.astype(BF)
    along = dctx[...].astype(F32) * ctx[...].astype(F32)
    pick = lax.broadcasted_iota(jnp.int32, (8, SLAB), 0) == lax.broadcasted_iota(jnp.int32, (8, SLAB), 1) // HEAD_DIM
    delta[...] = lax.dot_general(
        pick.astype(F32), along, (((1,), (1,)), ((), ())),
        precision=lax.Precision.HIGHEST, preferred_element_type=F32,
    )
    ktr[...] = jnp.transpose(joined[:, SLAB : 2 * SLAB])
    rows = one_b.shape[0]
    parts = (slice(0, QROWS), slice(QROWS, rows))
    for pair in range(SLAB // 128):
        lo = pair * 128
        qs = joined[:, lo : lo + 128] * BF(HEAD_DIM**-0.5)
        ks = joined[:, SLAB + lo : SLAB + lo + 128]
        vs = joined[:, 2 * SLAB + lo : 2 * SLAB + lo + 128]
        do = dctx[:, lo : lo + 128]
        qms = [head_lanes(qs, h, jnp.zeros_like(qs)) for h in range(2)]
        dms = [head_lanes(do, h, jnp.zeros_like(do)) for h in range(2)]
        ps, dss = ([], []), ([], [])
        for h in range(2):
            head = pair * 2 + h
            hh = slice(head * HEAD_DIM, head * HEAD_DIM + HEAD_DIM)
            qh = head_lanes(qs, h, qcode[...])
            kh = head_lanes(ks, h, kcode[...])
            for i, at in enumerate(parts):
                p = jnp.exp(dot_nt(kh[at], qh[at]) - lse[head : head + 1, at])
                dp = dot_nt(vs[at], dms[h][at])
                ds = (p * (dp - delta[head : head + 1, at])).astype(BF)
                ps[i].append(p.astype(BF))
                dss[i].append(ds)
                dqtr[hh, at] = dot_nn(ktr[hh, at], ds)
        for i, at in enumerate(parts):
            q_heads = jnp.concatenate([qm[at] for qm in qms])
            d_heads = jnp.concatenate([dm[at] for dm in dms])
            dk_out[at, lo : lo + 128] = dot_nn(jnp.concatenate(dss[i], axis=1), q_heads).astype(BF)
            dv_out[at, lo : lo + 128] = dot_nn(jnp.concatenate(ps[i], axis=1), d_heads).astype(BF)
    dq = (jnp.transpose(dqtr[...]) * HEAD_DIM**-0.5).astype(BF)
    dq_out[...] = dq
    dk = dk_out[...]
    dv = dv_out[...]
    sum_out[0:1, 0:SLAB] = column_sum(dq.astype(F32))
    sum_out[0:1, SLAB : 2 * SLAB] = column_sum(dv.astype(F32))
    if not with_send:
        return
    acc[...] += dot_nt(
        jnp.concatenate([dq, dk, dv], axis=1), jnp.concatenate([wq[...], wk[...], wv[...]], axis=1)
    )

    @pl.when(g == count - 1)
    def _():
        send_out[...] = (resid[...] + acc[...]).astype(BF)


def attn_bwd_parts(section, micro, micros, shape, kept, weights, step):
    (joined, lse, ctx) = kept
    (wa, wm) = weights
    slots, rows, width = shape
    count = width // SLAB
    slot = lambda i: slot_of(i, section, micro, micros)
    at = lambda g, i: step_of(i, section, step(g))
    in_specs = [
        pl.BlockSpec((None, None, rows, 3 * SLAB), lambda g, i: (slot(i), at(g, i), 0, 0)),
        pl.BlockSpec((None, None, 8, rows), lambda g, i: (slot(i), at(g, i), 0, 0)),
        pl.BlockSpec((None, rows, SLAB), lambda g, i: (slot(i), 0, at(g, i))),
        pl.BlockSpec((SLAB, width), lambda g, i: (at(g, i), 0)),
    ]
    args = [joined, lse, ctx, wm]
    slab = ((slots, rows, width), BF, (None, rows, SLAB), lambda g, i: (slot(i), 0, at(g, i)))
    shapes = [
        slab,
        slab,
        slab,
        ((slots, count, 8, 2 * SLAB), F32, (None, None, 8, 2 * SLAB), lambda g, i: (slot(i), at(g, i), 0, 0)),
    ]
    scratch = [
        pltpu.VMEM((rows, 128), BF),
        pltpu.VMEM((rows, 128), BF),
        pltpu.VMEM((rows, SLAB), BF),
        pltpu.VMEM((8, rows), F32),
        pltpu.VMEM((SLAB, rows), BF),
        pltpu.VMEM((SLAB, rows), F32),
    ]
    return in_specs, args, shapes, scratch


def attn_backward(phase, micros, info, one_all, kept, weights, old, slabs):
    section, micro = 1 - phase // micros, phase % micros
    slots, rows, width = one_all.shape
    in_specs, args, shapes, scratch = attn_bwd_parts(
        section, micro, micros, one_all.shape, kept, weights, lambda g: slabs[0] + g
    )
    in_specs = [pl.BlockSpec((None, rows, width), lambda g, i: (slot_of(i, section, micro, micros), 0, 0))] + in_specs

    def body(micro, info, *refs):
        attn_bwd_live(pl.program_id(0), len(slabs), False, micro, info, *refs)

    return call(
        live_only(body, section, micro), len(slabs), info, [one_all] + args, in_specs, shapes, old, scratch,
        flops=FLOPS_ATTN * len(slabs) * SLAB // width // 32, limit=SLAB_VMEM,
    )


def layer_backward(phase, micros, grad_scale, info, received, ffn_kept, attn_kept, weights, old):
    (wc, gains, wr, we, wa, wm) = weights
    section, micro = 1 - phase // micros, phase % micros
    shape = ffn_kept[0].shape
    _, rows, width = shape
    first, second = we.shape[1] // FFBLOCK, width // SLAB
    in_specs, args, shapes, scratch = ffn_bwd_parts(
        section, micro, micros, received, ffn_kept, (wc, gains, wr, we), lambda g: jnp.minimum(g, first - 1)
    )
    step = lambda g: jnp.maximum(g - first, 0)
    more = attn_bwd_parts(section, micro, micros, shape, attn_kept, (wa, wm), step)
    count = len(args)
    in_specs, args, shapes, scratch = in_specs + more[0], args + more[1], shapes + more[2], scratch + more[3]
    sends = section == 1
    if sends:
        at = lambda g, i: step_of(i, section, step(g))
        in_specs += [
            pl.BlockSpec((width, SLAB), lambda g, i, k=k: (0, k * second + at(g, i))) for k in range(3)
        ]
        args += [wa, wa, wa]
        shapes += [((rows, width), BF, (rows, width), lambda g, i: (0, 0))]

    def body(micro, info, *refs):
        ffn_in, attn_in = refs[:count], refs[count : count + 4]
        ins_q = refs[count + 4 : count + 7]
        inner = refs[-6:]
        acc, resid = refs[-8:-6]
        ends = 11 if sends else 10
        outs = refs[-8 - ends : -8]
        g = pl.program_id(0)

        @pl.when(g < first)
        def _():
            ffn_bwd_live(g, first, sends, micros, grad_scale, micro, info, *ffn_in, *outs[:6], acc, resid)

        @pl.when(g >= first)
        def _():
            extra = ins_q + (resid, acc) if sends else ()
            attn_bwd_live(g - first, second, sends, micro, info, outs[2], *attn_in, *extra, *outs[6:], *inner)

    return call(
        live_only(body, section, micro), first + second, info, args, in_specs, shapes, old, scratch,
        flops=FLOPS_FFN + FLOPS_ATTN,
    )


def mesh_bits():
    place = lax.axis_index("dp")
    bits = []
    bit = 1
    while bit < lax.axis_size("dp"):
        bits.append((bit, (place // bit) % 2))
        bit *= 2
    return bits


def grad_call(body, steps, core, in_specs, args, out_shape, out_specs, flops, limit=VMEM_LIMIT):
    return pl.pallas_call(
        body,
        out_shape=out_shape,
        grid_spec=pltpu.PrefetchScalarGridSpec(
            num_scalar_prefetch=1,
            grid=(steps,),
            in_specs=in_specs,
            out_specs=out_specs,
        ),
        compiler_params=pltpu.CompilerParams(vmem_limit_bytes=limit),
        cost_estimate=pl.CostEstimate(flops=flops // 16, bytes_accessed=100_000, transcendentals=0),
    )(core, *args)


def grad_half_body(info, left, right, *refs):
    total = dot_nn(jnp.transpose(left[...]), right[...])
    if len(refs) > 1:
        total = total + refs[0][...].astype(F32)
    refs[-1][...] = total.astype(BF)


def grad_half(rows, micro, core, mine, left, right, base):
    tall, wide = left.shape[1] // 2, right.shape[1]
    block = wide // GRAD_STEPS
    spec = pl.BlockSpec((tall, block), lambda s, h: (0, s))
    in_specs = [
        pl.BlockSpec((rows, tall), lambda s, h: (micro, h[0] if mine else 1 - h[0])),
        pl.BlockSpec((rows, block), lambda s, h: (micro, s)),
    ]
    args = [left, right]
    if base is not None:
        in_specs += [spec]
        args += [base]
    return grad_call(
        grad_half_body, GRAD_STEPS, core, in_specs, args,
        jax.ShapeDtypeStruct((tall, wide), BF), spec, 2 * rows * tall * wide, VMEM_LIMIT,
    )


def grad_rest_body(with_context, info, inputs, *refs):
    out = refs[-1]
    turned = jnp.transpose(inputs[...])
    parts = []
    if with_context:
        parts.append(dot_nn(jnp.transpose(refs[0][...]), refs[1][...]))
        refs = refs[2:]
    for at in range(0, len(refs) - 3, 3):
        parts.append(dot_nn(turned, jnp.concatenate([right[...] for right in refs[at : at + 3]], axis=1)))
    at = 0
    for part in parts:
        here = slice(at, at + part.shape[1])
        total = part if refs[-2] is None else part + refs[-2][:, here].astype(F32)
        out[:, here] = total.astype(BF)
        at += part.shape[1]


def grad_rest(rows, micro, core, mine, inputs, joined_grads, slabs, context, d_one, base):
    width = inputs.shape[1]
    side = pl.BlockSpec((rows, width // 2), lambda s, h: (micro, h[0] if mine else 1 - h[0]))
    in_specs, args = [side], [inputs]
    columns = 0
    if context is not None:
        in_specs += [side, pl.BlockSpec((rows, width), lambda s, h: (micro, 0))]
        args += [context, d_one]
        columns += width
    for slab in slabs:
        in_specs += [pl.BlockSpec((rows, SLAB), lambda s, h, slab=slab: (micro, slab))] * 3
        args += joined_grads
        columns += 3 * SLAB
    out = jax.ShapeDtypeStruct((width // 2, columns), BF)
    whole = pl.BlockSpec(out.shape, lambda s, h: (0, 0))
    if base is not None:
        in_specs += [whole]
        args += [base]
    body = functools.partial(grad_rest_body, context is not None)
    return grad_call(
        body if base is not None else lambda *refs: body(*refs[:-1], None, refs[-1]), 1, core, in_specs, args,
        out, whole, rows * columns * width,
    )


def widen_body(info, *refs):
    step = pl.program_id(0)
    count = 2 if len(refs) == 6 else 1
    outs = refs[2 * count :]
    for s in range(2):

        @pl.when(step == s)
        def _(s=s):
            parts = [ref[...].astype(F32) for ref in refs[s * count : s * count + count]]
            if count == 1:
                outs[0][...] = parts[0]
                return
            width = outs[1].shape[1]
            outs[1][...] = parts[0][:, :width]
            slabs = [parts[0][:, width:]] + [
                parts[1][:, at : at + 3 * SLAB] for at in range(0, parts[1].shape[1], 3 * SLAB)
            ]
            for g, slab in enumerate(slabs):
                for kind in range(3):
                    at = kind * width + g * SLAB
                    outs[0][:, at : at + SLAB] = slab[:, kind * SLAB : kind * SLAB + SLAB]


def widened(core, own, other, out_shapes):
    return pl.pallas_call(
        widen_body,
        out_shape=[jax.ShapeDtypeStruct(shape, F32) for shape in out_shapes],
        grid_spec=pltpu.PrefetchScalarGridSpec(
            num_scalar_prefetch=1,
            grid=(2,),
            in_specs=[pl.BlockSpec(one.shape, lambda s, h: (0, 0)) for one in own + other],
            out_specs=[
                pl.BlockSpec((shape[0] // 2, shape[1]), lambda s, h: (jnp.where(s == 0, h[0], 1 - h[0]), 0))
                for shape in out_shapes
            ],
        ),
        compiler_params=pltpu.CompilerParams(vmem_limit_bytes=SMALL_VMEM),
        cost_estimate=pl.CostEstimate(flops=0, bytes_accessed=14_000_000, transcendentals=0),
    )(core, *own, *other)


EXCHANGE = (
    "SR", "KR", "SE", "R", "KE", "E", "S0", "PS", "PK", "R", "S1", "E", "P", "R", "S2", "E", "QS", "R", "QK",
    "P", "E", "Q", "R", "P", "E", "V", "Q", "P", "R", "V", "E", "Q", "P", "Q", "Q", "R", "P", "V", "Q", "E",
    "WR", "V", "P", "Q", "WE", "WP",
)
ORDERS = {"R": 0, "E": 1, "P": 1, "Q": 0}
WIDENED = {"WR": ("R",), "WE": ("E",), "WP": ("P", "Q")}
KEEPERS = {"KR": ("R", "SR"), "KE": ("E", "SE"), "PK": ("P", "PS"), "QK": ("Q", "QS")}
KERNELS = ("SR", "KR", "SE", "KE", "S0", "PS", "PK", "S1", "S2", "QS", "QK")


def passed_along(array, axis, by):
    count = lax.axis_size(axis)
    pairs = [(i, i + by) for i in range(count) if 0 <= i + by < count]
    return lax.ppermute(array, axis, pairs)


def tied(array, *others):
    return lax.optimization_barrier((array, *others))[0]


def flatten_rows(leaf):
    return leaf.reshape(-1, leaf.shape[-1])


def swapped(array, bit, axis="dp"):
    count = lax.axis_size(axis)
    return lax.ppermute(array, axis, [(i, i ^ bit) for i in range(count)])


def piece(array, index):
    return lax.dynamic_index_in_dim(array, index, 0, keepdims=False)


def sum_low(kept, got):
    return (kept.astype(F32) + got.astype(F32)).astype(BF)


class Sequence:
    def __init__(self):
        self.last = ()

    def after(self, array):
        return tied(array, *self.last)

    def did(self, *arrays):
        self.last = arrays
        return arrays


class Adder:
    def __init__(self, sequence, value, bits):
        self.sequence, self.value = sequence, value
        self.bits = [step for step, _ in bits]
        self.got = swapped(value, self.bits[0])

    def take(self):
        self.bits.pop(0)
        self.value = sum_low(self.sequence.after(self.value), self.got)
        self.sequence.did(self.value)
        if self.bits:
            self.got = swapped(self.value, self.bits[0])


class Piece:
    def __init__(self, sequence, sent, kept, bits, order):
        self.sequence = sequence
        self.value = kept
        self.steps = [(sum_low, None)]
        self.steps += [(halved, bits[place]) for place in order]
        self.steps += [(doubled, bits[place]) for place in reversed(order)]
        self.got = swapped(sent, 1)

    def send(self):
        if not self.steps:
            self.sequence.did(self.value)
            self.got = swapped(self.value, 1)
            return
        step, (bit, mine) = self.steps[0]
        sent = self.value
        if step is halved:
            sent = piece(sent.reshape(2, sent.shape[0] // 2, sent.shape[1]), 1 - mine)
        self.sequence.did(self.value, sent)
        self.got = swapped(sent, bit)

    def take(self):
        step, bit = self.steps.pop(0)
        value = self.sequence.after(self.value)
        self.value = step(value, self.got) if bit is None else step(value, self.got, bit[1])
        self.send()


def halved(array, got, mine):
    halves = array.reshape(2, array.shape[0] // 2, array.shape[1])
    return sum_low(piece(halves, mine), got)


def doubled(array, got, mine):
    both = jnp.zeros((2,) + array.shape, array.dtype)
    both = lax.dynamic_update_index_in_dim(both, array, mine, 0)
    both = lax.dynamic_update_index_in_dim(both, got, 1 - mine, 0)
    return flatten_rows(both)


def exchange_order(digits):
    if digits == 4:
        return EXCHANGE
    rounds = ("R", "E", "P", "Q") * (2 * digits - 1)
    return KERNELS + rounds + ("V",) * digits + tuple(WIDENED)


def ends_of_pieces(pieces):
    return [one.value for one in pieces], [one.got for one in pieces]


def take(*pieces):
    for one in pieces:
        one.take()


def shards(
    hidden_in,
    attend_weight,
    attend_bias,
    mixing_weight,
    mixing_bias,
    norm_gain,
    norm_shift,
    expand_weight,
    expand_bias,
    reduce_weight,
    reduce_bias,
    colbert_weight,
    pass_lengths,
    positives,
):
    section_id = lax.axis_index("pipe")
    data_count = lax.axis_size("dp")
    micros = pass_lengths.shape[0]
    rows = hidden_in.shape[0] // micros
    width = hidden_in.shape[1]
    grad_scale = 1.0 / (data_count * micros * NQ)
    wa, wm, we, wr = attend_weight[0], mixing_weight[0], expand_weight[0], reduce_weight[0]
    gains, shifts = norm_gain[0], norm_shift[0]
    info = jnp.concatenate(
        [section_id.astype(jnp.int32)[None], pass_lengths.reshape(-1), positives.reshape(-1)]
    )
    bits = mesh_bits()
    core = bits[0][1].astype(jnp.int32)[None]
    along_x_first = list(range(1, len(bits)))
    along_z_first = [2, 1] + list(range(3, len(bits)))
    orders = (along_x_first, along_z_first)
    weights = (wa, attend_bias, wm, mixing_bias, we, expand_bias, wr, reduce_bias, gains, shifts)
    state = {"fwd": None, "bwd": None}
    arriving, returning = {}, {}

    def forward(phase, after=()):
        source = hidden_in if phase < micros else arriving[phase - micros]
        old = state["fwd"]
        state["fwd"] = layer_forward(
            phase, micros, info, tied(source, *after), weights, old and old[:14]
        )
        if phase < micros:
            arriving[phase] = passed_along(state["fwd"][14], "pipe", 1)

    def kept():
        fwd = state["fwd"]
        return (fwd[10], fwd[11], fwd[12], fwd[9], fwd[5], fwd[6]), (fwd[1], fwd[2], fwd[3])

    def arrived(phase, after):
        return None if phase < micros else tied(returning[phase - micros], *after)

    def backward(phase, after=()):
        old = state["bwd"]
        state["bwd"] = layer_backward(
            phase, micros, grad_scale, info, arrived(phase, after), *kept(),
            (colbert_weight, gains, wr, we, wa, wm), old and old[:10],
        )
        if phase < micros:
            returning[phase] = passed_along(state["bwd"][10], "pipe", -1)

    def backward_ffn(phase, after=()):
        made = ffn_backward(
            phase, micros, grad_scale, info, arrived(phase, after), kept()[0],
            (colbert_weight, gains, wr, we), state["bwd"][:6],
        )
        state["bwd"] = list(made) + list(state["bwd"][6:10])

    def backward_attn(phase, after, slabs):
        old = state["bwd"]
        made = attn_backward(
            phase, micros, tied(info, *after), old[2], kept()[1], (wa, wm), old[6:10], slabs
        )
        state["bwd"] = list(old[:6]) + list(made)

    for phase in range(micros):
        forward(phase)
    done = ()
    for phase in range(micros):
        forward(micros + phase, done)
        backward(phase)
        done = (state["bwd"][9],)
    fwd = state["fwd"]
    inputs, context, hidden, squares_one = fwd[0], fwd[3], fwd[4], fwd[7]
    active, outputs, squares_two = fwd[8], fwd[10], fwd[13]
    squares = jnp.stack(
        [
            jnp.sum(squares_one[:micros, 0], axis=1),
            jnp.sum(squares_one[:micros, 1], axis=1),
            jnp.sum(squares_two[:micros, 0], axis=1),
        ],
        axis=1,
    )
    for phase in range(micros, 2 * micros - 1):
        backward(phase, done)
        done = (state["bwd"][9],)
    last = 2 * micros - 1
    after_back = state["bwd"][9]
    colbert = dot_tn(flatten_rows(outputs[:micros]), flatten_rows(tied(state["bwd"][3], after_back)[:micros])).astype(BF)
    facts = jnp.concatenate([squares, tied(state["bwd"][4], after_back)[:micros, 6, 0:1]], axis=1)
    facts_down, colbert_down = passed_along(facts, "pipe", -1), passed_along(colbert, "pipe", -1)
    slabs = tuple(range(width // SLAB))
    ffn_back = state["bwd"][:6]
    lefts = [flatten_rows(a) for a in (active, hidden, inputs, context)]

    bases = {}
    for micro in range(micros - 1):
        first_core = tied(core, after_back)
        d_two, d_inner = (flatten_rows(ffn_back[i]) for i in range(2))
        for mine in (0, 1):
            old = bases.get(mine, (None,) * 2)
            bases[mine] = (
                grad_half(rows, micro, first_core, mine, lefts[0], d_two, old[0]),
                grad_half(rows, micro, first_core, mine, lefts[1], d_inner, old[1]),
            )
    backward_ffn(last, (facts, colbert, facts_down, colbert_down) + tuple(jax.tree.leaves(bases)))
    bases = bases or {0: (None,) * 2, 1: (None,) * 2}
    micro = micros - 1
    ffn_back = state["bwd"]
    d_two, d_inner, d_one = (flatten_rows(ffn_back[i]) for i in range(3))
    line = Sequence()

    def half_of(mine, left, right, which):
        [one] = line.did(grad_half(rows, micro, line.after(core), mine, left, right, bases[mine][which]))
        return one

    def rest_half(mine, some, which):
        joined_grads = [flatten_rows(a) for a in state["bwd"][6:9]]
        extra = (lefts[3], d_one) if which == 2 else (None, None)
        [one] = line.did(
            grad_rest(micros * rows, 0, line.after(core), mine, lefts[2], joined_grads, some, *extra, None)
        )
        return one

    def slab_back(slab):
        backward_attn(last, line.last, (slab,))
        line.did(*state["bwd"][6:10])

    made, pieces, widths = {}, {}, {}

    def run_kernel(name):
        made[name] = {
            "SR": lambda: half_of(0, lefts[0], d_two, 0),
            "KR": lambda: half_of(1, lefts[0], d_two, 0),
            "SE": lambda: half_of(0, lefts[1], d_inner, 1),
            "KE": lambda: half_of(1, lefts[1], d_inner, 1),
            "PS": lambda: rest_half(0, slabs[:1], 2),
            "PK": lambda: rest_half(1, slabs[:1], 2),
            "QS": lambda: rest_half(0, slabs[1:], 3),
            "QK": lambda: rest_half(1, slabs[1:], 3),
            "S0": lambda: slab_back(slabs[0]),
            "S1": lambda: slab_back(slabs[1]),
            "S2": lambda: [slab_back(slab) for slab in slabs[2:]],
        }[name]()

    def small_sums():
        small, small_ff, joined_sums = ffn_back[4], ffn_back[5], state["bwd"][9]
        small_sum = jnp.sum(small[:micros], axis=0)
        joined_sum = jnp.sum(joined_sums[:micros, :, 0], axis=0)
        attend_sum = jnp.concatenate(
            [joined_sum[:, :SLAB].reshape(-1), joined_sum[:, SLAB:].reshape(-1)]
        )
        of_colbert = jnp.where(section_id == 1, colbert, colbert_down)
        parts = [
            small_sum[:6],
            attend_sum.reshape(2, width),
            jnp.sum(small_ff[:micros, 0], axis=0).reshape(-1, width),
            of_colbert.astype(F32).reshape(-1, width),
        ]
        return jnp.concatenate(parts).astype(BF)

    for step in exchange_order(len(bits)):
        if step == "V" and step not in pieces:
            pieces[step] = Adder(line, small_sums(), bits)
        if step in pieces:
            pieces[step].take()
        elif step[0] == "W":
            if step == "WE":
                made["up"] = passed_along(line.after(facts), "pipe", 1)
            widths[step] = widened(
                line.after(core), *ends_of_pieces([pieces[one] for one in WIDENED[step]]),
                {"WR": [wr.shape], "WE": [we.shape], "WP": [wa.shape, wm.shape]}[step],
            )
            line.did(*widths[step])
        else:
            run_kernel(step)
            if step in KEEPERS:
                name, send = KEEPERS[step]
                pieces[name] = Piece(line, made[send], made[step], bits, orders[ORDERS[name]])
    first = jnp.where(section_id == 0, facts, made["up"])
    second = jnp.where(section_id == 0, facts_down, facts)
    [big_reduce], [big_expand], (big_attend, big_mixing) = (widths[one] for one in ("WR", "WE", "WP"))
    vector = pieces["V"].value
    vector = vector.astype(F32)
    colbert_sum = vector[8 + we.shape[1] // width :].reshape(colbert_weight.shape)
    counted = (QROWS + jnp.sum(pass_lengths, axis=1)).astype(F32)
    stats = jnp.stack([first[:, :3], second[:, :3]], axis=1)
    stats = jnp.sqrt(stats / (counted[:, None, None] * width))
    return (
        big_attend[None],
        vector[6:8].reshape(1, -1),
        big_mixing[None],
        vector[5][None],
        jnp.stack([vector[3], vector[0]])[None],
        jnp.stack([vector[4], vector[1]])[None],
        big_expand[None],
        vector[8 : 8 + we.shape[1] // width].reshape(1, -1),
        big_reduce[None],
        vector[2][None],
        colbert_sum,
        second[:, 3] / NQ,
        stats,
    )


def solution(mesh):
    placed = (
        P("dp", None),
        P("pipe", None, None),
        P("pipe", None),
        P("pipe", None, None),
        P("pipe", None),
        P("pipe", None, None),
        P("pipe", None, None),
        P("pipe", None, None),
        P("pipe", None),
        P("pipe", None, None),
        P("pipe", None),
        P(),
        P("dp", None),
        P("dp", None),
    )
    return jax.shard_map(
        shards,
        mesh=mesh,
        in_specs=placed,
        out_specs=(
            P("pipe", None, None),
            P("pipe", None),
            P("pipe", None, None),
            P("pipe", None),
            P("pipe", None, None),
            P("pipe", None, None),
            P("pipe", None, None),
            P("pipe", None),
            P("pipe", None, None),
            P("pipe", None),
            P(),
            P("dp"),
            P("dp", None, None),
        ),
        check_vma=False,
    )
```

```python
import functools
import jax
import jax.numpy as jnp
from jax import lax
from jax.experimental import pallas as pl
from jax.experimental.pallas import tpu as pltpu
from jax.sharding import PartitionSpec as P

HEAD_DIM = 64
QLEN = 32
NQ = 4
NP = 4
PSLOTS = 512
LAYER_EPSILON = 1e-12
UNIT_EPSILON = 1e-06
SMOOTHING = 0.05
LOGIT_SCALE = 4.0
ROOT_HALF = 0.7071067811865476
NORMAL_PEAK = 0.3989422804014327
BF = jnp.bfloat16
F32 = jnp.float32
QROWS = NQ * QLEN
SLAB = 256
FFBLOCK = 1536
BACKBLOCK = 768
VMEM_LIMIT = 56 * 1024 * 1024
NEG = -1e30
GRAD_STEPS = 2
SMALL_VMEM = 26 * 1024 * 1024
SLAB_VMEM = VMEM_LIMIT
FLOPS_FFN = 12_000_000_000
FLOPS_ATTN = 20_000_000_000


def dot_nn(a, b):
    return jnp.dot(a, b, preferred_element_type=F32)


def dot_nt(a, b):
    return lax.dot_general(a, b, (((1,), (1,)), ((), ())), preferred_element_type=F32)


def dot_tn(a, b):
    return lax.dot_general(a, b, (((0,), (0,)), ((), ())), preferred_element_type=F32)


def gelu_pair(u):
    phi = 0.5 + 0.5 * lax.erf(u * ROOT_HALF)
    return u * phi, phi + NORMAL_PEAK * u * jnp.exp(-0.5 * u * u)


def norm_rows(resid):
    centre = resid - jnp.mean(resid, axis=1, keepdims=True)
    inv = lax.rsqrt(jnp.mean(centre * centre, axis=1, keepdims=True) + LAYER_EPSILON)
    return centre * inv, inv


def ends_of(info, micro):
    base = 1 + micro * NP
    ends = []
    total = jnp.int32(0)
    for j in range(NP):
        total = total + info[base + j]
        ends.append(total)
    return ends


def passage_of(place, ends):
    out = jnp.zeros(place.shape, jnp.int32)
    for end in ends:
        out = out + jnp.where(place >= end, 1, 0)
    return out


def when_live(info, section, body):
    pl.when(info[0] == section)(body)


def slot_of(info, section, micro, spare):
    return jnp.where(info[0] == section, micro, spare)


def step_of(info, section, step):
    return jnp.where(info[0] == section, step, 0)


def fill_codes(info, micro, query_code, key_code):
    rows = query_code.shape[0]
    ends = [QROWS + end for end in ends_of(info, micro)]
    place = lax.broadcasted_iota(jnp.int32, (rows, 1), 0)
    segment = jnp.where(place < QROWS, place // QLEN, NQ + passage_of(place, ends))
    lane = lax.broadcasted_iota(jnp.int32, (1, 128), 1) % HEAD_DIM
    query_code[...] = jnp.where(segment == lane, 1.0, 0.0).astype(BF)
    key_code[...] = jnp.where((segment == lane) | (lane > NQ + NP), 0.0, NEG).astype(BF)


def usable_rows(info, micro, rows):
    ends = ends_of(info, micro)
    place = lax.broadcasted_iota(jnp.int32, (rows, 1), 0)
    return (place < QROWS + ends[-1]).astype(F32)


def head_lanes(value, h, others):
    lane = lax.broadcasted_iota(jnp.int32, (1, 128), 1) // HEAD_DIM
    return jnp.where(lane == h, value, others)


def live_only(body, section, micro):
    def kernel(info, *refs):
        when_live(info, section, lambda: body(micro, info, *refs))

    return kernel


def attn_fwd_live(g, count, micro, info, hid, wq, wk, wv, bq, bv, wm, bm, gain, shift, *rest):
    x_out, joined_out, lse_out, ctx_out, hid_out, n_out, inv_out, sq_out, acc, qcode, kcode, otr, vtr = rest
    rows = hid.shape[0]

    @pl.when(g == 0)
    def _():
        x_out[...] = hid[...]
        fill_codes(info, micro, qcode, kcode)
        acc[...] = jnp.zeros(acc.shape, F32)

    x = hid[...]
    qkv = dot_nn(x, jnp.concatenate([wq[...], wk[...], wv[...]], axis=1))
    q = (qkv[:, :SLAB] + bq[...]).astype(BF)
    joined_out[:, 0:SLAB] = q
    k = qkv[:, SLAB : 2 * SLAB].astype(BF)
    joined_out[:, SLAB : 2 * SLAB] = k
    v = (qkv[:, 2 * SLAB :] + bv[...]).astype(BF)
    joined_out[:, 2 * SLAB : 3 * SLAB] = v
    vtr[...] = jnp.transpose(v)
    parts = (slice(0, QROWS), slice(QROWS, rows))
    for pair in range(SLAB // 128):
        cols = slice(pair * 128, pair * 128 + 128)
        qs = joined_out[:, cols] * BF(HEAD_DIM**-0.5)
        ks = joined_out[:, SLAB + pair * 128 : SLAB + pair * 128 + 128]
        for h in range(2):
            head = pair * 2 + h
            vh = slice(head * HEAD_DIM, head * HEAD_DIM + HEAD_DIM)
            qh = head_lanes(qs, h, qcode[...])
            kh = head_lanes(ks, h, kcode[...])
            for at in parts:
                st = dot_nt(kh[at], qh[at])
                top = jnp.max(st, axis=0, keepdims=True)
                p = jnp.exp(st - top)
                total = jnp.sum(p, axis=0, keepdims=True)
                lse_out[head : head + 1, at] = top + jnp.log(total)
                otr[vh, at] = dot_nn(vtr[vh, at], p.astype(BF)) * (1.0 / total)
    ctx = jnp.transpose(otr[...]).astype(BF)
    ctx_out[...] = ctx
    acc[...] += dot_nn(ctx, wm[...])

    @pl.when(g == count - 1)
    def _():
        b1 = acc[...] + bm[...]
        x32 = hid[...].astype(F32)
        n, inv = norm_rows(x32 + b1)
        hid_out[...] = (n * gain[...] + shift[...]).astype(BF)
        n_out[...] = n.astype(BF)
        inv_out[...] = inv
        mask = usable_rows(info, micro, rows)
        sq_out[0:1, :] = jnp.sum(mask * x32 * x32, axis=0, keepdims=True)
        sq_out[1:2, :] = jnp.sum(mask * b1 * b1, axis=0, keepdims=True)


def call(body, steps, info, args, in_specs, shapes, old, scratch, flops, limit=VMEM_LIMIT):
    aliases = {}
    if old is not None:
        in_specs = in_specs + [pl.BlockSpec(memory_space=pl.ANY)] * len(old)
        aliases = {1 + len(args) + i: i for i in range(len(old))}
        args = args + list(old)
    return pl.pallas_call(
        body,
        out_shape=[jax.ShapeDtypeStruct(s[0], s[1]) for s in shapes],
        grid_spec=pltpu.PrefetchScalarGridSpec(
            num_scalar_prefetch=1,
            grid=(steps,),
            in_specs=in_specs,
            out_specs=[pl.BlockSpec(s[2], s[3]) for s in shapes],
            scratch_shapes=scratch,
        ),
        input_output_aliases=aliases,
        compiler_params=pltpu.CompilerParams(
            dimension_semantics=("arbitrary",), vmem_limit_bytes=limit
        ),
        cost_estimate=pl.CostEstimate(flops=flops, bytes_accessed=min(20_000_000, flops // 600), transcendentals=0),
    )(info, *args)


def ffn_fwd_live(j, count, micro, info, hid, we, be, wr, br, gain, shift, *rest):
    act_out, slope_out, out_all, n_out, inv_out, sq_out, send_out, acc = rest
    rows = hid.shape[0]

    @pl.when(j == 0)
    def _():
        acc[...] = jnp.zeros(acc.shape, F32)

    inner = dot_nn(hid[...], we[...]) + be[...]
    active, slope = gelu_pair(inner)
    active = active.astype(BF)
    act_out[...] = active
    slope_out[...] = slope.astype(BF)
    acc[...] += dot_nn(active, wr[...])

    @pl.when(j == count - 1)
    def _():
        b2 = acc[...] + br[...]
        n, inv = norm_rows(hid[...].astype(F32) + b2)
        out = (n * gain[...] + shift[...]).astype(BF)
        out_all[...] = out
        send_out[...] = out
        n_out[...] = n.astype(BF)
        inv_out[...] = inv
        mask = usable_rows(info, micro, rows)
        sq_out[0:1, :] = jnp.sum(mask * b2 * b2, axis=0, keepdims=True)


def layer_fwd_live(first, second, micro, info, *refs):
    attn_in, ffn_in = refs[:10], refs[10:16]
    attn_out, ffn_out = refs[-20:-12], refs[-12:-5]
    acc, qcode, kcode, otr, vtr = refs[-5:]
    g = pl.program_id(0)

    @pl.when(g < first)
    def _():
        attn_fwd_live(g, first, micro, info, *attn_in, *attn_out, acc, qcode, kcode, otr, vtr)

    @pl.when(g >= first)
    def _():
        ffn_fwd_live(g - first, second, micro, info, attn_out[4], *ffn_in, *ffn_out, acc)


def layer_forward(phase, micros, info, source, weights, old):
    (wa, ba, wm, bm, we, be, wr, br, gains, shifts) = weights
    section, micro = phase // micros, phase % micros
    width, ff = we.shape
    rows = source.shape[0] // micros if section == 0 else source.shape[0]
    place = micro if section == 0 else 0
    first, second = width // SLAB, ff // FFBLOCK
    slot = lambda i: slot_of(i, section, micro, micros)
    at = lambda g, i: step_of(i, section, jnp.minimum(g, first - 1))
    on = lambda g, i: step_of(i, section, jnp.maximum(g - first, 0))
    one = lambda *shape: pl.BlockSpec(shape, lambda g, i: (0,) * len(shape))
    in_specs = [
        pl.BlockSpec((rows, width), lambda g, i: (place, 0)),
        pl.BlockSpec((width, SLAB), lambda g, i: (0, at(g, i))),
        pl.BlockSpec((width, SLAB), lambda g, i: (0, first + at(g, i))),
        pl.BlockSpec((width, SLAB), lambda g, i: (0, 2 * first + at(g, i))),
        pl.BlockSpec((1, SLAB), lambda g, i: (0, at(g, i))),
        pl.BlockSpec((1, SLAB), lambda g, i: (0, first + at(g, i))),
        pl.BlockSpec((SLAB, width), lambda g, i: (at(g, i), 0)),
        one(1, width),
        one(1, width),
        one(1, width),
        pl.BlockSpec((width, FFBLOCK), lambda g, i: (0, on(g, i))),
        pl.BlockSpec((1, FFBLOCK), lambda g, i: (0, on(g, i))),
        pl.BlockSpec((FFBLOCK, width), lambda g, i: (on(g, i), 0)),
        one(1, width),
        one(1, width),
        one(1, width),
    ]
    args = [source, wa, wa, wa, ba, ba, wm, bm, gains[0:1], shifts[0:1]]
    args += [we, be, wr, br, gains[1:2], shifts[1:2]]
    slots = micros + 1
    rows_at = lambda shape, kind: ((slots,) + shape, kind, (None,) + shape, lambda g, i: (slot(i), 0, 0))
    wide = ((slots, rows, ff), BF, (None, rows, FFBLOCK), lambda g, i: (slot(i), 0, on(g, i)))
    shapes = [
        rows_at((rows, width), BF),
        ((slots, first, rows, 3 * SLAB), BF, (None, None, rows, 3 * SLAB), lambda g, i: (slot(i), at(g, i), 0, 0)),
        ((slots, first, 8, rows), F32, (None, None, 8, rows), lambda g, i: (slot(i), at(g, i), 0, 0)),
        ((slots, rows, width), BF, (None, rows, SLAB), lambda g, i: (slot(i), 0, at(g, i))),
        rows_at((rows, width), BF),
        rows_at((rows, width), BF),
        rows_at((rows, 1), F32),
        rows_at((8, width), F32),
        wide,
        wide,
        rows_at((rows, width), BF),
        rows_at((rows, width), BF),
        rows_at((rows, 1), F32),
        rows_at((8, width), F32),
        ((rows, width), BF, (rows, width), lambda g, i: (0, 0)),
    ]
    return call(
        live_only(functools.partial(layer_fwd_live, first, second), section, micro),
        first + second, info, args, in_specs, shapes, old,
        [
            pltpu.VMEM((rows, width), F32),
            pltpu.VMEM((rows, 128), BF),
            pltpu.VMEM((rows, 128), BF),
            pltpu.VMEM((SLAB, rows), F32),
            pltpu.VMEM((SLAB, rows), BF),
        ],
        flops=FLOPS_FFN + FLOPS_ATTN,
    )


def column_sum(value):
    return jnp.sum(value, axis=0, keepdims=True)


def norm_rows_back(grad_out, n, inv, gain):
    grad_unit = grad_out * gain
    mean_grad = jnp.mean(grad_unit, axis=1, keepdims=True)
    mean_along = jnp.mean(grad_unit * n, axis=1, keepdims=True)
    return inv * (grad_unit - mean_grad - n * mean_along)


def loss_parts(info, micro, micros, grad_scale, out_b, wc):
    ends = ends_of(info, micro)
    embedded = dot_nn(out_b, wc)
    inv_norm = lax.rsqrt(jnp.sum(embedded * embedded, axis=1, keepdims=True) + UNIT_EPSILON)
    unit = embedded * inv_norm
    unit_b = unit.astype(BF)
    queries, passages = unit_b[:QROWS], unit_b[QROWS:]
    scaled = dot_nt(queries, passages) / SMOOTHING
    owner = passage_of(lax.broadcasted_iota(jnp.int32, (1, PSLOTS), 1), ends)
    top = jnp.max(jnp.where(owner < NP, scaled, NEG), axis=1, keepdims=True)
    terms = jnp.exp(scaled - top)
    lane = lax.broadcasted_iota(jnp.int32, (1, 128), 1)
    totals = jnp.ones((QROWS, 128), F32)
    lengths = jnp.ones((1, 128), F32)
    for j in range(NP):
        total = jnp.sum(jnp.where(owner == j, terms, 0.0), axis=1, keepdims=True)
        totals = jnp.where(lane == j, total, totals)
        lengths = jnp.where(lane == j, info[1 + micro * NP + j].astype(F32), lengths)
    smooth = SMOOTHING * (jnp.log(totals) + top - jnp.log(lengths))
    grouped = jnp.sum(smooth.reshape(NQ, QLEN, 128), axis=1, keepdims=True)
    scores = LOGIT_SCALE * grouped
    scores = jnp.where(lane[None] < NP, scores, NEG)
    score_max = jnp.max(scores, axis=2, keepdims=True)
    score_exp = jnp.exp(scores - score_max)
    score_total = jnp.sum(score_exp, axis=2, keepdims=True)
    query = lax.broadcasted_iota(jnp.int32, (NQ, 1, 128), 0)
    chosen = jnp.zeros((NQ, 1, 128), jnp.int32)
    for i in range(NQ):
        chosen = jnp.where(query == i, info[1 + micros * NP + micro * NQ + i], chosen)
    onehot = (chosen == lane[None]).astype(F32)
    own_score = jnp.sum(jnp.where(chosen == lane[None], scores, 0.0), axis=2, keepdims=True)
    losses = jnp.log(score_total) + score_max - own_score
    loss = jnp.sum(losses, axis=0)
    grad_scores = (score_exp / score_total - onehot) * grad_scale
    grad_smooth = jnp.broadcast_to(LOGIT_SCALE * grad_scores, (NQ, QLEN, 128)).reshape(QROWS, 128)
    share = grad_smooth / totals
    weight = jnp.zeros((QROWS, PSLOTS), F32)
    for j in range(NP):
        weight = jnp.where(owner == j, share[:, j : j + 1], weight)
    grad_similar = jnp.where(owner < NP, terms * weight, 0.0).astype(BF)
    grad_unit = jnp.concatenate([dot_nn(grad_similar, passages), dot_tn(grad_similar, queries)])
    grad_embed = inv_norm * (grad_unit - unit * jnp.sum(grad_unit * unit, axis=1, keepdims=True))
    return loss, grad_embed.astype(BF)


def ffn_bwd_live(j, count, with_loss, micros, grad_scale, micro, info, *refs):
    if with_loss:
        out_all, wc = refs[:2]
    else:
        rec = refs[0]
    n2, inv2, gain2, slope, wr, we, n1, inv1, gain1 = refs[2 if with_loss else 1 :][:9]
    two_out, inner_out, one_out, emb_out, small_out, ff_out, acc, resid = refs[-8:]

    @pl.when(j == 0)
    def _():
        small_out[...] = jnp.zeros(small_out.shape, F32)
        if with_loss:
            loss, grad_embed = loss_parts(info, micro, micros, grad_scale, out_all[...], wc[...])
            emb_out[...] = grad_embed
            upstream = dot_nt(grad_embed, wc[...])
            small_out[6:7, 0:128] = jnp.broadcast_to(loss, (1, 128))
        else:
            upstream = rec[...].astype(F32)
        acc[...] = jnp.zeros(acc.shape, F32)
        n = n2[...].astype(F32)
        small_out[0:1, :] = column_sum(upstream * n)
        small_out[1:2, :] = column_sum(upstream)
        d_two = norm_rows_back(upstream, n, inv2[...], gain2[...])
        resid[...] = d_two
        d_two_b = d_two.astype(BF)
        two_out[...] = d_two_b
        small_out[2:3, :] = column_sum(d_two_b.astype(F32))

    d_act = dot_nt(two_out[...], wr[...])
    d_inner = (d_act * slope[...].astype(F32)).astype(BF)
    inner_out[...] = d_inner
    ff_out[0:1, :] = column_sum(d_inner.astype(F32))
    acc[...] += dot_nt(d_inner, we[...])

    @pl.when(j == count - 1)
    def _():
        upstream = resid[...] + acc[...]
        n = n1[...].astype(F32)
        small_out[3:4, :] = column_sum(upstream * n)
        small_out[4:5, :] = column_sum(upstream)
        d_one = norm_rows_back(upstream, n, inv1[...], gain1[...])
        resid[...] = d_one
        d_one_b = d_one.astype(BF)
        one_out[...] = d_one_b
        small_out[5:6, :] = column_sum(d_one_b.astype(F32))


def ffn_bwd_parts(section, micro, micros, received, kept, weights, step):
    (out_all, n2, inv2, slope, n1, inv1) = kept
    (wc, gains, wr, we) = weights
    slots, rows, width = out_all.shape
    ff = we.shape[1]
    slot = lambda i: slot_of(i, section, micro, micros)
    at = lambda g, i: step_of(i, section, step(g))
    one = lambda *shape: pl.BlockSpec(shape, lambda g, i: (0,) * len(shape))
    at_slot = lambda *shape: pl.BlockSpec((None,) + shape, lambda g, i: (slot(i), 0, 0))
    if section == 1:
        in_specs = [at_slot(rows, width), one(*wc.shape)]
        args = [out_all, wc]
    else:
        in_specs = [one(rows, width)]
        args = [received]
    in_specs += [
        at_slot(rows, width),
        at_slot(rows, 1),
        one(1, width),
        pl.BlockSpec((None, rows, BACKBLOCK), lambda g, i: (slot(i), 0, at(g, i))),
        pl.BlockSpec((BACKBLOCK, width), lambda g, i: (at(g, i), 0)),
        pl.BlockSpec((width, BACKBLOCK), lambda g, i: (0, at(g, i))),
        at_slot(rows, width),
        at_slot(rows, 1),
        one(1, width),
    ]
    args += [n2, inv2, gains[1:2], slope, wr, we, n1, inv1, gains[0:1]]
    rows_at = lambda shape, kind: ((slots,) + shape, kind, (None,) + shape, lambda g, i: (slot(i), 0, 0))
    shapes = [
        rows_at((rows, width), BF),
        ((slots, rows, ff), BF, (None, rows, BACKBLOCK), lambda g, i: (slot(i), 0, at(g, i))),
        rows_at((rows, width), BF),
        rows_at((rows, wc.shape[1]), BF),
        rows_at((8, width), F32),
        ((slots, 8, ff), F32, (None, 8, BACKBLOCK), lambda g, i: (slot(i), 0, at(g, i))),
    ]
    return in_specs, args, shapes, [pltpu.VMEM((rows, width), F32), pltpu.VMEM((rows, width), F32)]


def ffn_backward(phase, micros, grad_scale, info, received, kept, weights, old):
    section, micro = 1 - phase // micros, phase % micros
    in_specs, args, shapes, scratch = ffn_bwd_parts(section, micro, micros, received, kept, weights, lambda g: g)
    steps = weights[3].shape[1] // BACKBLOCK

    def body(micro, info, *refs):
        ffn_bwd_live(pl.program_id(0), steps, section == 1, micros, grad_scale, micro, info, *refs)

    return call(
        live_only(body, section, micro), steps, info, args, in_specs, shapes, old, scratch, flops=FLOPS_FFN
    )


def attn_bwd_live(g, count, with_send, micro, info, one_b, joined, lse, ctx, wm, *rest):
    qcode, kcode, dctx, delta, ktr, dqtr = rest[-6:]
    if with_send:
        wq, wk, wv, resid, acc = rest[:5]
        dq_out, dk_out, dv_out, sum_out, send_out = rest[-11:-6]
    else:
        dq_out, dk_out, dv_out, sum_out = rest[-10:-6]

    @pl.when(g == 0)
    def _():
        fill_codes(info, micro, qcode, kcode)
        if with_send:
            acc[...] = jnp.zeros(acc.shape, F32)

    dctx32 = dot_nt(one_b[...], wm[...])
    dctx[...] = dctx32.astype(BF)
    along = dctx[...].astype(F32) * ctx[...].astype(F32)
    pick = lax.broadcasted_iota(jnp.int32, (8, SLAB), 0) == lax.broadcasted_iota(jnp.int32, (8, SLAB), 1) // HEAD_DIM
    delta[...] = lax.dot_general(
        pick.astype(F32), along, (((1,), (1,)), ((), ())),
        precision=lax.Precision.HIGHEST, preferred_element_type=F32,
    )
    ktr[...] = jnp.transpose(joined[:, SLAB : 2 * SLAB])
    rows = one_b.shape[0]
    parts = (slice(0, QROWS), slice(QROWS, rows))
    for pair in range(SLAB // 128):
        lo = pair * 128
        qs = joined[:, lo : lo + 128] * BF(HEAD_DIM**-0.5)
        ks = joined[:, SLAB + lo : SLAB + lo + 128]
        vs = joined[:, 2 * SLAB + lo : 2 * SLAB + lo + 128]
        do = dctx[:, lo : lo + 128]
        qms = [head_lanes(qs, h, jnp.zeros_like(qs)) for h in range(2)]
        dms = [head_lanes(do, h, jnp.zeros_like(do)) for h in range(2)]
        ps, dss = ([], []), ([], [])
        for h in range(2):
            head = pair * 2 + h
            hh = slice(head * HEAD_DIM, head * HEAD_DIM + HEAD_DIM)
            qh = head_lanes(qs, h, qcode[...])
            kh = head_lanes(ks, h, kcode[...])
            for i, at in enumerate(parts):
                p = jnp.exp(dot_nt(kh[at], qh[at]) - lse[head : head + 1, at])
                dp = dot_nt(vs[at], dms[h][at])
                ds = (p * (dp - delta[head : head + 1, at])).astype(BF)
                ps[i].append(p.astype(BF))
                dss[i].append(ds)
                dqtr[hh, at] = dot_nn(ktr[hh, at], ds)
        for i, at in enumerate(parts):
            q_heads = jnp.concatenate([qm[at] for qm in qms])
            d_heads = jnp.concatenate([dm[at] for dm in dms])
            dk_out[at, lo : lo + 128] = dot_nn(jnp.concatenate(dss[i], axis=1), q_heads).astype(BF)
            dv_out[at, lo : lo + 128] = dot_nn(jnp.concatenate(ps[i], axis=1), d_heads).astype(BF)
    dq = (jnp.transpose(dqtr[...]) * HEAD_DIM**-0.5).astype(BF)
    dq_out[...] = dq
    dk = dk_out[...]
    dv = dv_out[...]
    sum_out[0:1, 0:SLAB] = column_sum(dq.astype(F32))
    sum_out[0:1, SLAB : 2 * SLAB] = column_sum(dv.astype(F32))
    if not with_send:
        return
    acc[...] += dot_nt(
        jnp.concatenate([dq, dk, dv], axis=1), jnp.concatenate([wq[...], wk[...], wv[...]], axis=1)
    )

    @pl.when(g == count - 1)
    def _():
        send_out[...] = (resid[...] + acc[...]).astype(BF)


def attn_bwd_parts(section, micro, micros, shape, kept, weights, step):
    (joined, lse, ctx) = kept
    (wa, wm) = weights
    slots, rows, width = shape
    count = width // SLAB
    slot = lambda i: slot_of(i, section, micro, micros)
    at = lambda g, i: step_of(i, section, step(g))
    in_specs = [
        pl.BlockSpec((None, None, rows, 3 * SLAB), lambda g, i: (slot(i), at(g, i), 0, 0)),
        pl.BlockSpec((None, None, 8, rows), lambda g, i: (slot(i), at(g, i), 0, 0)),
        pl.BlockSpec((None, rows, SLAB), lambda g, i: (slot(i), 0, at(g, i))),
        pl.BlockSpec((SLAB, width), lambda g, i: (at(g, i), 0)),
    ]
    args = [joined, lse, ctx, wm]
    slab = ((slots, rows, width), BF, (None, rows, SLAB), lambda g, i: (slot(i), 0, at(g, i)))
    shapes = [
        slab,
        slab,
        slab,
        ((slots, count, 8, 2 * SLAB), F32, (None, None, 8, 2 * SLAB), lambda g, i: (slot(i), at(g, i), 0, 0)),
    ]
    scratch = [
        pltpu.VMEM((rows, 128), BF),
        pltpu.VMEM((rows, 128), BF),
        pltpu.VMEM((rows, SLAB), BF),
        pltpu.VMEM((8, rows), F32),
        pltpu.VMEM((SLAB, rows), BF),
        pltpu.VMEM((SLAB, rows), F32),
    ]
    return in_specs, args, shapes, scratch


def attn_backward(phase, micros, info, one_all, kept, weights, old, slabs):
    section, micro = 1 - phase // micros, phase % micros
    slots, rows, width = one_all.shape
    in_specs, args, shapes, scratch = attn_bwd_parts(
        section, micro, micros, one_all.shape, kept, weights, lambda g: slabs[0] + g
    )
    in_specs = [pl.BlockSpec((None, rows, width), lambda g, i: (slot_of(i, section, micro, micros), 0, 0))] + in_specs

    def body(micro, info, *refs):
        attn_bwd_live(pl.program_id(0), len(slabs), False, micro, info, *refs)

    return call(
        live_only(body, section, micro), len(slabs), info, [one_all] + args, in_specs, shapes, old, scratch,
        flops=FLOPS_ATTN * len(slabs) * SLAB // width // 32, limit=SLAB_VMEM,
    )


def layer_backward(phase, micros, grad_scale, info, received, ffn_kept, attn_kept, weights, old):
    (wc, gains, wr, we, wa, wm) = weights
    section, micro = 1 - phase // micros, phase % micros
    shape = ffn_kept[0].shape
    _, rows, width = shape
    first, second = we.shape[1] // BACKBLOCK, width // SLAB
    in_specs, args, shapes, scratch = ffn_bwd_parts(
        section, micro, micros, received, ffn_kept, (wc, gains, wr, we), lambda g: jnp.minimum(g, first - 1)
    )
    step = lambda g: jnp.maximum(g - first, 0)
    more = attn_bwd_parts(section, micro, micros, shape, attn_kept, (wa, wm), step)
    count = len(args)
    in_specs, args, shapes, scratch = in_specs + more[0], args + more[1], shapes + more[2], scratch + more[3]
    sends = section == 1
    if sends:
        at = lambda g, i: step_of(i, section, step(g))
        in_specs += [
            pl.BlockSpec((width, SLAB), lambda g, i, k=k: (0, k * second + at(g, i))) for k in range(3)
        ]
        args += [wa, wa, wa]
        shapes += [((rows, width), BF, (rows, width), lambda g, i: (0, 0))]

    def body(micro, info, *refs):
        ffn_in, attn_in = refs[:count], refs[count : count + 4]
        ins_q = refs[count + 4 : count + 7]
        inner = refs[-6:]
        acc, resid = refs[-8:-6]
        ends = 11 if sends else 10
        outs = refs[-8 - ends : -8]
        g = pl.program_id(0)

        @pl.when(g < first)
        def _():
            ffn_bwd_live(g, first, sends, micros, grad_scale, micro, info, *ffn_in, *outs[:6], acc, resid)

        @pl.when(g >= first)
        def _():
            extra = ins_q + (resid, acc) if sends else ()
            attn_bwd_live(g - first, second, sends, micro, info, outs[2], *attn_in, *extra, *outs[6:], *inner)

    return call(
        live_only(body, section, micro), first + second, info, args, in_specs, shapes, old, scratch,
        flops=FLOPS_FFN + FLOPS_ATTN,
    )


def mesh_bits():
    place = lax.axis_index("dp")
    bits = []
    bit = 1
    while bit < lax.axis_size("dp"):
        bits.append((bit, (place // bit) % 2))
        bit *= 2
    return bits


def grad_call(body, steps, core, in_specs, args, out_shape, out_specs, flops, limit=VMEM_LIMIT):
    return pl.pallas_call(
        body,
        out_shape=out_shape,
        grid_spec=pltpu.PrefetchScalarGridSpec(
            num_scalar_prefetch=1,
            grid=(steps,),
            in_specs=in_specs,
            out_specs=out_specs,
        ),
        compiler_params=pltpu.CompilerParams(vmem_limit_bytes=limit),
        cost_estimate=pl.CostEstimate(flops=flops // 16, bytes_accessed=100_000, transcendentals=0),
    )(core, *args)


def grad_half_body(info, left, right, *refs):
    total = dot_nn(jnp.transpose(left[...]), right[...])
    if len(refs) > 1:
        total = total + refs[0][...].astype(F32)
    refs[-1][...] = total.astype(BF)


def grad_half(rows, micro, core, mine, left, right, base):
    tall, wide = left.shape[1] // 2, right.shape[1]
    block = wide // GRAD_STEPS
    spec = pl.BlockSpec((tall, block), lambda s, h: (0, s))
    in_specs = [
        pl.BlockSpec((rows, tall), lambda s, h: (micro, h[0] if mine else 1 - h[0])),
        pl.BlockSpec((rows, block), lambda s, h: (micro, s)),
    ]
    args = [left, right]
    if base is not None:
        in_specs += [spec]
        args += [base]
    return grad_call(
        grad_half_body, GRAD_STEPS, core, in_specs, args,
        jax.ShapeDtypeStruct((tall, wide), BF), spec, 2 * rows * tall * wide, VMEM_LIMIT,
    )


def grad_rest_body(with_context, info, inputs, *refs):
    out = refs[-1]
    turned = jnp.transpose(inputs[...])
    parts = []
    if with_context:
        parts.append(dot_nn(jnp.transpose(refs[0][...]), refs[1][...]))
        refs = refs[2:]
    for at in range(0, len(refs) - 3, 3):
        parts.append(dot_nn(turned, jnp.concatenate([right[...] for right in refs[at : at + 3]], axis=1)))
    at = 0
    for part in parts:
        here = slice(at, at + part.shape[1])
        total = part if refs[-2] is None else part + refs[-2][:, here].astype(F32)
        out[:, here] = total.astype(BF)
        at += part.shape[1]


def grad_rest(rows, micro, core, mine, inputs, joined_grads, slabs, context, d_one, base):
    width = inputs.shape[1]
    side = pl.BlockSpec((rows, width // 2), lambda s, h: (micro, h[0] if mine else 1 - h[0]))
    in_specs, args = [side], [inputs]
    columns = 0
    if context is not None:
        in_specs += [side, pl.BlockSpec((rows, width), lambda s, h: (micro, 0))]
        args += [context, d_one]
        columns += width
    for slab in slabs:
        in_specs += [pl.BlockSpec((rows, SLAB), lambda s, h, slab=slab: (micro, slab))] * 3
        args += joined_grads
        columns += 3 * SLAB
    out = jax.ShapeDtypeStruct((width // 2, columns), BF)
    whole = pl.BlockSpec(out.shape, lambda s, h: (0, 0))
    if base is not None:
        in_specs += [whole]
        args += [base]
    body = functools.partial(grad_rest_body, context is not None)
    return grad_call(
        body if base is not None else lambda *refs: body(*refs[:-1], None, refs[-1]), 1, core, in_specs, args,
        out, whole, rows * columns * width,
    )


def widen_body(info, *refs):
    step = pl.program_id(0)
    count = 2 if len(refs) == 6 else 1
    outs = refs[2 * count :]
    for s in range(2):

        @pl.when(step == s)
        def _(s=s):
            parts = [ref[...].astype(F32) for ref in refs[s * count : s * count + count]]
            if count == 1:
                outs[0][...] = parts[0]
                return
            width = outs[1].shape[1]
            outs[1][...] = parts[0][:, :width]
            slabs = [parts[0][:, width:]] + [
                parts[1][:, at : at + 3 * SLAB] for at in range(0, parts[1].shape[1], 3 * SLAB)
            ]
            for g, slab in enumerate(slabs):
                for kind in range(3):
                    at = kind * width + g * SLAB
                    outs[0][:, at : at + SLAB] = slab[:, kind * SLAB : kind * SLAB + SLAB]


def widened(core, own, other, out_shapes):
    return pl.pallas_call(
        widen_body,
        out_shape=[jax.ShapeDtypeStruct(shape, F32) for shape in out_shapes],
        grid_spec=pltpu.PrefetchScalarGridSpec(
            num_scalar_prefetch=1,
            grid=(2,),
            in_specs=[pl.BlockSpec(one.shape, lambda s, h: (0, 0)) for one in own + other],
            out_specs=[
                pl.BlockSpec((shape[0] // 2, shape[1]), lambda s, h: (jnp.where(s == 0, h[0], 1 - h[0]), 0))
                for shape in out_shapes
            ],
        ),
        compiler_params=pltpu.CompilerParams(vmem_limit_bytes=SMALL_VMEM),
        cost_estimate=pl.CostEstimate(flops=0, bytes_accessed=14_000_000, transcendentals=0),
    )(core, *own, *other)


EXCHANGE = (
    "SR", "KR", "SE", "R", "KE", "E", "S0", "PS", "PK", "R", "S1", "E", "P", "R", "S2", "E", "QS", "R", "QK",
    "P", "E", "Q", "R", "P", "E", "V", "Q", "P", "R", "V", "E", "Q", "P", "Q", "Q", "R", "P", "V", "Q", "E",
    "WR", "V", "P", "Q", "WE", "WP",
)
ORDERS = {"R": 0, "E": 1, "P": 1, "Q": 0}
WIDENED = {"WR": ("R",), "WE": ("E",), "WP": ("P", "Q")}
KEEPERS = {"KR": ("R", "SR"), "KE": ("E", "SE"), "PK": ("P", "PS"), "QK": ("Q", "QS")}
KERNELS = ("SR", "KR", "SE", "KE", "S0", "PS", "PK", "S1", "S2", "QS", "QK")


def passed_along(array, axis, by):
    count = lax.axis_size(axis)
    pairs = [(i, i + by) for i in range(count) if 0 <= i + by < count]
    return lax.ppermute(array, axis, pairs)


def tied(array, *others):
    return lax.optimization_barrier((array, *others))[0]


def flatten_rows(leaf):
    return leaf.reshape(-1, leaf.shape[-1])


def swapped(array, bit, axis="dp"):
    count = lax.axis_size(axis)
    return lax.ppermute(array, axis, [(i, i ^ bit) for i in range(count)])


def piece(array, index):
    return lax.dynamic_index_in_dim(array, index, 0, keepdims=False)


def sum_low(kept, got):
    return (kept.astype(F32) + got.astype(F32)).astype(BF)


class Sequence:
    def __init__(self):
        self.last = ()

    def after(self, array):
        return tied(array, *self.last)

    def did(self, *arrays):
        self.last = arrays
        return arrays


class Adder:
    def __init__(self, sequence, value, bits):
        self.sequence, self.value = sequence, value
        self.bits = [step for step, _ in bits]
        self.got = swapped(value, self.bits[0])

    def take(self):
        self.bits.pop(0)
        self.value = sum_low(self.sequence.after(self.value), self.got)
        self.sequence.did(self.value)
        if self.bits:
            self.got = swapped(self.value, self.bits[0])


class Piece:
    def __init__(self, sequence, sent, kept, bits, order):
        self.sequence = sequence
        self.value = kept
        self.steps = [(sum_low, None)]
        self.steps += [(halved, bits[place]) for place in order]
        self.steps += [(doubled, bits[place]) for place in reversed(order)]
        self.got = swapped(sent, 1)

    def send(self):
        if not self.steps:
            self.sequence.did(self.value)
            self.got = swapped(self.value, 1)
            return
        step, (bit, mine) = self.steps[0]
        sent = self.value
        if step is halved:
            sent = piece(sent.reshape(2, sent.shape[0] // 2, sent.shape[1]), 1 - mine)
        self.sequence.did(self.value, sent)
        self.got = swapped(sent, bit)

    def take(self):
        step, bit = self.steps.pop(0)
        value = self.sequence.after(self.value)
        self.value = step(value, self.got) if bit is None else step(value, self.got, bit[1])
        self.send()


def halved(array, got, mine):
    halves = array.reshape(2, array.shape[0] // 2, array.shape[1])
    return sum_low(piece(halves, mine), got)


def doubled(array, got, mine):
    both = jnp.zeros((2,) + array.shape, array.dtype)
    both = lax.dynamic_update_index_in_dim(both, array, mine, 0)
    both = lax.dynamic_update_index_in_dim(both, got, 1 - mine, 0)
    return flatten_rows(both)


def exchange_order(digits):
    if digits == 4:
        return EXCHANGE
    rounds = ("R", "E", "P", "Q") * (2 * digits - 1)
    return KERNELS + rounds + ("V",) * digits + tuple(WIDENED)


def ends_of_pieces(pieces):
    return [one.value for one in pieces], [one.got for one in pieces]


def take(*pieces):
    for one in pieces:
        one.take()


def shards(
    hidden_in,
    attend_weight,
    attend_bias,
    mixing_weight,
    mixing_bias,
    norm_gain,
    norm_shift,
    expand_weight,
    expand_bias,
    reduce_weight,
    reduce_bias,
    colbert_weight,
    pass_lengths,
    positives,
):
    section_id = lax.axis_index("pipe")
    data_count = lax.axis_size("dp")
    micros = pass_lengths.shape[0]
    rows = hidden_in.shape[0] // micros
    width = hidden_in.shape[1]
    grad_scale = 1.0 / (data_count * micros * NQ)
    wa, wm, we, wr = attend_weight[0], mixing_weight[0], expand_weight[0], reduce_weight[0]
    gains, shifts = norm_gain[0], norm_shift[0]
    info = jnp.concatenate(
        [section_id.astype(jnp.int32)[None], pass_lengths.reshape(-1), positives.reshape(-1)]
    )
    bits = mesh_bits()
    core = bits[0][1].astype(jnp.int32)[None]
    along_x_first = list(range(1, len(bits)))
    along_z_first = [2, 1] + list(range(3, len(bits)))
    orders = (along_x_first, along_z_first)
    weights = (wa, attend_bias, wm, mixing_bias, we, expand_bias, wr, reduce_bias, gains, shifts)
    state = {"fwd": None, "bwd": None}
    arriving, returning = {}, {}

    def forward(phase, after=()):
        source = hidden_in if phase < micros else arriving[phase - micros]
        old = state["fwd"]
        state["fwd"] = layer_forward(
            phase, micros, info, tied(source, *after), weights, old and old[:14]
        )
        if phase < micros:
            arriving[phase] = passed_along(state["fwd"][14], "pipe", 1)

    def kept():
        fwd = state["fwd"]
        return (fwd[10], fwd[11], fwd[12], fwd[9], fwd[5], fwd[6]), (fwd[1], fwd[2], fwd[3])

    def arrived(phase, after):
        return None if phase < micros else tied(returning[phase - micros], *after)

    def backward(phase, after=()):
        old = state["bwd"]
        state["bwd"] = layer_backward(
            phase, micros, grad_scale, info, arrived(phase, after), *kept(),
            (colbert_weight, gains, wr, we, wa, wm), old and old[:10],
        )
        if phase < micros:
            returning[phase] = passed_along(state["bwd"][10], "pipe", -1)

    def backward_ffn(phase, after=()):
        made = ffn_backward(
            phase, micros, grad_scale, info, arrived(phase, after), kept()[0],
            (colbert_weight, gains, wr, we), state["bwd"][:6],
        )
        state["bwd"] = list(made) + list(state["bwd"][6:10])

    def backward_attn(phase, after, slabs):
        old = state["bwd"]
        made = attn_backward(
            phase, micros, tied(info, *after), old[2], kept()[1], (wa, wm), old[6:10], slabs
        )
        state["bwd"] = list(old[:6]) + list(made)

    for phase in range(micros):
        forward(phase)
    done = ()
    for phase in range(micros):
        forward(micros + phase, done)
        backward(phase)
        done = (state["bwd"][9],)
    fwd = state["fwd"]
    inputs, context, hidden, squares_one = fwd[0], fwd[3], fwd[4], fwd[7]
    active, outputs, squares_two = fwd[8], fwd[10], fwd[13]
    squares = jnp.stack(
        [
            jnp.sum(squares_one[:micros, 0], axis=1),
            jnp.sum(squares_one[:micros, 1], axis=1),
            jnp.sum(squares_two[:micros, 0], axis=1),
        ],
        axis=1,
    )
    for phase in range(micros, 2 * micros - 1):
        backward(phase, done)
        done = (state["bwd"][9],)
    last = 2 * micros - 1
    after_back = state["bwd"][9]
    colbert = dot_tn(flatten_rows(outputs[:micros]), flatten_rows(tied(state["bwd"][3], after_back)[:micros])).astype(BF)
    facts = jnp.concatenate([squares, tied(state["bwd"][4], after_back)[:micros, 6, 0:1]], axis=1)
    facts_down, colbert_down = passed_along(facts, "pipe", -1), passed_along(colbert, "pipe", -1)
    slabs = tuple(range(width // SLAB))
    ffn_back = state["bwd"][:6]
    lefts = [flatten_rows(a) for a in (active, hidden, inputs, context)]

    bases = {}
    for micro in range(micros - 1):
        first_core = tied(core, after_back)
        d_two, d_inner = (flatten_rows(ffn_back[i]) for i in range(2))
        for mine in (0, 1):
            old = bases.get(mine, (None,) * 2)
            bases[mine] = (
                grad_half(rows, micro, first_core, mine, lefts[0], d_two, old[0]),
                grad_half(rows, micro, first_core, mine, lefts[1], d_inner, old[1]),
            )
    backward_ffn(last, (facts, colbert, facts_down, colbert_down) + tuple(jax.tree.leaves(bases)))
    bases = bases or {0: (None,) * 2, 1: (None,) * 2}
    micro = micros - 1
    ffn_back = state["bwd"]
    d_two, d_inner, d_one = (flatten_rows(ffn_back[i]) for i in range(3))
    line = Sequence()

    def half_of(mine, left, right, which):
        [one] = line.did(grad_half(rows, micro, line.after(core), mine, left, right, bases[mine][which]))
        return one

    def rest_half(mine, some, which):
        joined_grads = [flatten_rows(a) for a in state["bwd"][6:9]]
        extra = (lefts[3], d_one) if which == 2 else (None, None)
        [one] = line.did(
            grad_rest(micros * rows, 0, line.after(core), mine, lefts[2], joined_grads, some, *extra, None)
        )
        return one

    def slab_back(slab):
        backward_attn(last, line.last, (slab,))
        line.did(*state["bwd"][6:10])

    made, pieces, widths = {}, {}, {}

    def run_kernel(name):
        made[name] = {
            "SR": lambda: half_of(0, lefts[0], d_two, 0),
            "KR": lambda: half_of(1, lefts[0], d_two, 0),
            "SE": lambda: half_of(0, lefts[1], d_inner, 1),
            "KE": lambda: half_of(1, lefts[1], d_inner, 1),
            "PS": lambda: rest_half(0, slabs[:1], 2),
            "PK": lambda: rest_half(1, slabs[:1], 2),
            "QS": lambda: rest_half(0, slabs[1:], 3),
            "QK": lambda: rest_half(1, slabs[1:], 3),
            "S0": lambda: slab_back(slabs[0]),
            "S1": lambda: slab_back(slabs[1]),
            "S2": lambda: [slab_back(slab) for slab in slabs[2:]],
        }[name]()

    def small_sums():
        small, small_ff, joined_sums = ffn_back[4], ffn_back[5], state["bwd"][9]
        small_sum = jnp.sum(small[:micros], axis=0)
        joined_sum = jnp.sum(joined_sums[:micros, :, 0], axis=0)
        attend_sum = jnp.concatenate(
            [joined_sum[:, :SLAB].reshape(-1), joined_sum[:, SLAB:].reshape(-1)]
        )
        of_colbert = jnp.where(section_id == 1, colbert, colbert_down)
        parts = [
            small_sum[:6],
            attend_sum.reshape(2, width),
            jnp.sum(small_ff[:micros, 0], axis=0).reshape(-1, width),
            of_colbert.astype(F32).reshape(-1, width),
        ]
        return jnp.concatenate(parts).astype(BF)

    for step in exchange_order(len(bits)):
        if step == "V" and step not in pieces:
            pieces[step] = Adder(line, small_sums(), bits)
        if step in pieces:
            pieces[step].take()
        elif step[0] == "W":
            if step == "WE":
                made["up"] = passed_along(line.after(facts), "pipe", 1)
            widths[step] = widened(
                line.after(core), *ends_of_pieces([pieces[one] for one in WIDENED[step]]),
                {"WR": [wr.shape], "WE": [we.shape], "WP": [wa.shape, wm.shape]}[step],
            )
            line.did(*widths[step])
        else:
            run_kernel(step)
            if step in KEEPERS:
                name, send = KEEPERS[step]
                pieces[name] = Piece(line, made[send], made[step], bits, orders[ORDERS[name]])
    first = jnp.where(section_id == 0, facts, made["up"])
    second = jnp.where(section_id == 0, facts_down, facts)
    [big_reduce], [big_expand], (big_attend, big_mixing) = (widths[one] for one in ("WR", "WE", "WP"))
    vector = pieces["V"].value
    vector = vector.astype(F32)
    colbert_sum = vector[8 + we.shape[1] // width :].reshape(colbert_weight.shape)
    counted = (QROWS + jnp.sum(pass_lengths, axis=1)).astype(F32)
    stats = jnp.stack([first[:, :3], second[:, :3]], axis=1)
    stats = jnp.sqrt(stats / (counted[:, None, None] * width))
    return (
        big_attend[None],
        vector[6:8].reshape(1, -1),
        big_mixing[None],
        vector[5][None],
        jnp.stack([vector[3], vector[0]])[None],
        jnp.stack([vector[4], vector[1]])[None],
        big_expand[None],
        vector[8 : 8 + we.shape[1] // width].reshape(1, -1),
        big_reduce[None],
        vector[2][None],
        colbert_sum,
        second[:, 3] / NQ,
        stats,
    )


def solution(mesh):
    placed = (
        P("dp", None),
        P("pipe", None, None),
        P("pipe", None),
        P("pipe", None, None),
        P("pipe", None),
        P("pipe", None, None),
        P("pipe", None, None),
        P("pipe", None, None),
        P("pipe", None),
        P("pipe", None, None),
        P("pipe", None),
        P(),
        P("dp", None),
        P("dp", None),
    )
    return jax.shard_map(
        shards,
        mesh=mesh,
        in_specs=placed,
        out_specs=(
            P("pipe", None, None),
            P("pipe", None),
            P("pipe", None, None),
            P("pipe", None),
            P("pipe", None, None),
            P("pipe", None, None),
            P("pipe", None, None),
            P("pipe", None),
            P("pipe", None, None),
            P("pipe", None),
            P(),
            P("dp"),
            P("dp", None, None),
        ),
        check_vma=False,
    )
```
